32 devices in a mesh: wide: 8 (over y, x, core), narrow: 4 (over z).
Axes of the slice: x: 2, y: 2, z: 4, core: 2. Of those that a mesh axis runs over, the one named last changes fastest.
Arguments:
- tokens: bfloat16 [16384, 1024], P(('wide', 'narrow')), may hold values from -6 to 6
- patch_keep: int32 [32, 196], P(('wide', 'narrow')), may hold values 0 or 1
- text_len: int32 [32], P(('wide', 'narrow')), may hold values from 64 to 316, as said below
- buckets: int32 [16384, 512], P(('wide', 'narrow')), may hold values from 0 to 31
- mask_embed: bfloat16 [1024], P(('wide', 'narrow')), may hold values from -6 to 6
- norm_attn: bfloat16 [1024], P(('wide', 'narrow')), may hold values from 0.099609375 to 1.8984375
- w_query: bfloat16 [1024, 1024], P(('wide', 'narrow')), may hold values from -0.046875 to 0.046875
- w_key: bfloat16 [1024, 1024], P(('wide', 'narrow')), may hold values from -0.1875 to 0.1875
- w_value: bfloat16 [1024, 1024], P(('wide', 'narrow')), may hold values from -0.1875 to 0.1875
- w_out: bfloat16 [1024, 1024], P(('wide', 'narrow')), may hold values from -0.5 to 0.5
- bias_table: bfloat16 [512], P(('wide', 'narrow')), may hold values from -5 to 5
- norm_ffn: bfloat16 [1024], P(('wide', 'narrow')), may hold values from 0.099609375 to 1.8984375
- w_gate: bfloat16 [1024, 2816], P(('wide', 'narrow')), may hold values from -0.1875 to 0.1875
- w_up: bfloat16 [1024, 2816], P(('wide', 'narrow')), may hold values from -0.1875 to 0.1875
- w_down: bfloat16 [2816, 1024], P(('wide', 'narrow')), may hold values from -0.109375 to 0.109375
- cotangent: bfloat16 [16384, 1024], P(('wide', 'narrow')), may hold values from -6 to 6
Outputs:
- layer_out: bfloat16 [16384, 1024], P(('wide', 'narrow'))
- input_grad: float32 [16384, 1024], P(('wide', 'narrow'))
- embed_grad: float32 [1024], P(('wide', 'narrow'))
- norm_attn_grad: float32 [1024], P(('wide', 'narrow'))
- query_grad: float32 [1024, 1024], P(('wide', 'narrow'))
- key_grad: float32 [1024, 1024], P(('wide', 'narrow'))
- value_grad: float32 [1024, 1024], P(('wide', 'narrow'))
- out_proj_grad: float32 [1024, 1024], P(('wide', 'narrow'))
- table_grad: float32 [512], P(('wide', 'narrow'))
- norm_ffn_grad: float32 [1024], P(('wide', 'narrow'))
- gate_grad: float32 [1024, 2816], P(('wide', 'narrow'))
- up_grad: float32 [1024, 2816], P(('wide', 'narrow'))
- down_grad: float32 [2816, 1024], P(('wide', 'narrow'))
The draws below stay inside these ranges and needn't reach their ends.
Inputs may be any that keep to these rules, and one draw needn't show every extreme that they name: `text_len`: live text tokens of a page; some page has all 316.
All inputs are finite; a program needn't handle non-finite values. No bound on the sum of `patch_keep` on one device may be relied on, other than what follows from the above.
Results may differ from the reference program's by a relative error of at most 0.014.
The reference program's roundings to bfloat16 on the way count: a program that leaves them out, or rounds other values in their place, can miss the bound.
Values may be sent and summed in bfloat16 or wider, within the bound.
A program may use at most 256 MiB of HBM per device.

```python
import jax
import jax.numpy as jnp
from jax import lax

D = 1024
HEADS = 16
HEAD = 64
FF = 2816
BUCKETS = 32
PATCH = 196
TEXT = 316
PAGE = 512
INNER = 1024
PAGES = 32
TOKENS = 16384


def draw_text_len(key, part):
    key = jax.random.fold_in(key, 7)
    lengths = jax.random.randint(key, (PAGES,), TEXT // 5 + 1, TEXT + 1).astype(jnp.int32)
    return lengths.at[0].set(TEXT)


def with_ends(entries, stream_key, smallest, high):
    longest = entries.shape.index(max(entries.shape))
    spots = []
    for shift in (0, 1):
        where = [jax.random.randint(jax.random.fold_in(stream_key, axis), (), 0, length) for axis, length in enumerate(entries.shape)]
        where[longest] = (where[longest] + shift) % entries.shape[longest]
        spots.append(tuple(where))
    return entries.at[spots[0]].set(smallest).at[spots[1]].set(high)


def block_levels(own_key, dims, split, low, largest):
    factor_of = 1.0
    for axis_at, parts in split:
        draws = jax.random.uniform(jax.random.fold_in(jax.random.fold_in(own_key, 6), axis_at), (parts,), jnp.float32, low / len(split), largest / len(split))
        factor_of = factor_of * jnp.repeat(jnp.exp(draws), dims[axis_at] // parts).reshape((-1,) + (1,) * (len(dims) - 1 - axis_at))
    return factor_of


def scatter_about(stream_key, extent, spread, reach, shards=(), kind=jnp.bfloat16):
    entries = spread * jax.random.normal(stream_key, extent, jnp.float32)
    if shards:
        entries = entries * block_levels(stream_key, extent, shards, -0.22, 0.18)
    return jnp.clip(entries, -reach, reach).astype(kind)


def setup_inputs(seed: int = 0) -> dict:
    key_list = jax.random.split(jax.random.key(seed), 17)
    return {
        "tokens": scatter_about(key_list[0], (TOKENS, D), 1.0, 6.0, ((0, 32),)),
        "patch_keep": with_ends((jax.random.randint(key_list[1], (PAGES, PATCH), 0, 4) < 1).astype(jnp.int32), jax.random.fold_in(key_list[1], 1), 0, 1),
        "text_len": draw_text_len(jax.random.fold_in(key_list[16], 71), 0),
        "buckets": with_ends(jax.random.randint(key_list[3], (TOKENS, PAGE), 0, BUCKETS), jax.random.fold_in(key_list[3], 1), 0, BUCKETS - 1).astype(jnp.int32),
        "mask_embed": scatter_about(key_list[4], (D,), 1.0, 6.0, ((0, 32),)),
        "norm_attn": jnp.clip(1.0 + 0.18 * jax.random.normal(key_list[5], (D,), jnp.float32), 0.099609375, 1.8984375).astype(jnp.bfloat16),
        "w_query": scatter_about(key_list[6], (D, INNER), (16 * D) ** -0.5, 0.046875, ((0, 32),)),
        "w_key": scatter_about(key_list[7], (D, INNER), D ** -0.5, 0.1875, ((0, 32),)),
        "w_value": scatter_about(key_list[8], (D, INNER), D ** -0.5, 0.1875, ((0, 32),)),
        "w_out": scatter_about(key_list[9], (INNER, D), (INNER // 8) ** -0.5, 0.5, ((0, 32),)),
        "bias_table": scatter_about(key_list[10], (BUCKETS * HEADS,), 1.0, 5.0, ((0, 32),)),
        "norm_ffn": jnp.clip(1.0 + 0.18 * jax.random.normal(key_list[11], (D,), jnp.float32), 0.099609375, 1.8984375).astype(jnp.bfloat16),
        "w_gate": scatter_about(key_list[12], (D, FF), D ** -0.5, 0.1875, ((0, 32),)),
        "w_up": scatter_about(key_list[13], (D, FF), D ** -0.5, 0.1875, ((0, 32),)),
        "w_down": scatter_about(key_list[14], (FF, D), FF ** -0.5, 0.109375, ((0, 32),)),
        "cotangent": scatter_about(key_list[15], (TOKENS, D), 1.0, 6.0, ((0, 32),)),
    }


@jax.custom_vjp
def low(v):
    return lax.optimization_barrier(v.astype(jnp.bfloat16)).astype(jnp.float32)

@jax.custom_vjp
def low_back(v):
    return v

def low_keep(v):
    return (low(v), None)

def low_pass(kept, grad):
    return (grad,)

def back_keep(v):
    return (v, None)

def back_low(kept, grad):
    return (low(grad),)
low.defvjp(low_keep, low_pass)
low_back.defvjp(back_keep, back_low)
EPSILON = 1e-06
NEG_FILL = -1000000000.0
HIGHEST = lax.Precision.HIGHEST

def round_both(value_in):
    return low_back(low(value_in))

def norm_rows(inputs, scale_gain):
    return inputs * lax.rsqrt(lax.optimization_barrier(jnp.mean(inputs * inputs, axis=-1, keepdims=True)) + EPSILON) * scale_gain

def matmul(left, right):
    return jnp.dot(left, right, precision=HIGHEST, preferred_element_type=jnp.float32)

def encoder_layer(inputs, keep_rows, valid_keys, bucket_pages, mask_embed, norm_attn, w_query, w_key, w_value, w_out, bias_table, norm_ffn, w_gate, w_up, w_down):
    start_rows = jnp.where(keep_rows[:, None] == 1, inputs, mask_embed[None, :])
    normed = low(norm_rows(start_rows, norm_attn))
    queries = round_both(matmul(normed, w_query))
    keys_all = round_both(matmul(normed, w_key))
    values = round_both(matmul(normed, w_value))
    table_heads = bias_table.reshape(BUCKETS, HEADS).T
    page_count = valid_keys.shape[0]

    def shaped(tensor):
        return tensor.reshape(page_count, PAGE, HEADS, HEAD)

    def attend(page_items):
        query_page, key_page, value_page, bucket, live_keys = page_items
        scores = jnp.einsum('qhd,khd->hqk', query_page, key_page, precision=HIGHEST) + table_heads[:, bucket]
        scores = low_back(scores)
        scores = jnp.where(live_keys[None, None, :], scores, NEG_FILL)
        attn_prob = jax.nn.softmax(scores, axis=-1)
        return jnp.einsum('hqk,khd->qhd', low(attn_prob), value_page, precision=HIGHEST)
    mixed_all = lax.map(jax.checkpoint(attend), (shaped(queries), shaped(keys_all), shaped(values), bucket_pages, valid_keys))
    attended = round_both(mixed_all.reshape(-1, INNER))
    mid_rows = start_rows + low_back(matmul(attended, w_out))
    normed_two = low(norm_rows(mid_rows, norm_ffn))
    gate_pre = low_back(matmul(normed_two, w_gate))
    up_pre = low_back(matmul(normed_two, w_up))
    hidden_act = low(jax.nn.gelu(gate_pre, approximate=True) * up_pre)
    return mid_rows + low_back(matmul(hidden_act, w_down))

def reference(tokens, patch_keep, text_len, buckets, mask_embed, norm_attn, w_query, w_key, w_value, w_out, bias_table, norm_ffn, w_gate, w_up, w_down, cotangent):

    def as_float(array):
        return array.astype(jnp.float32)
    keep_rows = jnp.concatenate([patch_keep, jnp.ones((patch_keep.shape[0], TEXT), jnp.int32)], axis=1).reshape(-1)
    valid_keys = jnp.arange(PAGE, dtype=jnp.int32)[None, :] < (PATCH + text_len)[:, None]
    bucket_pages = buckets.reshape(-1, PAGE, PAGE)

    def forward(inputs, *weights):
        return encoder_layer(inputs, keep_rows, valid_keys, bucket_pages, *weights)
    result, backward = jax.vjp(forward, as_float(tokens), as_float(mask_embed), as_float(norm_attn), as_float(w_query), as_float(w_key), as_float(w_value), as_float(w_out), as_float(bias_table), as_float(norm_ffn), as_float(w_gate), as_float(w_up), as_float(w_down))
    grads = backward(as_float(cotangent))
    return (result.astype(jnp.bfloat16), grads[0], grads[1], grads[2], grads[3], grads[4], grads[5], grads[6], grads[7], grads[8], grads[9], grads[10], grads[11])
```

```python
import functools

import jax
import jax.numpy as jnp
from jax import lax
from jax.experimental import pallas as pl
from jax.experimental.pallas import tpu as pltpu
from jax.sharding import PartitionSpec as P

MESH = pl.DeviceIdType.MESH
VMEM_LIMIT = 60 << 20


def round_up(value, unit):
    return -(-value // unit) * unit


class Plan:
    def __init__(self, wide, narrow):
        self.wide, self.narrow = wide, narrow
        self.bits = [2 << i for i in range(wide.bit_length() - 2)]
        assert wide == 2 * 2 ** len(self.bits)

    def orders(self, parts):
        return [self.bits, self.bits[::-1]][:parts]


def span(bits):
    out = [0]
    for bit in bits:
        out = out + [member ^ bit for member in out]
    return out


def column_parts(columns):
    if columns < 512:
        return [(0, columns)]
    half = round_up(columns // 2, 128)
    return [(0, half), (half, columns - half)]


def enter(plan):
    w, n = lax.axis_index("wide"), lax.axis_index("narrow")
    barrier = pltpu.get_barrier_semaphore()
    partners = [(w ^ bit, n) for bit in [1] + plan.bits]
    partners += [(w, lax.rem(n + d, plan.narrow)) for d in range(1, plan.narrow)]
    for partner in partners:
        pl.semaphore_signal(barrier, inc=1, device_id=partner, device_id_type=MESH)
    pl.semaphore_wait(barrier, len(partners))
    return w, n


class Gather:
    def __init__(self, plan, shape):
        self.plan = plan
        self.rows, self.columns = shape
        self.padded = round_up(self.rows, 16)
        self.aligned = self.padded == self.rows
        self.group = plan.narrow * self.rows
        self.parts = column_parts(self.columns)
        self.orders = plan.orders(len(self.parts))
        self.chunks = 1 << len(plan.bits)

    def out_shape(self):
        return jax.ShapeDtypeStruct((self.plan.wide, self.group, self.columns), jnp.bfloat16)

    def scratch(self):
        sem = pltpu.SemaphoreType.DMA
        count, parts = self.plan.narrow, len(self.parts)
        base = [sem((2, count)), sem((2, parts, self.chunks)), sem((2, parts, self.chunks)), sem((2,))]
        if not self.aligned:
            base += [
                pltpu.VMEM((count, self.padded, self.columns), jnp.bfloat16),
                pltpu.VMEM((self.group, self.columns), jnp.bfloat16),
            ]
        return base

    def bind(self, place, shard, out, scratch):
        self.w, self.n = place
        self.shard, self.out = shard, out
        self.zsem, self.bsem, self.csem, self.lsem = scratch[:4]
        if not self.aligned:
            self.stage, self.compact = scratch[4:]

    def own_slot(self):
        if self.aligned:
            return self.out.at[self.w, pl.ds(pl.multiple_of(self.n * self.rows, self.rows), self.rows), :]
        return self.stage.at[self.n]

    def z_copy(self, d):
        return pltpu.make_async_remote_copy(
            src_ref=self.shard,
            dst_ref=self.own_slot(),
            send_sem=self.zsem.at[0, d],
            recv_sem=self.zsem.at[1, d],
            device_id=(self.w, lax.rem(self.n + d, self.plan.narrow)),
            device_id_type=MESH,
        )

    def place_copy(self):
        return pltpu.make_async_copy(self.shard, self.own_slot(), self.lsem.at[0])

    def group_copy(self):
        return pltpu.make_async_copy(self.compact, self.out.at[self.w], self.lsem.at[1])

    def start(self):
        for d in range(1, self.plan.narrow):
            self.z_copy(d).start()
        self.place_copy().start()

    def piece(self, ref, part):
        start, size = self.parts[part]
        return ref if size == self.columns else ref.at[:, pl.ds(start, size)]

    def hop(self, sems, part, mask, bit, slot):
        chunk = self.out.at[self.w ^ mask]
        source = self.compact if mask == 0 and not self.aligned else chunk
        return pltpu.make_async_remote_copy(
            src_ref=self.piece(source, part),
            dst_ref=self.piece(chunk, part),
            send_sem=sems.at[0, part, slot],
            recv_sem=sems.at[1, part, slot],
            device_id=(self.w ^ bit, self.n),
            device_id_type=MESH,
        )

    def hops(self, part, stage):
        order = self.orders[part]
        masks = span(order[:stage])
        return [self.hop(self.bsem, part, mask, order[stage], len(masks) + i - 1) for i, mask in enumerate(masks)]

    def core_hops(self, part, stage):
        masks = span(self.orders[part])
        low, high = (0, 1) if stage == 0 else (1 << (stage - 1), 1 << stage)
        return [self.hop(self.csem, part, masks[i], 1, i) for i in range(low, high)]

    def stages(self):
        return len(self.plan.bits) + 2

    def step(self, stage):
        bits, parts = len(self.plan.bits), range(len(self.parts))
        if stage == 0:
            for d in range(1, self.plan.narrow):
                self.z_copy(d).wait_recv()
            self.place_copy().wait()
            if not self.aligned:
                size, wide = self.group, self.plan.narrow * self.padded
                row = lax.broadcasted_iota(jnp.int32, (size, wide), 0)
                column = lax.broadcasted_iota(jnp.int32, (size, wide), 1)
                pick = column == (row // self.rows) * self.padded + row % self.rows
                self.compact[...] = jnp.dot(
                    pick.astype(jnp.bfloat16),
                    self.stage[...].reshape(wide, self.columns),
                    preferred_element_type=jnp.float32,
                ).astype(jnp.bfloat16)
                self.group_copy().start()
        elif stage <= bits:
            for part in parts:
                for copy in self.hops(part, stage - 1):
                    copy.wait_recv()
        else:
            for part in parts:
                for s in range(bits + 1):
                    for copy in self.core_hops(part, s):
                        copy.wait_recv()
            if not self.aligned:
                self.group_copy().wait()
        if stage < bits:
            for part in parts:
                for copy in self.hops(part, stage):
                    copy.start()
        if stage <= bits:
            for part in parts:
                for copy in self.core_hops(part, stage):
                    copy.start()

    def finish(self):
        for d in range(1, self.plan.narrow):
            self.z_copy(d).wait_send()
        for part in range(len(self.parts)):
            for s in range(len(self.plan.bits)):
                for copy in self.hops(part, s):
                    copy.wait_send()
            for s in range(len(self.plan.bits) + 1):
                for copy in self.core_hops(part, s):
                    copy.wait_send()


def split(flat, sizes):
    out, at = [], 0
    for size in sizes:
        out.append(flat[at : at + size])
        at += size
    return out


def gather_kernel(plan, items, *refs):
    count = len(items)
    shards, outs = refs[:count], refs[count : 2 * count]
    scratch = split(refs[2 * count :], [len(item.scratch()) for item in items])
    place = enter(plan)
    for item, shard, out, own in zip(items, shards, outs, scratch):
        item.bind(place, shard, out, own)
    stages = items[0].stages()
    for item in items[:3]:
        item.start()
    for tick in range(count + stages - 1):
        for stage in range(stages):
            k = tick - stage
            if 0 <= k < count:
                items[k].step(stage)
        if tick + 3 < count:
            items[tick + 3].start()
    for item in items:
        item.finish()


def gather_all(plan, shards):
    items = [Gather(plan, shard.shape) for shard in shards]
    padded = [
        shard if item.aligned else jnp.pad(shard, ((0, item.padded - item.rows), (0, 0)))
        for item, shard in zip(items, shards)
    ]
    return pl.pallas_call(
        functools.partial(gather_kernel, plan, items),
        out_shape=[item.out_shape() for item in items],
        in_specs=[pl.BlockSpec(memory_space=pl.ANY)] * len(items),
        out_specs=[pl.BlockSpec(memory_space=pl.ANY)] * len(items),
        scratch_shapes=[piece for item in items for piece in item.scratch()],
        compiler_params=pltpu.CompilerParams(
            collective_id=0, has_side_effects=True, vmem_limit_bytes=VMEM_LIMIT
        ),
    )(*padded)


class Reduce:
    def __init__(self, plan, rows, columns):
        self.plan = plan
        self.rows, self.columns = rows, columns
        self.padded = round_up(rows, 16)
        self.aligned = self.padded == rows
        self.group = plan.narrow * rows
        self.parts = column_parts(columns)
        self.orders = plan.orders(len(self.parts))
        self.chunks = 1 << len(plan.bits)

    def grad_shape(self):
        return jax.ShapeDtypeStruct((self.plan.wide, self.group, self.columns), jnp.bfloat16)

    def out_shape(self):
        return jax.ShapeDtypeStruct((self.rows, self.columns), jnp.float32)

    def scratch(self):
        sem = pltpu.SemaphoreType.DMA
        count, parts = self.plan.narrow, len(self.parts)
        base = [
            sem((2, self.chunks)),
            sem((2, parts, self.chunks)),
            sem((2, count)),
            sem((self.chunks,)),
            pltpu.VMEM((self.chunks, self.group, self.columns), jnp.bfloat16),
            pltpu.VMEM((self.chunks, self.group, self.columns), jnp.bfloat16),
            pltpu.VMEM((self.chunks - 1, self.group, self.columns), jnp.bfloat16),
            pltpu.VMEM((count - 1, self.padded, self.columns), jnp.bfloat16),
        ]
        if not self.aligned:
            base.append(pltpu.VMEM((count, self.padded, self.columns), jnp.bfloat16))
        return base

    def bind(self, place, grad, out, scratch):
        self.w, self.n = place
        self.grad, self.out = grad, out
        self.csem, self.bsem, self.zsem, self.lsem = scratch[:4]
        self.acc, self.crecv, self.brecv, self.zrecv = scratch[4:8]
        if not self.aligned:
            self.stage = scratch[8]

    def core_copy(self, slot):
        return pltpu.make_async_remote_copy(
            src_ref=self.grad.at[self.w ^ 1 ^ (2 * slot)],
            dst_ref=self.crecv.at[slot],
            send_sem=self.csem.at[0, slot],
            recv_sem=self.csem.at[1, slot],
            device_id=(self.w ^ 1, self.n),
            device_id_type=MESH,
        )

    def load_copy(self, slot):
        return pltpu.make_async_copy(self.grad.at[self.w ^ (2 * slot)], self.acc.at[slot], self.lsem.at[slot])

    def piece(self, ref, part):
        start, size = self.parts[part]
        return ref if size == self.columns else ref.at[:, pl.ds(start, size)]

    def hops(self, part, stage):
        order = self.orders[part]
        bit, masks = order[stage], span(order[stage + 1 :])
        base = self.chunks - 2 * len(masks)
        return [
            (
                mask >> 1,
                base + i,
                pltpu.make_async_remote_copy(
                    src_ref=self.piece(self.acc.at[(bit ^ mask) >> 1], part),
                    dst_ref=self.piece(self.brecv.at[base + i], part),
                    send_sem=self.bsem.at[0, part, base + i],
                    recv_sem=self.bsem.at[1, part, base + i],
                    device_id=(self.w ^ bit, self.n),
                    device_id_type=MESH,
                ),
            )
            for i, mask in enumerate(masks)
        ]

    def z_copy(self, d):
        peer = lax.rem(self.n + d, self.plan.narrow)
        if self.aligned:
            source = self.acc.at[0, pl.ds(pl.multiple_of(peer * self.rows, self.rows), self.rows), :]
        else:
            source = self.stage.at[peer]
        return pltpu.make_async_remote_copy(
            src_ref=source,
            dst_ref=self.zrecv.at[d - 1],
            send_sem=self.zsem.at[0, d],
            recv_sem=self.zsem.at[1, d],
            device_id=(self.w, peer),
            device_id_type=MESH,
        )

    def start(self):
        for slot in range(self.chunks):
            self.core_copy(slot).start()
        for slot in range(self.chunks):
            self.load_copy(slot).start()

    def add(self, slot, received, start, size):
        def body(i, carry):
            rows = pl.ds(pl.multiple_of(i * 16, 16), 16)
            self.acc[slot, rows, pl.ds(start, size)] += received[rows, pl.ds(start, size)]
            return carry

        lax.fori_loop(0, self.group // 16, body, 0)

    def stages(self):
        return len(self.plan.bits) + 2

    def step(self, stage):
        bits, parts = len(self.plan.bits), range(len(self.parts))
        if stage == 0:
            for slot in range(self.chunks):
                self.load_copy(slot).wait()
                self.core_copy(slot).wait_recv()
                self.add(slot, self.crecv.at[slot], 0, self.columns)
        elif stage <= bits:
            for part in parts:
                for slot, at, copy in self.hops(part, stage - 1):
                    copy.wait_recv()
                    self.add(slot, self.brecv.at[at], *self.parts[part])
        if stage < bits:
            for part in parts:
                for _, _, copy in self.hops(part, stage):
                    copy.start()
        elif stage == bits:
            if not self.aligned:
                size, wide = self.group, self.plan.narrow * self.padded
                row = lax.broadcasted_iota(jnp.int32, (wide, size), 0)
                column = lax.broadcasted_iota(jnp.int32, (wide, size), 1)
                pick = row == (column // self.rows) * self.padded + column % self.rows
                self.stage[...] = (
                    jnp.dot(pick.astype(jnp.bfloat16), self.acc[0], preferred_element_type=jnp.float32)
                    .astype(jnp.bfloat16)
                    .reshape(self.stage.shape)
                )
            for d in range(1, self.plan.narrow):
                self.z_copy(d).start()
        else:
            if self.aligned:
                total = self.acc[0, pl.ds(pl.multiple_of(self.n * self.rows, self.rows), self.rows), :]
            else:
                total = self.stage[self.n]
            total = total.astype(jnp.float32)
            for d in range(1, self.plan.narrow):
                self.z_copy(d).wait_recv()
                total = total + self.zrecv[d - 1].astype(jnp.float32)
            self.out[...] = total[: self.rows]

    def finish(self):
        for slot in range(self.chunks):
            self.core_copy(slot).wait_send()
        for part in range(len(self.parts)):
            for s in range(len(self.plan.bits)):
                for _, _, copy in self.hops(part, s):
                    copy.wait_send()
        for d in range(1, self.plan.narrow):
            self.z_copy(d).wait_send()


class SumAll:
    def __init__(self, plan, shape):
        self.plan, self.shape = plan, shape
        self.rounds = [(bit, 0) for bit in [1] + plan.bits]
        self.rounds += [(0, 1 << i) for i in range(plan.narrow.bit_length() - 1)]

    def scratch(self):
        sem, count = pltpu.SemaphoreType.DMA, len(self.rounds)
        return [sem((2, count)), pltpu.VMEM((count, *self.shape), jnp.float32), pltpu.VMEM((count, *self.shape), jnp.float32)]

    def bind(self, place, out, scratch):
        self.w, self.n = place
        self.out = out
        self.sem, self.held, self.received = scratch

    def copy(self, turn):
        bit, other = self.rounds[turn]
        return pltpu.make_async_remote_copy(
            src_ref=self.held.at[turn],
            dst_ref=self.received.at[turn],
            send_sem=self.sem.at[0, turn],
            recv_sem=self.sem.at[1, turn],
            device_id=(self.w ^ bit, self.n ^ other),
            device_id_type=MESH,
        )

    def start(self, value):
        self.held[0] = value
        self.copy(0).start()

    def step(self, turn):
        self.copy(turn).wait_recv()
        total = self.held[turn] + self.received[turn]
        if turn + 1 < len(self.rounds):
            self.held[turn + 1] = total
            self.copy(turn + 1).start()
        else:
            self.out[...] = total

    def finish(self):
        for turn in range(len(self.rounds)):
            self.copy(turn).wait_send()


def reduce_kernel(plan, items, small, *refs):
    count = len(items)
    grads, small_in = refs[:count], refs[count]
    outs, small_out = refs[count + 1 : 2 * count + 1], refs[2 * count + 1]
    pieces = split(refs[2 * count + 2 :], [len(item.scratch()) for item in items] + [len(small.scratch())])
    place = enter(plan)
    for item, grad, out, own in zip(items, grads, outs, pieces):
        item.bind(place, grad, out, own)
    small.bind(place, small_out, pieces[-1])
    stages = items[0].stages()
    items[0].start()
    items[1].start()
    small.start(small_in[...])
    for tick in range(count + stages - 1):
        if tick < len(small.rounds):
            small.step(tick)
        for stage in range(stages):
            k = tick - stage
            if 0 <= k < count:
                items[k].step(stage)
        if tick + 2 < count:
            items[tick + 2].start()
    for item in items:
        item.finish()
    small.finish()


def reduce_all(plan, grads, rows, small_value):
    items = [Reduce(plan, r, grad.shape[-1]) for grad, r in zip(grads, rows)]
    small = SumAll(plan, small_value.shape)
    return pl.pallas_call(
        functools.partial(reduce_kernel, plan, items, small),
        out_shape=[item.out_shape() for item in items] + [jax.ShapeDtypeStruct(small_value.shape, jnp.float32)],
        in_specs=[pl.BlockSpec(memory_space=pl.ANY)] * len(items) + [pl.BlockSpec(memory_space=pltpu.VMEM)],
        out_specs=[pl.BlockSpec(memory_space=pltpu.VMEM)] * (len(items) + 1),
        scratch_shapes=[piece for item in items + [small] for piece in item.scratch()],
        compiler_params=pltpu.CompilerParams(
            collective_id=1, has_side_effects=True, vmem_limit_bytes=VMEM_LIMIT
        ),
    )(*[grad.reshape(item.grad_shape().shape) for grad, item in zip(grads, items)], small_value)


HEADS = 16
HEAD = 64
BUCKETS = 32
EPSILON = 1e-06
NEG_FILL = -1000000000.0
LANES = 128


def norm_rows(inputs, scale_gain):
    return (
        inputs * lax.rsqrt(jnp.mean(inputs * inputs, axis=-1, keepdims=True) + EPSILON) * scale_gain
    )


def gelu_tanh(inputs):
    return jax.nn.gelu(inputs, approximate=True)


def matmul(left, right):
    return jnp.dot(left, right, preferred_element_type=jnp.float32)


def times_trans(left, right):
    return lax.dot_general(left, right, (((1,), (1,)), ((), ())), preferred_element_type=jnp.float32)


def trans_times(left, right):
    return lax.dot_general(left, right, (((0,), (0,)), ((), ())), preferred_element_type=jnp.float32)


def bucket_table(bucket):
    return (bucket[:, :, None] == jnp.arange(BUCKETS, dtype=jnp.int32)[None, None, :]).astype(jnp.bfloat16)


def page_scores(query_page, key_page, one_hot, live_keys, table_rows):
    position_bias = jnp.einsum("qkb,bh->hqk", one_hot, table_rows, preferred_element_type=jnp.float32)
    scores = (
        jnp.einsum("qhd,khd->hqk", query_page, key_page, preferred_element_type=jnp.float32)
        + position_bias
    )
    return jnp.where(live_keys[None, None, :], scores, NEG_FILL)


def pack_small(vectors, device):
    rows = []
    for vector in vectors:
        size = vector.shape[0]
        rows.append(
            lax.dynamic_update_slice(
                jnp.zeros((LANES,), vector.dtype), vector, (lax.rem(device * size, LANES),)
            )
        )
    rows += [jnp.zeros((LANES,), vectors[0].dtype)] * (16 - len(rows))
    return jnp.stack(rows)


def unpack_small(gathered, sizes):
    out = []
    for i, size in enumerate(sizes):
        blocks = gathered[:, i, :].astype(jnp.float32).reshape(-1, LANES // size, LANES)
        out.append(jnp.sum(blocks, axis=1).reshape(-1))
    return out


def per_device(
    plan,
    tokens,
    patch_keep,
    text_len,
    buckets,
    mask_embed,
    norm_attn,
    w_query,
    w_key,
    w_value,
    w_out,
    bias_table,
    norm_ffn,
    w_gate,
    w_up,
    w_down,
    cotangent,
):
    page_count, patches = patch_keep.shape
    row_count = tokens.shape[0]
    page_rows = row_count // page_count
    device = lax.axis_index("wide") * plan.narrow + lax.axis_index("narrow")
    keep_rows = (
        jnp.concatenate(
            [patch_keep, jnp.ones((page_count, page_rows - patches), jnp.int32)], axis=1
        ).reshape(row_count, 1)
        == 1
    )
    live_keys = jnp.arange(page_rows, dtype=jnp.int32)[None, :] < (patches + text_len)[:, None]
    bucket_pages = buckets.reshape(page_count, page_rows, page_rows)

    def shaped(tensor):
        return tensor.reshape(page_count, page_rows, HEADS, HEAD)

    small_set = (mask_embed, norm_attn, norm_ffn, bias_table)
    gathered = gather_all(
        plan, (pack_small(small_set, device), w_query, w_key, w_value, w_out, w_gate, w_up, w_down)
    )
    embed_all, gain_one, gain_two, table_all = unpack_small(
        gathered[0].reshape(-1, 16, LANES), [member.shape[0] for member in small_set]
    )
    query_all, key_all, value_all, out_all, gate_all, up_all, down_all = (
        member.reshape(-1, member.shape[-1]) for member in gathered[1:]
    )
    start_rows = jnp.where(keep_rows, tokens.astype(jnp.float32), embed_all[None, :])
    normed = norm_rows(start_rows, gain_one).astype(jnp.bfloat16)
    queries = matmul(normed, query_all).astype(jnp.bfloat16)
    keys_local = matmul(normed, key_all).astype(jnp.bfloat16)
    values = matmul(normed, value_all).astype(jnp.bfloat16)
    table_rows = table_all.astype(jnp.bfloat16).reshape(BUCKETS, HEADS)

    def attend_forward(page_items):
        query_page, key_page, value_page, bucket, live_page = page_items
        scores = page_scores(query_page, key_page, bucket_table(bucket), live_page, table_rows)
        row_max = jnp.max(scores, axis=-1, keepdims=True)
        exponent = jnp.exp(scores - row_max)
        row_total = jnp.sum(exponent, axis=-1, keepdims=True)
        attn_prob = (exponent / row_total).astype(jnp.bfloat16)
        mixed_page = jnp.einsum(
            "hqk,khd->qhd", attn_prob, value_page, preferred_element_type=jnp.float32
        )
        return (mixed_page, row_max + jnp.log(row_total))

    mixed_all, log_total = lax.map(
        attend_forward,
        (shaped(queries), shaped(keys_local), shaped(values), bucket_pages, live_keys),
    )
    attended = mixed_all.reshape(row_count, -1).astype(jnp.bfloat16)
    mid_rows = start_rows + matmul(attended, out_all)
    normed_two = norm_rows(mid_rows, gain_two).astype(jnp.bfloat16)
    gate_pre = matmul(normed_two, gate_all)
    up_pre = matmul(normed_two, up_all)
    gelu_val, gelu_back = jax.vjp(gelu_tanh, gate_pre)
    hidden_act = (gelu_val * up_pre).astype(jnp.bfloat16)
    result = (mid_rows + matmul(hidden_act, down_all)).astype(jnp.bfloat16)
    grad_down = trans_times(hidden_act, cotangent).astype(jnp.bfloat16)
    grad_act = times_trans(cotangent, down_all)
    grad_gate = gelu_back(grad_act * up_pre)[0].astype(jnp.bfloat16)
    grad_up = (grad_act * gelu_val).astype(jnp.bfloat16)
    grad_gate_w = trans_times(normed_two, grad_gate).astype(jnp.bfloat16)
    grad_up_w = trans_times(normed_two, grad_up).astype(jnp.bfloat16)
    grad_normed_two = times_trans(grad_gate, gate_all) + times_trans(grad_up, up_all)
    grad_mid_norm, grad_gain_two = jax.vjp(norm_rows, mid_rows, gain_two)[1](grad_normed_two)
    grad_mid = cotangent.astype(jnp.float32) + grad_mid_norm
    grad_attn = grad_mid.astype(jnp.bfloat16)
    grad_out_w = trans_times(attended, grad_attn).astype(jnp.bfloat16)
    grad_attended = times_trans(grad_attn, out_all).astype(jnp.bfloat16)

    def attend_back(page_items):
        query_page, key_page, value_page, bucket, live_page, total_page, grad_page = page_items
        one_hot = bucket_table(bucket)
        scores = page_scores(query_page, key_page, one_hot, live_page, table_rows)
        attn_prob = jnp.exp(scores - total_page)
        grad_prob = jnp.einsum(
            "qhd,khd->hqk", grad_page, value_page, preferred_element_type=jnp.float32
        )
        row_delta = jnp.sum(grad_prob * attn_prob, axis=-1, keepdims=True)
        grad_scores = (attn_prob * (grad_prob - row_delta)).astype(jnp.bfloat16)
        grad_query = jnp.einsum(
            "hqk,khd->qhd", grad_scores, key_page, preferred_element_type=jnp.float32
        ).astype(jnp.bfloat16)
        grad_key = jnp.einsum(
            "hqk,qhd->khd", grad_scores, query_page, preferred_element_type=jnp.float32
        ).astype(jnp.bfloat16)
        grad_value = jnp.einsum(
            "hqk,qhd->khd",
            attn_prob.astype(jnp.bfloat16),
            grad_page,
            preferred_element_type=jnp.float32,
        ).astype(jnp.bfloat16)
        grad_bias = jnp.einsum(
            "qkb,hqk->bh", one_hot, grad_scores, preferred_element_type=jnp.float32
        )
        return (grad_query, grad_key, grad_value, grad_bias)

    grad_q, grad_k, grad_v, grad_bias = lax.map(
        attend_back,
        (
            shaped(queries),
            shaped(keys_local),
            shaped(values),
            bucket_pages,
            live_keys,
            log_total,
            shaped(grad_attended),
        ),
    )
    grad_q = grad_q.reshape(row_count, -1)
    grad_k = grad_k.reshape(row_count, -1)
    grad_v = grad_v.reshape(row_count, -1)
    grad_table = jnp.sum(grad_bias, axis=0).reshape(-1)
    grad_query_w = trans_times(normed, grad_q).astype(jnp.bfloat16)
    grad_key_w = trans_times(normed, grad_k).astype(jnp.bfloat16)
    grad_value_w = trans_times(normed, grad_v).astype(jnp.bfloat16)
    grad_normed = (
        times_trans(grad_q, query_all)
        + times_trans(grad_k, key_all)
        + times_trans(grad_v, value_all)
    )
    grad_start_norm, grad_gain_one = jax.vjp(norm_rows, start_rows, gain_one)[1](grad_normed)
    grad_start = grad_mid + grad_start_norm
    input_grad = jnp.where(keep_rows, grad_start, 0.0)
    grad_embed = jnp.sum(jnp.where(keep_rows, 0.0, grad_start), axis=0)
    width = grad_embed.shape[0]
    small_grads = jnp.stack(
        [grad_embed, grad_gain_one, grad_gain_two, jnp.pad(grad_table, (0, width - grad_table.shape[0]))]
        + [jnp.zeros((width,), jnp.float32)] * 4
    )
    weight_rows = [w.shape[0] for w in (w_down, w_gate, w_up, w_out, w_query, w_key, w_value)]
    down_part, gate_part, up_part, out_part, query_part, key_part, value_part, small_sums = reduce_all(
        plan,
        (grad_down, grad_gate_w, grad_up_w, grad_out_w, grad_query_w, grad_key_w, grad_value_w),
        weight_rows,
        small_grads,
    )

    def own(row, size):
        return lax.dynamic_slice(small_sums[row], (device * size,), (size,))

    return (
        result,
        input_grad,
        own(0, mask_embed.shape[0]),
        own(1, norm_attn.shape[0]),
        query_part,
        key_part,
        value_part,
        out_part,
        own(3, bias_table.shape[0]),
        own(2, norm_ffn.shape[0]),
        gate_part,
        up_part,
        down_part,
    )


def solution(mesh):
    rows, flat = P(("wide", "narrow"), None), P(("wide", "narrow"))
    plan = Plan(mesh.shape["wide"], mesh.shape["narrow"])
    return jax.shard_map(
        functools.partial(per_device, plan),
        mesh=mesh,
        in_specs=(rows, rows, flat, rows, flat, flat, rows, rows, rows, rows, flat, flat, rows, rows, rows, rows),
        out_specs=(rows, rows, flat, flat, rows, rows, rows, rows, flat, flat, rows, rows, rows),
        check_vma=False,
    )
```

```python
import functools
import types

import jax
import jax.numpy as jnp
from jax import lax
from jax.experimental import pallas as pl
from jax.experimental.pallas import tpu as pltpu
from jax.sharding import PartitionSpec as P

MESH = pl.DeviceIdType.MESH
VMEM_LIMIT = 62 << 20
HEADS = 16
HEAD = 64
BUCKETS = 32
EPSILON = 1e-06
NEG_FILL = -1000000000.0
LANES = 128
TILE = 256
CONTRACT_LAST = (((1,), (1,)), ((), ()))
CONTRACT_FIRST = (((0,), (0,)), ((), ()))
BF16, F32, I32 = jnp.bfloat16, jnp.float32, jnp.int32
GELU_SCALE = 0.7978845608028654
GELU_CUBE = 0.044715


def round_up(value, unit):
    return -(-value // unit) * unit


def matmul(left, right):
    return jnp.dot(left, right, preferred_element_type=F32)


def times_trans(left, right):
    return lax.dot_general(left, right, CONTRACT_LAST, preferred_element_type=F32)


def trans_times(left, right):
    return lax.dot_general(left, right, CONTRACT_FIRST, preferred_element_type=F32)


class Plan:
    def __init__(self, wide, narrow):
        self.wide, self.narrow = wide, narrow
        self.bits = [2 << i for i in range(wide.bit_length() - 2)]
        self.chunks = wide // 2
        assert wide == 2 << len(self.bits)


def span(bits):
    out = [0]
    for bit in bits:
        out = out + [member ^ bit for member in out]
    return out


def halves(start, size):
    half = round_up(size // 2, LANES)
    return [(start, half), (start + half, size - half)] if size > 2 * LANES else [(start, size)]


def enter(plan):
    w, n = lax.axis_index("wide"), lax.axis_index("narrow")
    barrier = pltpu.get_barrier_semaphore()
    partners = [(w ^ bit, n) for bit in [1] + plan.bits]
    partners += [(w, lax.rem(n + d, plan.narrow)) for d in range(1, plan.narrow)]
    for partner in partners:
        pl.semaphore_signal(barrier, inc=1, device_id=partner, device_id_type=MESH)
    pl.semaphore_wait(barrier, len(partners))
    return w, n


def loop(low, high, body):
    def step(i, carry):
        body(i)
        return carry

    lax.fori_loop(low, high, step, 0)


def at(index, size):
    return pl.ds(pl.multiple_of(index * size, size), size)


def streamed(low, high, copies, body):
    for copy in copies(lax.rem(low, 2), low):
        copy.start()

    def step(i):
        slot = lax.rem(i, 2)

        @pl.when(i + 1 < high)
        def _():
            for copy in copies(1 - slot, i + 1):
                copy.start()

        for copy in copies(slot, i):
            copy.wait()
        body(i, slot)

    loop(low, high, step)


def run(kernel, inputs, outputs, scratch, in_vmem, out_vmem, collective_id, name):
    sizes = [len(jax.tree.leaves(tree)) for tree in (inputs, outputs, scratch)]
    forms = [jax.tree.structure(tree) for tree in (inputs, outputs, scratch)]

    def flat(*refs):
        first, second = sizes[0], sizes[0] + sizes[1]
        parts = (refs[:first], refs[first:second], refs[second:])
        kernel(*(types.SimpleNamespace(**form.unflatten(part)) for form, part in zip(forms, parts)))

    def specs(tree, resident):
        return jax.tree.leaves(
            {
                key: jax.tree.map(
                    lambda _: pl.BlockSpec(memory_space=pltpu.VMEM if key in resident else pl.ANY), value
                )
                for key, value in tree.items()
            }
        )

    result = pl.pallas_call(
        flat,
        out_shape=jax.tree.leaves(outputs),
        in_specs=specs(inputs, in_vmem),
        out_specs=specs(outputs, out_vmem),
        scratch_shapes=jax.tree.leaves(scratch),
        compiler_params=pltpu.CompilerParams(
            collective_id=collective_id, has_side_effects=True, vmem_limit_bytes=VMEM_LIMIT
        ),
        name=name,
    )(*jax.tree.leaves(inputs))
    return types.SimpleNamespace(**forms[1].unflatten(result))


def sems(*shape):
    return pltpu.SemaphoreType.DMA(shape)


def struct(shape, dtype):
    return jax.ShapeDtypeStruct(shape, dtype)


class Gather:
    def __init__(self, plan, rows, window):
        self.plan, self.rows = plan, rows
        self.start_column, self.columns = window
        self.padded = round_up(self.rows, 16)
        self.aligned = self.padded == self.rows
        self.group = plan.narrow * self.rows
        self.parts = halves(*window)
        self.orders = [plan.bits, plan.bits[::-1]][: len(self.parts)]
        self.chunks = plan.chunks

    def reserve(self):
        count, parts = self.plan.narrow, len(self.parts)
        shapes = [sems(2, count), sems(2, parts, self.chunks), sems(2, parts, self.chunks), sems(2)]
        if not self.aligned:
            shapes.append(pltpu.VMEM((count, self.padded, self.columns), BF16))
            shapes.append(pltpu.VMEM((self.group, self.columns), BF16))
        return shapes

    def bind(self, place, shard, out, refs):
        self.w, self.n = place
        self.shard, self.out = shard, out
        self.zsem, self.bsem, self.csem, self.lsem = refs[:4]
        if not self.aligned:
            self.stage, self.compact = refs[4:]

    def window(self):
        return pl.ds(self.start_column, self.columns)

    def own_slot(self):
        if self.aligned:
            rows = pl.ds(pl.multiple_of(self.n * self.rows, self.rows), self.rows)
            return self.out.at[self.w, rows, self.window()]
        return self.stage.at[self.n]

    def z_copy(self, d):
        return pltpu.make_async_remote_copy(
            src_ref=self.shard.at[:, self.window()],
            dst_ref=self.own_slot(),
            send_sem=self.zsem.at[0, d],
            recv_sem=self.zsem.at[1, d],
            device_id=(self.w, lax.rem(self.n + d, self.plan.narrow)),
            device_id_type=MESH,
        )

    def place_copy(self):
        return pltpu.make_async_copy(self.shard.at[:, self.window()], self.own_slot(), self.lsem.at[0])

    def group_copy(self):
        return pltpu.make_async_copy(self.compact, self.out.at[self.w, :, self.window()], self.lsem.at[1])

    def start(self):
        for d in range(1, self.plan.narrow):
            self.z_copy(d).start()
        self.place_copy().start()

    def hop(self, sems, part, mask, bit, slot):
        start, size = self.parts[part]
        target = self.out.at[self.w ^ mask, :, pl.ds(start, size)]
        source = target
        if mask == 0 and not self.aligned:
            source = self.compact.at[:, pl.ds(start - self.start_column, size)]
        return pltpu.make_async_remote_copy(
            src_ref=source,
            dst_ref=target,
            send_sem=sems.at[0, part, slot],
            recv_sem=sems.at[1, part, slot],
            device_id=(self.w ^ bit, self.n),
            device_id_type=MESH,
        )

    def hops(self, part, stage):
        order = self.orders[part]
        masks = span(order[:stage])
        return [self.hop(self.bsem, part, mask, order[stage], len(masks) + i - 1) for i, mask in enumerate(masks)]

    def core_hops(self, part, stage):
        masks = span(self.orders[part])
        low, high = (0, 1) if stage == 0 else (1 << (stage - 1), 1 << stage)
        return [self.hop(self.csem, part, masks[i], 1, i) for i in range(low, high)]

    def stages(self):
        return len(self.plan.bits) + 2

    def step(self, stage):
        bits, parts = len(self.plan.bits), range(len(self.parts))
        if stage == 0:
            for d in range(1, self.plan.narrow):
                self.z_copy(d).wait_recv()
            self.place_copy().wait()
            if not self.aligned:
                size, wide = self.group, self.plan.narrow * self.padded
                row = lax.broadcasted_iota(I32, (size, wide), 0)
                column = lax.broadcasted_iota(I32, (size, wide), 1)
                pick = column == (row // self.rows) * self.padded + row % self.rows
                self.compact[...] = matmul(
                    pick.astype(F32).astype(BF16), self.stage[...].reshape(wide, self.columns)
                ).astype(BF16)
                self.group_copy().start()
        elif stage <= bits:
            for part in parts:
                for copy in self.hops(part, stage - 1):
                    copy.wait_recv()
        else:
            for part in parts:
                for s in range(bits + 1):
                    for copy in self.core_hops(part, s):
                        copy.wait_recv()
            if not self.aligned:
                self.group_copy().wait()
        if stage < bits:
            for part in parts:
                for copy in self.hops(part, stage):
                    copy.start()
        if stage <= bits:
            for part in parts:
                for copy in self.core_hops(part, stage):
                    copy.start()

    def finish(self):
        for d in range(1, self.plan.narrow):
            self.z_copy(d).wait_send()
        for part in range(len(self.parts)):
            for s in range(len(self.plan.bits)):
                for copy in self.hops(part, s):
                    copy.wait_send()
            for s in range(len(self.plan.bits) + 1):
                for copy in self.core_hops(part, s):
                    copy.wait_send()


class Swap:
    def __init__(self, plan):
        self.plan = plan

    def reserve(self):
        return sems(3, self.plan.chunks)

    def bind(self, place, source, kept, sent, sem):
        self.w, self.n = place
        self.source, self.kept, self.sent, self.sem = source, kept, sent, sem
        self.group = source.shape[0] // self.plan.wide

    def chunk(self, index):
        return self.source.at[pl.ds(pl.multiple_of(index * self.group, self.group), self.group), :]

    def local(self, slot):
        return pltpu.make_async_copy(self.chunk(self.w ^ (2 * slot)), self.kept.at[slot], self.sem.at[2, slot])

    def remote(self, slot):
        return pltpu.make_async_remote_copy(
            src_ref=self.chunk(self.w ^ 1 ^ (2 * slot)),
            dst_ref=self.sent.at[slot],
            send_sem=self.sem.at[0, slot],
            recv_sem=self.sem.at[1, slot],
            device_id=(self.w ^ 1, self.n),
            device_id_type=MESH,
        )

    def start(self):
        for slot in range(self.plan.chunks):
            self.remote(slot).start()
            if self.kept is not None:
                self.local(slot).start()

    def wait_recv(self):
        for slot in range(self.plan.chunks):
            self.remote(slot).wait_recv()

    def finish(self):
        for slot in range(self.plan.chunks):
            self.remote(slot).wait_send()
            if self.kept is not None:
                self.local(slot).wait()


def to_sibling(place, source, target, sem):
    return pltpu.make_async_remote_copy(
        src_ref=source,
        dst_ref=target,
        send_sem=sem.at[0],
        recv_sem=sem.at[1],
        device_id=(place[0] ^ 1, place[1]),
        device_id_type=MESH,
    )


def column_of(row):
    eye = lax.broadcasted_iota(I32, (LANES, LANES), 0) == lax.broadcasted_iota(I32, (LANES, LANES), 1)
    pieces = [
        jnp.sum(jnp.where(eye, row[:, start : start + LANES], 0.0), axis=1, keepdims=True)
        for start in range(0, row.shape[1], LANES)
    ]
    return jnp.concatenate(pieces, axis=0)


def unpack_small(plan, packed, sizes):
    summed = jnp.sum(packed.astype(F32).reshape(plan.wide, plan.narrow, 16, LANES), axis=1)
    rows = []
    for i, size in enumerate(sizes):
        each = LANES // (size * plan.narrow)
        blocks = [
            sum(summed[first + j, i : i + 1, :] for j in range(each))
            for first in range(0, plan.wide, each)
        ]
        rows.append(jnp.concatenate(blocks, axis=1))
    return rows


def same_bucket(width):
    row = lax.broadcasted_iota(I32, (width, width), 0) // HEADS
    column = lax.broadcasted_iota(I32, (width, width), 1) // HEADS
    return (row == column).astype(F32)


def spread_table(table_row):
    width = BUCKETS * HEADS
    lane = lax.broadcasted_iota(I32, (HEADS, width), 1)
    head = lax.broadcasted_iota(I32, (HEADS, width), 0)
    same = lane % HEADS == head
    picked = jnp.where(same, table_row, 0.0).astype(BF16)
    spread = matmul(picked, same_bucket(width).astype(BF16))
    return jnp.concatenate(
        [jnp.where(same, spread[h : h + 1, :], 0.0).astype(BF16) for h in range(HEADS)], axis=0
    )


def bucket_rows(bucket):
    small = bucket.astype(F32).astype(BF16)
    one, zero = jnp.ones_like(small), jnp.zeros_like(small)
    return jnp.concatenate(
        [jnp.where(small == jnp.asarray(j, BF16), one, zero) for j in range(BUCKETS)], axis=0
    )


class Sizes:
    def __init__(self, plan, rows, width, ff, shards):
        self.plan, self.rows, self.width, self.ff = plan, rows, width, ff
        self.shards = shards
        self.group = plan.narrow * shards[0]
        self.down_group = plan.narrow * shards[6]
        self.split = round_up(ff // 2, TILE)
        self.ff_windows = [(0, self.split), (self.split, ff - self.split)]
        self.half_windows = [(0, width // 2), (width // 2, width // 2)]

    def full(self):
        wide = self.plan.wide
        return (
            [(wide, self.group, self.width)] * 4
            + [(wide, self.group, self.ff)] * 2
            + [(wide, self.down_group, self.width)]
        )


QUERY, KEY, VALUE, OUT, GATE, UP, DOWN = range(7)


class Forward:
    def __init__(self, plan, sizes):
        self.plan, self.sizes = plan, sizes
        whole = (0, sizes.width)
        wide = [(weight, window) for window in sizes.ff_windows for weight in (GATE, UP)]
        down = [(DOWN, window) for window in sizes.half_windows]
        self.order = [(weight, whole) for weight in (QUERY, KEY, VALUE, OUT)] + wide + down
        self.small = Gather(plan, 16, (0, LANES))
        self.items = [self.small] + [Gather(plan, sizes.shards[weight], window) for weight, window in self.order]
        self.swaps = [Swap(plan) for _ in range(4)]
        self.extra = self.small.stages() - 4

    def call(self, small, shards, tokens, keep, live, buckets, cotangent):
        plan, s = self.plan, self.sizes
        rows, width, ff, chunks = s.rows, s.width, s.ff, plan.chunks
        turned = struct((2, chunks, s.group, rows), BF16)
        row_block, ff_block = struct((rows, width), BF16), struct((rows, ff), BF16)
        inputs = dict(
            small=small, shards=shards, tokens=tokens, keep=keep, live=live, buckets=buckets, cotangent=cotangent
        )
        outputs = dict(
            small=struct((plan.wide, plan.narrow * 16, LANES), BF16),
            full=[struct(shape, BF16) for shape in s.full()],
            queries=row_block,
            keys=row_block,
            values=row_block,
            prob=struct((HEADS, rows, rows), BF16),
            mid=struct((rows, width), F32),
            hidden=ff_block,
            gate_slope=ff_block,
            up_slope=ff_block,
            turned=[turned] * 3,
            grad_down=struct((chunks, s.down_group, width), BF16),
            rows=struct((8, width), F32),
        )
        square, stream = pltpu.VMEM((rows, width), BF16), pltpu.VMEM((rows, width), F32)
        scratch = dict(
            items=[item.reserve() for item in self.items],
            swaps=[swap.reserve() for swap in self.swaps],
            direct=sems(2),
            held=[pltpu.VMEM(shape, BF16) for shape in s.full()[:3] + s.full()[4:6]],
            load=sems(len(self.items)),
            small=pltpu.VMEM((plan.wide, plan.narrow * 16, LANES), BF16),
            keep=pltpu.VMEM((rows, 1), F32),
            table=pltpu.VMEM((HEADS * 16, BUCKETS * 16), BF16),
            bias=pltpu.VMEM((HEADS, rows, rows), BF16),
            stream=stream,
            normed=square,
            q=square,
            k=square,
            v=square,
            attended=square,
            normed_turned=pltpu.VMEM((width, rows), BF16),
            attended_turned=pltpu.VMEM((width, rows), BF16),
            hidden_turned=pltpu.VMEM((ff, rows), BF16),
            hidden_far=pltpu.VMEM((chunks, s.down_group, rows), BF16),
            cot_far=square,
            prob_stage=pltpu.VMEM((2, 2, rows, rows), BF16),
            prob_sem=sems(2),
            tile_stage=pltpu.VMEM((2, 3, rows, TILE), BF16),
            tile_sem=sems(2, 3),
            down_stage=pltpu.VMEM((2, s.down_group, width), BF16),
            down_sem=sems(2),
            store=sems(4),
        )
        return run(
            self.kernel,
            inputs,
            outputs,
            scratch,
            {"tokens", "keep", "live", "buckets", "cotangent"},
            {"rows"},
            0,
            "gather_forward",
        )

    def kernel(self, i, o, t):
        self.i, self.o, self.t = i, o, t
        self.place = place = enter(self.plan)
        self.small.bind(place, i.small, o.small, t.items[0])
        for item, (weight, _), refs in zip(self.items[1:], self.order, t.items[1:]):
            item.bind(place, i.shards[weight], o.full[weight], refs)
        direct = to_sibling(place, i.cotangent, t.cot_far, t.direct)
        normed, attended, second, hidden = self.swaps
        for swap, source, target, sem in zip(
            self.swaps, (t.normed_turned, t.attended_turned, t.normed_turned), o.turned, t.swaps
        ):
            swap.bind(place, source, target.at[0], target.at[1], sem)
        hidden.bind(place, t.hidden_turned, None, t.hidden_far, t.swaps[3])
        pairs = ((t.q, o.queries), (t.k, o.keys), (t.v, o.values), (t.stream, o.mid))
        store = [pltpu.make_async_copy(*pair, t.store.at[at_]) for at_, pair in enumerate(pairs)]

        for item in self.items[:3]:
            item.start()
        direct.start()
        for turn in range(-self.extra, 4):
            self.tick(turn)
        self.set_up()
        normed.start()
        self.tick(4)
        blocks = self.sizes.rows // 16
        self.bias(0, blocks // 2)
        self.tick(5)
        self.project(QUERY, t.q)
        store[0].start()
        self.bias(blocks // 2, blocks)
        self.tick(6)
        self.project(KEY, t.k)
        store[1].start()
        self.tick(7)
        self.project(VALUE, t.v)
        store[2].start()
        count = HEADS // 2
        self.attend(0, count // 4)
        self.tick(8)
        self.attend(count // 4, 5 * count // 8)
        self.tick(9)
        self.attend(5 * count // 8, count)
        for slot in range(2):
            self.prob_copy(slot, count - 2 + slot).wait()
        self.out_project()
        store[3].start()
        attended.start()
        normed.finish()
        self.norm(2)
        second.start()
        self.tick(10)
        tiles, first = self.sizes.ff // TILE, self.sizes.split // TILE
        self.feed(0, first)
        self.tick(11)
        self.feed(first, tiles)
        for j in (tiles - 2, tiles - 1):
            for copy in self.tile_copies(j % 2, j):
                copy.wait()
        hidden.start()
        self.tick(12)
        direct.wait_recv()
        hidden.wait_recv()
        self.down_gradient()
        self.tick(13)
        for item in self.items:
            item.finish()
        direct.wait_send()
        hidden.finish()
        attended.finish()
        second.finish()
        for swap in (normed, attended, second):
            swap.wait_recv()
        for copy in store:
            copy.wait()

    def held(self, weight):
        return self.t.held[{QUERY: 0, KEY: 1, VALUE: 2, OUT: 0, GATE: 3, UP: 4}[weight]]

    def load(self, k):
        if k == 0:
            return pltpu.make_async_copy(self.o.small, self.t.small, self.t.load.at[0])
        weight, window = self.order[k - 1]
        columns = pl.ds(*window)
        return pltpu.make_async_copy(
            self.o.full[weight].at[:, :, columns], self.held(weight).at[:, :, columns], self.t.load.at[k]
        )

    def tick(self, turn):
        stages, turn = self.small.stages(), turn + self.extra
        for stage in range(stages):
            k = turn - stage
            if 0 <= k < len(self.items):
                self.items[k].step(stage)
                if stage == stages - 1 and (k == 0 or self.order[k - 1][0] != DOWN):
                    self.load(k).start()
        if turn + 3 < len(self.items):
            self.items[turn + 3].start()

    def set_up(self):
        i, o, t = self.i, self.o, self.t
        self.load(0).wait()
        devices = self.plan.wide * self.plan.narrow
        counts = [self.sizes.width // devices] * 3 + [BUCKETS * HEADS // devices]
        embed, gain_one, gain_two, table = unpack_small(self.plan, t.small[...], counts)
        o.rows[...] = jnp.concatenate(
            [embed, gain_one, gain_two, jnp.zeros((5, self.sizes.width), F32)], axis=0
        )
        t.table[...] = spread_table(table)
        t.keep[...] = column_of(i.keep[...].astype(F32))

        def body(j):
            block = at(j, 64)
            t.stream[block, :] = jnp.where(
                t.keep[block, :] > 0.5, i.tokens[block, :].astype(F32), o.rows[0:1, :]
            )

        loop(0, self.sizes.rows // 64, body)
        self.norm(1)

    def norm(self, gain):
        o, t = self.o, self.t

        def body(j):
            block = at(j, 64)
            x = t.stream[block, :]
            scale = lax.rsqrt(jnp.mean(x * x, axis=-1, keepdims=True) + EPSILON)
            t.normed[block, :] = (x * scale * o.rows[gain : gain + 1, :]).astype(BF16)

        loop(0, self.sizes.rows // 64, body)
        self.turn(t.normed, t.normed_turned)

    def turn(self, source, target):
        def body(j):
            target[at(j, LANES), :] = source[:, at(j, LANES)].T

        loop(0, self.sizes.width // LANES, body)

    def bias(self, low, high):
        i, t = self.i, self.t

        def body(j):
            block = at(j, 16)
            spread = matmul(t.table[...], bucket_rows(i.buckets[block, :]))
            spread = jnp.where(i.live[...] > 0, spread, NEG_FILL).astype(BF16)
            t.bias[:, block, :] = spread.reshape(HEADS, 16, spread.shape[-1])

        loop(low, high, body)

    def project(self, weight, target):
        self.load(1 + weight).wait()
        held, width = self.held(weight), self.sizes.width

        def body(j):
            block = held[:, :, at(j, TILE)].reshape(width, TILE)
            target[:, at(j, TILE)] = matmul(self.t.normed[...], block).astype(BF16)

        loop(0, width // TILE, body)

    def prob_copy(self, slot, pair):
        t = self.t
        return pltpu.make_async_copy(
            t.prob_stage.at[slot], self.o.prob.at[pl.ds(2 * pair, 2)], t.prob_sem.at[slot]
        )

    def attend(self, low, high):
        t = self.t
        lane = lax.broadcasted_iota(I32, (1, LANES), 1)

        def body(pair):
            columns, slot = at(pair, LANES), lax.rem(pair, 2)

            @pl.when(pair >= 2)
            def _():
                self.prob_copy(slot, pair).wait()

            q, k, v = t.q[:, columns], t.k[:, columns], t.v[:, columns]
            mixed = []
            for e in range(2):
                own = jnp.where((lane < HEAD) == (e == 0), q, jnp.zeros_like(q))
                scores = times_trans(own, k) + t.bias[2 * pair + e].astype(F32)
                top = jnp.max(scores, axis=-1, keepdims=True)
                powers = jnp.exp(scores - top)
                total = jnp.sum(powers, axis=-1, keepdims=True)
                prob = (powers * (1.0 / total)).astype(BF16)
                t.prob_stage[slot, e] = prob
                mixed.append(matmul(prob, v))
            t.attended[:, columns] = jnp.where(lane < HEAD, mixed[0], mixed[1]).astype(BF16)
            self.prob_copy(slot, pair).start()

        loop(low, high, body)

    def out_project(self):
        t, width = self.t, self.sizes.width
        self.load(1 + OUT).wait()

        def body(j):
            block = self.held(OUT)[:, :, at(j, TILE)].reshape(width, TILE)
            t.stream[:, at(j, TILE)] += matmul(t.attended[...], block)

        loop(0, width // TILE, body)
        self.turn(t.attended, t.attended_turned)

    def tile_copies(self, slot, j):
        o, t = self.o, self.t
        return [
            pltpu.make_async_copy(t.tile_stage.at[slot, which], ref.at[:, at(j, TILE)], t.tile_sem.at[slot, which])
            for which, ref in enumerate((o.hidden, o.gate_slope, o.up_slope))
        ]

    def feed(self, low, high):
        t, width = self.t, self.sizes.width
        for k, (weight, window) in enumerate(self.order):
            if weight in (GATE, UP) and window[0] == low * TILE:
                self.load(1 + k).wait()

        def body(j):
            slot = lax.rem(j, 2)

            @pl.when(j >= 2)
            def _():
                for copy in self.tile_copies(slot, j):
                    copy.wait()

            second = t.normed[...]
            gate = matmul(second, self.held(GATE)[:, :, at(j, TILE)].reshape(width, TILE))
            up = matmul(second, self.held(UP)[:, :, at(j, TILE)].reshape(width, TILE))
            square = gate * gate
            bend = jnp.tanh(GELU_SCALE * gate * (1.0 + GELU_CUBE * square))
            half = 0.5 * (1.0 + bend)
            act = gate * half
            slope = half + (0.5 * GELU_SCALE) * gate * (1.0 - bend * bend) * (1.0 + (3.0 * GELU_CUBE) * square)
            hidden = (act * up).astype(BF16)
            t.tile_stage[slot, 0] = hidden
            t.tile_stage[slot, 1] = (up * slope).astype(BF16)
            t.tile_stage[slot, 2] = act.astype(BF16)
            for copy in self.tile_copies(slot, j):
                copy.start()
            t.hidden_turned[at(j, TILE), :] = hidden.T

        loop(low, high, body)

    def down_copy(self, slot):
        t = self.t
        return pltpu.make_async_copy(t.down_stage.at[slot % 2], self.o.grad_down.at[slot], t.down_sem.at[slot % 2])

    def down_gradient(self):
        i, t, group = self.i, self.t, self.sizes.down_group
        for slot in range(self.plan.chunks):
            if slot >= 2:
                self.down_copy(slot - 2).wait()

            def body(j, slot=slot):
                near = t.hidden_turned[at(self.place[0] ^ (2 * slot), group), :]
                t.down_stage[slot % 2, :, at(j, TILE)] = (
                    matmul(near, i.cotangent[:, at(j, TILE)])
                    + matmul(t.hidden_far[slot], t.cot_far[:, at(j, TILE)])
                ).astype(BF16)

            loop(0, self.sizes.width // TILE, body)
            self.down_copy(slot).start()
        for slot in range(self.plan.chunks - 2, self.plan.chunks):
            self.down_copy(slot).wait()


class Reduce:
    def __init__(self, plan, rows, window, order):
        self.plan, self.rows = plan, rows
        self.start_column, self.columns = window
        self.padded = round_up(rows, 16)
        self.aligned = self.padded == rows
        self.group = plan.narrow * rows
        self.order = order
        self.chunks = plan.chunks

    def reserve(self):
        count, columns = self.plan.narrow, self.columns
        shapes = [
            sems(2, self.chunks),
            sems(2, count),
            pltpu.VMEM((self.chunks, self.group, columns), BF16),
            pltpu.VMEM((self.chunks - 1, self.group, columns), BF16),
            pltpu.VMEM((count - 1, self.padded, columns), BF16),
        ]
        if not self.aligned:
            shapes.append(pltpu.VMEM((count, self.padded, columns), BF16))
        return shapes

    def bind(self, place, out, refs):
        self.w, self.n = place
        self.out, self.done = out, 0
        self.bsem, self.zsem, self.acc, self.received, self.zreceived = refs[:5]
        if not self.aligned:
            self.stage = refs[5]

    def hops(self, stage):
        bit, masks = self.order[stage], span(self.order[stage + 1 :])
        base = self.chunks - 2 * len(masks)
        return [
            (
                mask >> 1,
                base + k,
                pltpu.make_async_remote_copy(
                    src_ref=self.acc.at[(bit ^ mask) >> 1],
                    dst_ref=self.received.at[base + k],
                    send_sem=self.bsem.at[0, base + k],
                    recv_sem=self.bsem.at[1, base + k],
                    device_id=(self.w ^ bit, self.n),
                    device_id_type=MESH,
                ),
            )
            for k, mask in enumerate(masks)
        ]

    def z_copy(self, d):
        peer = lax.rem(self.n + d, self.plan.narrow)
        source = self.acc.at[0, at(peer, self.rows), :] if self.aligned else self.stage.at[peer]
        return pltpu.make_async_remote_copy(
            src_ref=source,
            dst_ref=self.zreceived.at[d - 1],
            send_sem=self.zsem.at[0, d],
            recv_sem=self.zsem.at[1, d],
            device_id=(self.w, peer),
            device_id_type=MESH,
        )

    def step(self, stage):
        bits = len(self.order)
        if 1 <= stage <= bits:
            for slot, k, copy in self.hops(stage - 1):
                copy.wait_recv()

                def body(j, slot=slot, k=k):
                    block = at(j, 16)
                    self.acc[slot, block, :] += self.received[k, block, :]

                loop(0, self.group // 16, body)
        if stage < bits:
            for _, _, copy in self.hops(stage):
                copy.start()
        elif stage == bits:
            if not self.aligned:
                size, wide = self.group, self.plan.narrow * self.padded
                row = lax.broadcasted_iota(I32, (wide, size), 0)
                column = lax.broadcasted_iota(I32, (wide, size), 1)
                pick = row == (column // self.rows) * self.padded + column % self.rows
                self.stage[...] = (
                    matmul(pick.astype(F32).astype(BF16), self.acc[0]).astype(BF16).reshape(self.stage.shape)
                )
            for d in range(1, self.plan.narrow):
                self.z_copy(d).start()
        else:
            total = self.acc[0, at(self.n, self.rows), :] if self.aligned else self.stage[self.n]
            total = total.astype(F32)
            for d in range(1, self.plan.narrow):
                self.z_copy(d).wait_recv()
                total = total + self.zreceived[d - 1].astype(F32)
            self.out[:, pl.ds(self.start_column, self.columns)] = total[: self.rows]

    def finish(self):
        for stage in range(len(self.order)):
            for _, _, copy in self.hops(stage):
                copy.wait_send()
        for d in range(1, self.plan.narrow):
            self.z_copy(d).wait_send()


class SumAll:
    def __init__(self, plan, shape):
        self.shape = shape
        self.rounds = [(bit, 0) for bit in [1] + plan.bits]
        self.rounds += [(0, 1 << k) for k in range(plan.narrow.bit_length() - 1)]

    def reserve(self):
        count = len(self.rounds)
        return [sems(2, count)] + [pltpu.VMEM((count, *self.shape), F32)] * 2

    def bind(self, place, out, refs):
        self.w, self.n = place
        self.out = out
        self.sem, self.held, self.received = refs

    def copy(self, turn):
        bit, other = self.rounds[turn]
        return pltpu.make_async_remote_copy(
            src_ref=self.held.at[turn],
            dst_ref=self.received.at[turn],
            send_sem=self.sem.at[0, turn],
            recv_sem=self.sem.at[1, turn],
            device_id=(self.w ^ bit, self.n ^ other),
            device_id_type=MESH,
        )

    def start(self, value):
        self.held[0] = value
        self.copy(0).start()

    def step(self, turn):
        self.copy(turn).wait_recv()
        total = self.held[turn] + self.received[turn]
        if turn + 1 < len(self.rounds):
            self.held[turn + 1] = total
            self.copy(turn + 1).start()
        else:
            self.out[...] = total

    def finish(self):
        for turn in range(len(self.rounds)):
            self.copy(turn).wait_send()


class Backward:
    def __init__(self, plan, sizes):
        self.plan, self.sizes = plan, sizes
        ways = [plan.bits, plan.bits[::-1]]
        self.reduces = []
        for weight in range(7):
            windows = sizes.ff_windows if weight in (GATE, UP) else sizes.half_windows
            turn = 1 if weight in (UP, KEY, OUT) else 0
            self.reduces.append(
                [Reduce(plan, sizes.shards[weight], window, ways[k ^ turn]) for k, window in enumerate(windows)]
            )
        self.sums = SumAll(plan, (8, sizes.width))

    def call(self, f, tokens, keep, buckets, cotangent):
        plan, s = self.plan, self.sizes
        rows, width, ff, chunks = s.rows, s.width, s.ff, plan.chunks
        inputs = dict(
            full=f.full,
            queries=f.queries,
            keys=f.keys,
            values=f.values,
            prob=f.prob,
            mid=f.mid,
            hidden=f.hidden,
            gate_slope=f.gate_slope,
            up_slope=f.up_slope,
            turned=f.turned,
            grad_down=f.grad_down,
            rows=f.rows,
            tokens=tokens,
            keep=keep,
            buckets=buckets,
            cotangent=cotangent,
        )
        row_block = struct((rows, width), BF16)
        outputs = dict(
            result=row_block,
            input_grad=struct((rows, width), F32),
            grads=[struct((size, ff if weight in (GATE, UP) else width), F32) for weight, size in enumerate(s.shards)],
            sums=struct((8, width), F32),
            far_ff=[struct((rows, ff), BF16)] * 2,
            far_out=row_block,
            far_attn=[row_block] * 3,
        )
        square = pltpu.VMEM((rows, width), BF16)
        scratch = dict(
            reduces=[[item.reserve() for item in pair] for pair in self.reduces],
            small=self.sums.reserve(),
            keep=pltpu.VMEM((rows, 1), F32),
            stream=pltpu.VMEM((rows, width), F32),
            back=pltpu.VMEM((rows, width), F32),
            totals=pltpu.VMEM((8, width), F32),
            grad_mid=square,
            grad_attended=square,
            grad_qkv=[square] * 3,
            acc_sem=sems(2, chunks),
            load=sems(8),
            ff_sem=sems(2, 2, 2),
            out_sem=sems(2),
            attn_sem=sems(2, 3, 2),
            tile_sem=sems(2, 3),
            result_sem=sems(2),
        )
        return run(
            self.kernel,
            inputs,
            outputs,
            scratch,
            {"rows", "tokens", "keep", "buckets", "cotangent"},
            {"grads", "sums"},
            1,
            "backward_reduce",
        )

    def advance(self, weight, parts=(0, 1)):
        for part in parts:
            item = self.reduces[weight][part]
            item.step(item.done)
            item.done += 1

    def kernel(self, i, o, t):
        self.i, self.o, self.t = i, o, t
        plan, s = self.plan, self.sizes
        self.place = place = enter(plan)
        for pair, out, refs in zip(self.reduces, o.grads, t.reduces):
            for item, own in zip(pair, refs):
                item.bind(place, out, own)
        self.sums.bind(place, o.sums, t.small)
        last = len(plan.bits) + 1

        mid = pltpu.make_async_copy(i.mid, t.stream, t.load.at[0])
        mid.start()
        loads = []
        for part, (start, size) in enumerate(s.half_windows):
            for slot in range(plan.chunks):
                loads.append(
                    pltpu.make_async_copy(
                        i.grad_down.at[slot, :, pl.ds(start, size)],
                        self.reduces[DOWN][part].acc.at[slot],
                        t.acc_sem.at[part, slot],
                    )
                )
                loads[-1].start()
        for copy in loads:
            copy.wait()
        self.advance(DOWN)
        t.keep[...] = column_of(i.keep[...].astype(F32))
        t.totals[...] = jnp.zeros_like(t.totals)

        def feed_phase(near, turned, sem):
            turned_copy = pltpu.make_async_copy(i.turned[2], turned, sem)
            turned_copy.start()
            pl.run_scoped(
                functools.partial(self.feed_back, near, mid),
                pltpu.VMEM((s.ff, s.width), BF16),
                pltpu.VMEM((2, 2, s.rows, TILE), BF16),
                pltpu.VMEM((s.rows, s.ff), BF16),
                pltpu.VMEM((s.rows, s.width), BF16),
                sems(plan.wide),
                sems(2),
            )
            turned_copy.wait()
            pl.run_scoped(
                functools.partial(self.feed_weights, near, turned),
                pltpu.VMEM((2, 2, s.rows, TILE), BF16),
            )
            groups = TILE // s.group
            pl.run_scoped(
                functools.partial(self.feed_input, near),
                pltpu.VMEM((2, 2, groups, s.group, s.ff), BF16),
            )
            for part in range(2):
                for copy in self.ff_copies(near, part):
                    copy.wait_send()

        pl.run_scoped(
            feed_phase,
            [pltpu.VMEM((s.rows, s.ff), BF16)] * 2,
            pltpu.VMEM((2, plan.chunks, s.group, s.rows), BF16),
            pltpu.SemaphoreType.DMA,
        )
        self.norm_back(2)
        out_copy = to_sibling(place, t.grad_mid, o.far_out, t.out_sem)
        out_copy.start()
        pl.run_scoped(
            functools.partial(self.out_back, out_copy),
            pltpu.VMEM((plan.wide, s.group, s.width), BF16),
            pltpu.VMEM((2, plan.chunks, s.group, s.rows), BF16),
            pltpu.VMEM((s.rows, s.width), BF16),
            sems(3),
        )
        self.advance(DOWN)

        def attention_phase(q, k, v, grad_scores, prob, turned, far, sem):
            copies = [
                pltpu.make_async_copy(source, target, sem.at[which])
                for which, (source, target) in enumerate(
                    ((i.queries, q), (i.keys, k), (i.values, v), (i.turned[0], turned))
                )
            ]
            for copy in copies:
                copy.start()
            for copy in copies:
                copy.wait()
            half = HEADS // 4
            self.attend_back(0, half, q, k, v, grad_scores, prob)
            self.send_attention(0)
            self.advance(GATE)
            self.advance(UP)
            self.attention_weights(0, turned, far, sem.at[4])
            self.advance(DOWN)
            self.attend_back(half, 2 * half, q, k, v, grad_scores, prob)
            self.send_attention(1)
            self.advance(OUT)
            self.advance(GATE)
            self.advance(UP)
            self.attention_weights(1, turned, far, sem.at[4])
            self.table_back(grad_scores)

        pl.run_scoped(
            attention_phase,
            *[pltpu.VMEM((s.rows, s.width), BF16)] * 3,
            pltpu.VMEM((HEADS, s.rows, s.rows), BF16),
            pltpu.VMEM((2, 2, s.rows, s.rows), BF16),
            pltpu.VMEM((2, plan.chunks, s.group, s.rows), BF16),
            pltpu.VMEM((3, s.rows, s.width // 2), BF16),
            sems(5),
        )
        self.advance(OUT)
        for weight in (QUERY, KEY, VALUE):
            self.advance(weight)
        groups = TILE // s.group
        pl.run_scoped(self.attention_input, pltpu.VMEM((2, 3, groups, s.group, s.width), BF16))
        self.norm_back(1)
        self.sums.start(t.totals[...])
        store = pltpu.make_async_copy(t.stream, o.input_grad, t.load.at[1])
        store.start()
        turn = 0
        left = [GATE, UP, QUERY, KEY, VALUE, OUT, DOWN]
        while left:
            for weight in list(left):
                if self.reduces[weight][0].done > last:
                    left.remove(weight)
                    continue
                self.advance(weight)
                if turn < len(self.sums.rounds):
                    self.sums.step(turn)
                turn += 1
        store.wait()
        out_copy.wait_send()
        for part in range(2):
            for copy in self.attention_copies(part):
                copy.wait_send()
        for pair in self.reduces:
            for item in pair:
                item.finish()
        self.sums.finish()

    def ff_copies(self, near, part):
        window = pl.ds(*self.sizes.ff_windows[part])
        return [
            to_sibling(
                self.place, near[which].at[:, window], self.o.far_ff[which].at[:, window], self.t.ff_sem.at[part, which]
            )
            for which in range(2)
        ]

    def feed_back(self, near, mid, down, slopes, hidden, result, sem, other):
        i, o, t, s = self.i, self.o, self.t, self.sizes
        group = s.down_group
        copies = [
            pltpu.make_async_copy(i.full[DOWN].at[k], down.at[pl.ds(k * group, group), :], sem.at[k])
            for k in range(self.plan.wide)
        ]
        for copy in copies:
            copy.start()
        hidden_copy = pltpu.make_async_copy(i.hidden, hidden, other.at[0])
        hidden_copy.start()
        for copy in copies:
            copy.wait()

        def slope_copies(slot, j):
            return [
                pltpu.make_async_copy(ref.at[:, at(j, TILE)], slopes.at[slot, which], t.tile_sem.at[slot, which])
                for which, ref in enumerate((i.gate_slope, i.up_slope))
            ]

        def body(j, slot):
            grad_act = times_trans(i.cotangent[...], down[at(j, TILE), :])
            for which in range(2):
                near[which][:, at(j, TILE)] = (grad_act * slopes[slot, which].astype(F32)).astype(BF16)

        edges = [0, s.split // TILE, s.ff // TILE]
        for part in range(2):
            streamed(edges[part], edges[part + 1], slope_copies, body)
            for copy in self.ff_copies(near, part):
                copy.start()
        hidden_copy.wait()
        mid.wait()

        def finish(j):
            block = at(j, TILE)
            result[:, block] = (t.stream[:, block] + matmul(hidden[...], down[:, block])).astype(BF16)

        loop(0, s.width // TILE, finish)
        store = pltpu.make_async_copy(result, o.result, other.at[1])
        store.start()
        store.wait()

    def feed_weights(self, near, turned, far):
        o, t, s = self.o, self.t, self.sizes

        def far_copies(slot, j):
            return [
                pltpu.make_async_copy(o.far_ff[which].at[:, at(j, TILE)], far.at[slot, which], t.tile_sem.at[slot, which])
                for which in range(2)
            ]

        edges = [0, s.split // TILE, s.ff // TILE]
        rows = self.plan.chunks * s.group
        for part in range(2):
            for copy in self.ff_copies(near, part):
                copy.wait_recv()

            def body(j, slot, part=part):
                for which, weight in enumerate((GATE, UP)):
                    own = turned[0].reshape(rows, s.rows)
                    other = turned[1].reshape(rows, s.rows)
                    grad = matmul(own, near[which][:, at(j, TILE)]) + matmul(other, far[slot, which])
                    acc = self.reduces[weight][part].acc
                    acc[:, :, at(j - edges[part], TILE)] = grad.astype(BF16).reshape(self.plan.chunks, s.group, TILE)

            streamed(edges[part], edges[part + 1], far_copies, body)
            self.advance(GATE, (part,))
            self.advance(UP, (part,))
            if part == 0:
                self.advance(DOWN)

    def feed_input(self, near, held):
        i, t, s = self.i, self.t, self.sizes
        groups = TILE // s.group

        def weight_copies(slot, j):
            return [
                pltpu.make_async_copy(i.full[weight].at[pl.ds(j * groups, groups)], held.at[slot, which], t.tile_sem.at[slot, which])
                for which, weight in enumerate((GATE, UP))
            ]

        def body(j, slot):
            t.back[:, at(j, TILE)] = times_trans(near[0][...], held[slot, 0].reshape(TILE, s.ff)) + times_trans(
                near[1][...], held[slot, 1].reshape(TILE, s.ff)
            )

        streamed(0, s.width // TILE, weight_copies, body)

    def norm_back(self, which):
        i, t, s = self.i, self.t, self.sizes

        def body(j):
            block = at(j, 32)
            kept = t.keep[block, :] > 0.5
            back = t.back[block, :]
            if which == 2:
                x = t.stream[block, :]
                before = i.cotangent[block, :].astype(F32)
            else:
                x = jnp.where(kept, i.tokens[block, :].astype(F32), i.rows[0:1, :])
                before = t.stream[block, :]
            scale = lax.rsqrt(jnp.mean(x * x, axis=-1, keepdims=True) + EPSILON)
            scaled = x * scale
            u = back * i.rows[which : which + 1, :]
            inner = jnp.mean(u * scaled, axis=-1, keepdims=True)
            total = before + scale * (u - scaled * inner)
            t.totals[which : which + 1, :] += jnp.sum(back * scaled, axis=0, keepdims=True)
            if which == 2:
                t.stream[block, :] = total
                t.grad_mid[block, :] = total.astype(BF16)
            else:
                t.stream[block, :] = jnp.where(kept, total, 0.0)
                t.totals[0:1, :] += jnp.sum(jnp.where(kept, 0.0, total), axis=0, keepdims=True)

        loop(0, s.rows // 32, body)

    def out_back(self, out_copy, weight, turned, far, sem):
        i, o, t, s = self.i, self.o, self.t, self.sizes
        copies = [
            pltpu.make_async_copy(i.full[OUT], weight, sem.at[0]),
            pltpu.make_async_copy(i.turned[1], turned, sem.at[1]),
        ]
        for copy in copies:
            copy.start()
        for copy in copies:
            copy.wait()
        groups = TILE // s.group

        def attended(j):
            block = weight[pl.ds(j * groups, groups)].reshape(TILE, s.width)
            t.grad_attended[:, at(j, TILE)] = times_trans(t.grad_mid[...], block).astype(BF16)

        loop(0, s.width // TILE, attended)
        out_copy.wait_recv()
        load = pltpu.make_async_copy(o.far_out, far, sem.at[2])
        load.start()
        load.wait()
        rows = self.plan.chunks * s.group
        for part, (start, size) in enumerate(s.half_windows):

            def body(j, part=part, start=start):
                columns = pl.ds(pl.multiple_of(start + j * TILE, TILE), TILE)
                grad = matmul(turned[0].reshape(rows, s.rows), t.grad_mid[:, columns])
                grad += matmul(turned[1].reshape(rows, s.rows), far[:, columns])
                self.reduces[OUT][part].acc[:, :, at(j, TILE)] = grad.astype(BF16).reshape(
                    self.plan.chunks, s.group, TILE
                )

            loop(0, size // TILE, body)
            self.advance(OUT, (part,))

    def attend_back(self, low, high, q, k, v, grad_scores, prob):
        i, t = self.i, self.t
        lane = lax.broadcasted_iota(I32, (1, LANES), 1)

        def prob_copies(slot, pair):
            return [pltpu.make_async_copy(i.prob.at[pl.ds(2 * pair, 2)], prob.at[slot], t.tile_sem.at[slot, 0])]

        def body(pair, slot):
            columns = at(pair, LANES)
            q_pair, k_pair, v_pair, grad = q[:, columns], k[:, columns], v[:, columns], t.grad_attended[:, columns]
            found = [[], [], []]
            for e in range(2):
                own = jnp.where((lane < HEAD) == (e == 0), grad, jnp.zeros_like(grad))
                weights = prob[slot, e]
                wide = weights.astype(F32)
                grad_prob = times_trans(own, v_pair)
                delta = jnp.sum(grad_prob * wide, axis=-1, keepdims=True)
                scores = (wide * (grad_prob - delta)).astype(BF16)
                grad_scores[2 * pair + e] = scores
                found[0].append(matmul(scores, k_pair))
                found[1].append(trans_times(scores, q_pair))
                found[2].append(trans_times(weights, grad))
            for ref, (first, second) in zip(t.grad_qkv, found):
                ref[:, columns] = jnp.where(lane < HEAD, first, second).astype(BF16)

        streamed(low, high, prob_copies, body)

    def attention_copies(self, part):
        window = pl.ds(*self.sizes.half_windows[part])
        return [
            to_sibling(
                self.place,
                self.t.grad_qkv[which].at[:, window],
                self.o.far_attn[which].at[:, window],
                self.t.attn_sem.at[part, which],
            )
            for which in range(3)
        ]

    def send_attention(self, part):
        for copy in self.attention_copies(part):
            copy.start()

    def attention_weights(self, part, turned, far, sem):
        o, t, s = self.o, self.t, self.sizes
        start, size = s.half_windows[part]
        rows = self.plan.chunks * s.group
        for which, copy in enumerate(self.attention_copies(part)):
            copy.wait_recv()
            load = pltpu.make_async_copy(o.far_attn[which].at[:, pl.ds(start, size)], far.at[which], sem)
            load.start()
            load.wait()

            def body(j, which=which):
                columns = pl.ds(pl.multiple_of(start + j * TILE, TILE), TILE)
                grad = matmul(turned[0].reshape(rows, s.rows), t.grad_qkv[which][:, columns])
                grad += matmul(turned[1].reshape(rows, s.rows), far[which, :, at(j, TILE)])
                self.reduces[which][part].acc[:, :, at(j, TILE)] = grad.astype(BF16).reshape(
                    self.plan.chunks, s.group, TILE
                )

            loop(0, size // TILE, body)
            self.advance(which, (part,))

    def attention_input(self, held):
        i, t, s = self.i, self.t, self.sizes
        groups = TILE // s.group

        def weight_copies(slot, j):
            return [
                pltpu.make_async_copy(i.full[which].at[pl.ds(j * groups, groups)], held.at[slot, which], t.tile_sem.at[slot, which])
                for which in range(3)
            ]

        def body(j, slot):
            t.back[:, at(j, TILE)] = sum(
                times_trans(t.grad_qkv[which][...], held[slot, which].reshape(TILE, s.width)) for which in range(3)
            )

        streamed(0, s.width // TILE, weight_copies, body)

    def table_back(self, grad_scores):
        i, t, s = self.i, self.t, self.sizes
        width = BUCKETS * HEADS

        def count(total):
            total[...] = jnp.zeros_like(total)

            def body(j):
                block = at(j, 16)
                scores = grad_scores[:, block, :].reshape(HEADS * 16, s.rows)
                total[...] += times_trans(bucket_rows(i.buckets[block, :]), scores)

            loop(0, s.rows // 16, body)
            found = total[...].T
            row = lax.broadcasted_iota(I32, found.shape, 0)
            lane = lax.broadcasted_iota(I32, found.shape, 1)
            found = jnp.where(row % 16 == lane % 16, found, 0.0)
            by_head = jnp.sum(found.reshape(HEADS, 16, width), axis=1)
            summed = jnp.dot(
                by_head, same_bucket(width), precision=lax.Precision.HIGHEST, preferred_element_type=F32
            )
            head = lax.broadcasted_iota(I32, summed.shape, 0)
            lane = lax.broadcasted_iota(I32, summed.shape, 1)
            t.totals[3:4, :width] = jnp.sum(
                jnp.where(lane % HEADS == head, summed, 0.0), axis=0, keepdims=True
            )

        pl.run_scoped(count, pltpu.VMEM((width, HEADS * 16), F32))


def pack_small(vectors, device):
    rows = []
    for vector in vectors:
        size = vector.shape[0]
        mine = jnp.arange(LANES) // size == lax.rem(device, LANES // size)
        rows.append(jnp.where(mine, jnp.tile(vector, LANES // size), jnp.zeros((), vector.dtype)))
    rows += [jnp.zeros((LANES,), vectors[0].dtype)] * (16 - len(rows))
    return jnp.stack(rows)


def per_device(
    plan,
    tokens,
    patch_keep,
    text_len,
    buckets,
    mask_embed,
    norm_attn,
    w_query,
    w_key,
    w_value,
    w_out,
    bias_table,
    norm_ffn,
    w_gate,
    w_up,
    w_down,
    cotangent,
):
    rows, width = tokens.shape
    page_count, patches = patch_keep.shape
    assert page_count == 1
    device = lax.axis_index("wide") * plan.narrow + lax.axis_index("narrow")
    keep = jnp.concatenate([patch_keep, jnp.ones((1, rows - patches), I32)], axis=1)
    live = (jnp.arange(rows, dtype=I32)[None, :] < (patches + text_len)[:, None]).astype(I32)
    small = pack_small((mask_embed, norm_attn, norm_ffn, bias_table), device)
    weights = (w_query, w_key, w_value, w_out, w_gate, w_up, w_down)
    shards = [jnp.pad(weight, ((0, -weight.shape[0] % 16), (0, 0))) for weight in weights]
    sizes = Sizes(plan, rows, width, w_gate.shape[1], [weight.shape[0] for weight in weights])
    forward = Forward(plan, sizes).call(small, shards, tokens, keep, live, buckets, cotangent)
    back = Backward(plan, sizes).call(forward, tokens, keep, buckets, cotangent)

    def own(row, size):
        return lax.dynamic_slice(back.sums[row], (device * size,), (size,))

    query, key, value, out, gate, up, down = back.grads
    return (
        back.result,
        back.input_grad,
        own(0, mask_embed.shape[0]),
        own(1, norm_attn.shape[0]),
        query,
        key,
        value,
        out,
        own(3, bias_table.shape[0]),
        own(2, norm_ffn.shape[0]),
        gate,
        up,
        down,
    )


def solution(mesh):
    rows, flat = P(("wide", "narrow"), None), P(("wide", "narrow"))
    plan = Plan(mesh.shape["wide"], mesh.shape["narrow"])
    return jax.shard_map(
        functools.partial(per_device, plan),
        mesh=mesh,
        in_specs=(rows, rows, flat, rows, flat, flat, rows, rows, rows, rows, flat, flat, rows, rows, rows, rows),
        out_specs=(rows, rows, flat, flat, rows, rows, rows, rows, flat, flat, rows, rows, rows),
        check_vma=False,
    )
```

```python
import functools
import types

import jax
import jax.numpy as jnp
from jax import lax
from jax.experimental import pallas as pl
from jax.experimental.pallas import tpu as pltpu
from jax.sharding import PartitionSpec as P

MESH = pl.DeviceIdType.MESH
VMEM_LIMIT = 62 << 20
HEADS = 16
HEAD = 64
BUCKETS = 32
EPSILON = 1e-06
NEG_FILL = -1000000000.0
LANES = 128
TILE = 256
CONTRACT_LAST = (((1,), (1,)), ((), ()))
CONTRACT_FIRST = (((0,), (0,)), ((), ()))
BF16, F32, I32 = jnp.bfloat16, jnp.float32, jnp.int32
GELU_SCALE = 0.7978845608028654
GELU_CUBE = 0.044715


def round_up(value, unit):
    return -(-value // unit) * unit


def matmul(left, right):
    return jnp.dot(left, right, preferred_element_type=F32)


def times_trans(left, right):
    return lax.dot_general(left, right, CONTRACT_LAST, preferred_element_type=F32)


def trans_times(left, right):
    return lax.dot_general(left, right, CONTRACT_FIRST, preferred_element_type=F32)


class Plan:
    def __init__(self, wide, narrow):
        self.wide, self.narrow = wide, narrow
        self.bits = [2 << i for i in range(wide.bit_length() - 2)]
        self.chunks = wide // 2
        assert wide == 2 << len(self.bits)


def span(bits):
    out = [0]
    for bit in bits:
        out = out + [member ^ bit for member in out]
    return out


def halves(start, size):
    half = round_up(size // 2, LANES)
    return [(start, half), (start + half, size - half)] if size > 2 * LANES else [(start, size)]


def enter(plan):
    w, n = lax.axis_index("wide"), lax.axis_index("narrow")
    barrier = pltpu.get_barrier_semaphore()
    partners = [(w ^ bit, n) for bit in [1] + plan.bits]
    partners += [(w, lax.rem(n + d, plan.narrow)) for d in range(1, plan.narrow)]
    for partner in partners:
        pl.semaphore_signal(barrier, inc=1, device_id=partner, device_id_type=MESH)
    pl.semaphore_wait(barrier, len(partners))
    return w, n


def loop(low, high, body):
    def step(i, carry):
        body(i)
        return carry

    lax.fori_loop(low, high, step, 0)


def at(index, size):
    return pl.ds(pl.multiple_of(index * size, size), size)


def streamed(low, high, copies, body):
    for copy in copies(lax.rem(low, 2), low):
        copy.start()

    def step(i):
        slot = lax.rem(i, 2)

        @pl.when(i + 1 < high)
        def _():
            for copy in copies(1 - slot, i + 1):
                copy.start()

        for copy in copies(slot, i):
            copy.wait()
        body(i, slot)

    loop(low, high, step)


def run(kernel, inputs, outputs, scratch, resident, scalars, collective_id, name):
    sizes = [len(jax.tree.leaves(tree)) for tree in (inputs, outputs, scratch)]
    forms = [jax.tree.structure(tree) for tree in (inputs, outputs, scratch)]

    def flat(*refs):
        first, second = sizes[0], sizes[0] + sizes[1]
        parts = (refs[:first], refs[first:second], refs[second:])
        kernel(*(types.SimpleNamespace(**form.unflatten(part)) for form, part in zip(forms, parts)))

    def space(key):
        return pltpu.VMEM if key in resident else pltpu.SMEM if key in scalars else pl.ANY

    def specs(tree):
        return jax.tree.leaves(
            {
                key: jax.tree.map(lambda _, key=key: pl.BlockSpec(memory_space=space(key)), value)
                for key, value in tree.items()
            }
        )

    result = pl.pallas_call(
        flat,
        out_shape=jax.tree.leaves(outputs),
        in_specs=specs(inputs),
        out_specs=specs(outputs),
        scratch_shapes=jax.tree.leaves(scratch),
        compiler_params=pltpu.CompilerParams(
            collective_id=collective_id, has_side_effects=True, vmem_limit_bytes=VMEM_LIMIT
        ),
        name=name,
    )(*jax.tree.leaves(inputs))
    return types.SimpleNamespace(**forms[1].unflatten(result))


def sems(*shape):
    return pltpu.SemaphoreType.DMA(shape)


def struct(shape, dtype):
    return jax.ShapeDtypeStruct(shape, dtype)


class Gather:
    def __init__(self, plan, rows, window):
        self.plan, self.rows = plan, rows
        self.start_column, self.columns = window
        self.padded = round_up(self.rows, 16)
        self.aligned = self.padded == self.rows
        self.group = plan.narrow * self.rows
        self.parts = halves(*window)
        self.orders = [plan.bits, plan.bits[::-1]][: len(self.parts)]
        self.chunks = plan.chunks

    def reserve(self):
        count, parts = self.plan.narrow, len(self.parts)
        return [sems(2, count), sems(2, parts, self.chunks), sems(2, parts, self.chunks), sems(2)]

    def stages_out(self):
        return [] if self.aligned else [struct((self.plan.narrow, self.padded, self.columns), BF16)]

    def bind(self, place, shard, out, stage, refs):
        self.w, self.n = place
        self.shard, self.out = shard, out
        self.zsem, self.bsem, self.csem, self.lsem = refs
        if not self.aligned:
            self.stage = stage[0]

    def window(self):
        return pl.ds(self.start_column, self.columns)

    def own_slot(self):
        if self.aligned:
            rows = pl.ds(pl.multiple_of(self.n * self.rows, self.rows), self.rows)
            return self.out.at[self.w, rows, self.window()]
        return self.stage.at[self.n]

    def z_copy(self, d):
        return pltpu.make_async_remote_copy(
            src_ref=self.shard.at[:, self.window()],
            dst_ref=self.own_slot(),
            send_sem=self.zsem.at[0, d],
            recv_sem=self.zsem.at[1, d],
            device_id=(self.w, lax.rem(self.n + d, self.plan.narrow)),
            device_id_type=MESH,
        )

    def place_copy(self):
        return pltpu.make_async_copy(self.shard.at[:, self.window()], self.own_slot(), self.lsem.at[0])

    def pack_group(self, stage, compact):
        copy = pltpu.make_async_copy(self.stage, stage, self.lsem.at[1])
        copy.start()
        copy.wait()
        size, wide = self.group, self.plan.narrow * self.padded
        row = lax.broadcasted_iota(I32, (size, wide), 0)
        column = lax.broadcasted_iota(I32, (size, wide), 1)
        pick = column == (row // self.rows) * self.padded + row % self.rows
        compact[...] = matmul(pick.astype(F32).astype(BF16), stage[...].reshape(wide, self.columns)).astype(BF16)
        copy = pltpu.make_async_copy(compact, self.out.at[self.w, :, self.window()], self.lsem.at[1])
        copy.start()
        copy.wait()

    def start(self):
        for d in range(1, self.plan.narrow):
            self.z_copy(d).start()
        self.place_copy().start()

    def hop(self, sems, part, mask, bit, slot):
        start, size = self.parts[part]
        target = self.out.at[self.w ^ mask, :, pl.ds(start, size)]
        return pltpu.make_async_remote_copy(
            src_ref=target,
            dst_ref=target,
            send_sem=sems.at[0, part, slot],
            recv_sem=sems.at[1, part, slot],
            device_id=(self.w ^ bit, self.n),
            device_id_type=MESH,
        )

    def hops(self, part, stage):
        order = self.orders[part]
        masks = span(order[:stage])
        return [self.hop(self.bsem, part, mask, order[stage], len(masks) + i - 1) for i, mask in enumerate(masks)]

    def core_hops(self, part, stage):
        masks = span(self.orders[part])
        low, high = (0, 1) if stage == 0 else (1 << (stage - 1), 1 << stage)
        return [self.hop(self.csem, part, masks[i], 1, i) for i in range(low, high)]

    def stages(self):
        return len(self.plan.bits) + 2

    def step(self, stage):
        bits, parts = len(self.plan.bits), range(len(self.parts))
        if stage == 0:
            for d in range(1, self.plan.narrow):
                self.z_copy(d).wait_recv()
            self.place_copy().wait()
            if not self.aligned:
                pl.run_scoped(
                    self.pack_group,
                    pltpu.VMEM((self.plan.narrow, self.padded, self.columns), BF16),
                    pltpu.VMEM((self.group, self.columns), BF16),
                )
        elif stage <= bits:
            for part in parts:
                for copy in self.hops(part, stage - 1):
                    copy.wait_recv()
        else:
            for part in parts:
                for s in range(bits + 1):
                    for copy in self.core_hops(part, s):
                        copy.wait_recv()
        if stage < bits:
            for part in parts:
                for copy in self.hops(part, stage):
                    copy.start()
        if stage <= bits:
            for part in parts:
                for copy in self.core_hops(part, stage):
                    copy.start()

    def finish(self):
        for d in range(1, self.plan.narrow):
            self.z_copy(d).wait_send()
        for part in range(len(self.parts)):
            for s in range(len(self.plan.bits)):
                for copy in self.hops(part, s):
                    copy.wait_send()
            for s in range(len(self.plan.bits) + 1):
                for copy in self.core_hops(part, s):
                    copy.wait_send()


class Swap:
    def __init__(self, plan):
        self.plan = plan

    def reserve(self):
        return sems(3, self.plan.chunks)

    def bind(self, place, source, out, sem):
        self.w, self.n = place
        self.source, self.out, self.sem = source, out, sem
        self.both = len(out.shape) == 4
        self.group = source.shape[0] // self.plan.wide

    def chunk(self, index):
        return self.source.at[pl.ds(pl.multiple_of(index * self.group, self.group), self.group), :]

    def local(self, slot):
        return pltpu.make_async_copy(self.chunk(self.w ^ (2 * slot)), self.out.at[0, slot], self.sem.at[2, slot])

    def landing(self, slot):
        return self.out.at[1, slot] if self.both else self.out.at[slot]

    def remote(self, slot, source):
        return pltpu.make_async_remote_copy(
            src_ref=source,
            dst_ref=self.landing(slot),
            send_sem=self.sem.at[0, slot],
            recv_sem=self.sem.at[1, slot],
            device_id=(self.w ^ 1, self.n),
            device_id_type=MESH,
        )

    def send(self, slot):
        return self.remote(slot, self.chunk(self.w ^ 1 ^ (2 * slot)))

    def start(self):
        for slot in range(self.plan.chunks):
            self.send(slot).start()
            if self.both:
                self.local(slot).start()

    def wait_recv(self):
        for slot in range(self.plan.chunks):
            self.remote(slot, self.landing(slot)).wait_recv()

    def finish(self):
        for slot in range(self.plan.chunks):
            self.send(slot).wait_send()
            if self.both:
                self.local(slot).wait()


def to_sibling(place, source, target, sem):
    return pltpu.make_async_remote_copy(
        src_ref=source,
        dst_ref=target,
        send_sem=sem.at[0],
        recv_sem=sem.at[1],
        device_id=(place[0] ^ 1, place[1]),
        device_id_type=MESH,
    )


def column_of(row):
    eye = lax.broadcasted_iota(I32, (LANES, LANES), 0) == lax.broadcasted_iota(I32, (LANES, LANES), 1)
    pieces = [
        jnp.sum(jnp.where(eye, row[:, start : start + LANES], 0.0), axis=1, keepdims=True)
        for start in range(0, row.shape[1], LANES)
    ]
    return jnp.concatenate(pieces, axis=0)


def unpack_small(plan, packed, sizes):
    summed = jnp.sum(packed.astype(F32).reshape(plan.wide, plan.narrow, 16, LANES), axis=1)
    rows = []
    for i, size in enumerate(sizes):
        each = LANES // (size * plan.narrow)
        blocks = [
            sum(summed[first + j, i : i + 1, :] for j in range(each))
            for first in range(0, plan.wide, each)
        ]
        rows.append(jnp.concatenate(blocks, axis=1))
    return rows


def same_bucket(width):
    row = lax.broadcasted_iota(I32, (width, width), 0) // HEADS
    column = lax.broadcasted_iota(I32, (width, width), 1) // HEADS
    return (row == column).astype(F32)


def spread_table(table_row):
    width = BUCKETS * HEADS
    lane = lax.broadcasted_iota(I32, (HEADS, width), 1)
    head = lax.broadcasted_iota(I32, (HEADS, width), 0)
    same = lane % HEADS == head
    picked = jnp.where(same, table_row, 0.0).astype(BF16)
    spread = matmul(picked, same_bucket(width).astype(BF16))
    return jnp.concatenate(
        [jnp.where(same, spread[h : h + 1, :], 0.0).astype(BF16) for h in range(HEADS)], axis=0
    )


def bucket_rows(bucket):
    small = bucket.astype(F32).astype(BF16)
    one, zero = jnp.ones_like(small), jnp.zeros_like(small)
    return jnp.concatenate(
        [jnp.where(small == jnp.asarray(j, BF16), one, zero) for j in range(BUCKETS)], axis=0
    )


class Reduce:
    def __init__(self, plan, rows, window, order):
        self.plan, self.rows = plan, rows
        self.start_column, self.columns = window
        self.padded = round_up(rows, 16)
        self.aligned = self.padded == rows
        self.group = plan.narrow * rows
        self.order = order
        self.chunks = plan.chunks

    def reserve(self):
        count, columns = self.plan.narrow, self.columns
        shapes = [
            sems(2, self.chunks),
            sems(2, count),
            pltpu.VMEM((self.chunks, self.group, columns), BF16),
            pltpu.VMEM((self.chunks - 1, self.group, columns), BF16),
            pltpu.VMEM((count - 1, self.padded, columns), BF16),
        ]
        if not self.aligned:
            shapes.append(pltpu.VMEM((count, self.padded, columns), BF16))
        return shapes

    def bind(self, place, out, refs):
        self.w, self.n = place
        self.out, self.done = out, 0
        self.bsem, self.zsem, self.acc, self.received, self.zreceived = refs[:5]
        if not self.aligned:
            self.stage = refs[5]

    def hops(self, stage):
        bit, masks = self.order[stage], span(self.order[stage + 1 :])
        base = self.chunks - 2 * len(masks)
        return [
            (
                mask >> 1,
                base + k,
                pltpu.make_async_remote_copy(
                    src_ref=self.acc.at[(bit ^ mask) >> 1],
                    dst_ref=self.received.at[base + k],
                    send_sem=self.bsem.at[0, base + k],
                    recv_sem=self.bsem.at[1, base + k],
                    device_id=(self.w ^ bit, self.n),
                    device_id_type=MESH,
                ),
            )
            for k, mask in enumerate(masks)
        ]

    def z_copy(self, d):
        peer = lax.rem(self.n + d, self.plan.narrow)
        source = self.acc.at[0, at(peer, self.rows), :] if self.aligned else self.stage.at[peer]
        return pltpu.make_async_remote_copy(
            src_ref=source,
            dst_ref=self.zreceived.at[d - 1],
            send_sem=self.zsem.at[0, d],
            recv_sem=self.zsem.at[1, d],
            device_id=(self.w, peer),
            device_id_type=MESH,
        )

    def step(self, stage):
        bits = len(self.order)
        if 1 <= stage <= bits:
            for slot, k, copy in self.hops(stage - 1):
                copy.wait_recv()

                def body(j, slot=slot, k=k):
                    block = at(j, 16)
                    self.acc[slot, block, :] += self.received[k, block, :]

                loop(0, self.group // 16, body)
        if stage < bits:
            for _, _, copy in self.hops(stage):
                copy.start()
        elif stage == bits:
            if not self.aligned:
                size, wide = self.group, self.plan.narrow * self.padded
                row = lax.broadcasted_iota(I32, (wide, size), 0)
                column = lax.broadcasted_iota(I32, (wide, size), 1)
                pick = row == (column // self.rows) * self.padded + column % self.rows
                self.stage[...] = (
                    matmul(pick.astype(F32).astype(BF16), self.acc[0]).astype(BF16).reshape(self.stage.shape)
                )
            for d in range(1, self.plan.narrow):
                self.z_copy(d).start()
        else:
            total = self.acc[0, at(self.n, self.rows), :] if self.aligned else self.stage[self.n]
            total = total.astype(F32)
            for d in range(1, self.plan.narrow):
                self.z_copy(d).wait_recv()
                total = total + self.zreceived[d - 1].astype(F32)
            self.out[:, pl.ds(self.start_column, self.columns)] = total[: self.rows]

    def finish(self):
        for stage in range(len(self.order)):
            for _, _, copy in self.hops(stage):
                copy.wait_send()
        for d in range(1, self.plan.narrow):
            self.z_copy(d).wait_send()


class SumAll:
    def __init__(self, plan, shape):
        self.shape = shape
        self.rounds = [(bit, 0) for bit in [1] + plan.bits]
        self.rounds += [(0, 1 << k) for k in range(plan.narrow.bit_length() - 1)]

    def reserve(self):
        count = len(self.rounds)
        return [sems(2, count)] + [pltpu.VMEM((count, *self.shape), F32)] * 2

    def bind(self, place, out, refs):
        self.w, self.n = place
        self.out = out
        self.sem, self.held, self.received = refs

    def copy(self, turn):
        bit, other = self.rounds[turn]
        return pltpu.make_async_remote_copy(
            src_ref=self.held.at[turn],
            dst_ref=self.received.at[turn],
            send_sem=self.sem.at[0, turn],
            recv_sem=self.sem.at[1, turn],
            device_id=(self.w ^ bit, self.n ^ other),
            device_id_type=MESH,
        )

    def start(self, value):
        self.held[0] = value
        self.copy(0).start()

    def step(self, turn):
        self.copy(turn).wait_recv()
        total = self.held[turn] + self.received[turn]
        if turn + 1 < len(self.rounds):
            self.held[turn + 1] = total
            self.copy(turn + 1).start()
        else:
            self.out[...] = total

    def finish(self):
        for turn in range(len(self.rounds)):
            self.copy(turn).wait_send()


class Sizes:
    def __init__(self, plan, rows, width, ff, shards):
        self.plan, self.rows, self.width, self.ff = plan, rows, width, ff
        self.shards = shards
        self.group = plan.narrow * shards[0]
        self.down_group = plan.narrow * shards[DOWN]
        step = round_up(ff // 3, BLOCK)
        self.ff_windows = [(start, min(step, ff - start)) for start in range(0, ff, step)]
        self.half_windows = [(0, width // 2), (width // 2, width // 2)]
        self.blocks = round_up(ff, BLOCK) // BLOCK

    def full(self):
        wide = self.plan.wide
        return (
            [(wide, self.group, self.width)] * 4
            + [(wide, self.group, self.ff)] * 2
            + [(wide, self.down_group, self.width)]
        )


QUERY, KEY, VALUE, OUT, GATE, UP, DOWN = range(7)
BLOCK = 512


class Layer:
    def __init__(self, plan, sizes):
        self.plan, self.sizes = plan, sizes
        whole = (0, sizes.width)
        wide = [(weight, window) for window in sizes.ff_windows for weight in (GATE, UP)]
        down = [(DOWN, window) for window in sizes.half_windows]
        self.order = [(weight, whole) for weight in (QUERY, KEY, VALUE, OUT)] + down + wide
        self.small = Gather(plan, 16, (0, LANES))
        self.items = [self.small] + [Gather(plan, sizes.shards[weight], window) for weight, window in self.order]
        self.swaps = [Swap(plan) for _ in range(4)]
        self.extra = self.small.stages() - 4
        ways = [plan.bits, plan.bits[::-1]]
        self.reduces = []
        for weight in range(7):
            turn = 1 if weight in (UP, KEY, OUT) else 0
            pairs = enumerate(sizes.half_windows)
            if weight in (GATE, UP):
                pairs = [(0, window) for window in sizes.ff_windows]
            self.reduces.append([Reduce(plan, sizes.shards[weight], window, ways[k ^ turn]) for k, window in pairs])
        self.sums = SumAll(plan, (8, sizes.width))

    def call(self, vectors, counts, shards, tokens, patch_keep, text_len, buckets, cotangent):
        plan, s = self.plan, self.sizes
        self.counts = counts
        rows, width, chunks = s.rows, s.width, plan.chunks
        row_block = struct((rows, width), BF16)
        inputs = dict(
            vectors=vectors,
            shards=shards[:DOWN],
            down_shard=shards[DOWN],
            tokens=tokens,
            patch_keep=patch_keep,
            text_len=text_len,
            buckets=buckets,
            cotangent=cotangent,
        )
        outputs = dict(
            small=struct((plan.wide, plan.narrow * 16, LANES), BF16),
            full=[struct(shape, BF16) for shape in s.full()],
            stages=[item.stages_out() for item in self.items],
            qkv=[row_block] * 3,
            prob=struct((HEADS, rows, rows), BF16),
            turned=[struct((2, chunks, s.group, rows), BF16)] * 3,
            hidden_far=struct((chunks, s.down_group, rows), BF16),
            cot_far=row_block,
            far_ff=struct((2, s.blocks, rows, BLOCK), BF16),
            far_out=row_block,
            far_attn=[row_block] * 3,
            result=row_block,
            input_grad=struct((rows, width), F32),
            grads=[
                struct((size, s.ff if weight in (GATE, UP) else width), F32) for weight, size in enumerate(s.shards)
            ],
            sums=struct((8, width), F32),
        )
        square = pltpu.VMEM((rows, width), BF16)
        down_rows = round_up(s.shards[DOWN], 16)
        scratch = dict(
            items=[item.reserve() for item in self.items],
            swaps=[swap.reserve() for swap in self.swaps],
            reduces=[[item.reserve() for item in pair] for pair in self.reduces],
            exchange=self.sums.reserve(),
            direct=sems(2),
            load=sems(len(self.items)),
            pre=sems(8),
            packed=pltpu.VMEM((16, LANES), BF16),
            small=pltpu.VMEM((plan.wide, plan.narrow * 16, LANES), BF16),
            down_shard=pltpu.VMEM((down_rows, width), BF16),
            rows=pltpu.VMEM((8, width), F32),
            keep=pltpu.VMEM((rows, 1), F32),
            big=pltpu.VMEM((HEADS, rows, rows), BF16),
            stream=pltpu.VMEM((rows, width), F32),
            normed=square,
            totals=pltpu.VMEM((8, width), F32),
            pair_sem=sems(2),
            tile_sem=sems(2, 3),
            ff_sem=sems(len(s.ff_windows), 2, 2, 2),
            out_sem=sems(2),
            attn_sem=sems(2, 3, 2),
            store=sems(6),
        )
        return run(
            self.kernel,
            inputs,
            outputs,
            scratch,
            {"vectors", "down_shard", "patch_keep", "cotangent", "grads", "sums"},
            {"text_len"},
            0,
            "layer",
        )

    def kernel(self, i, o, t):
        self.i, self.o, self.t = i, o, t
        plan, s = self.plan, self.sizes
        square = pltpu.VMEM((s.rows, s.width), BF16)
        planes = pltpu.VMEM((2, plan.chunks, s.group, s.rows), BF16)
        weight_space = pltpu.VMEM((plan.wide, s.group, s.width), BF16)
        self.pack()
        self.place = place = enter(plan)
        self.small.bind(place, t.packed, o.small, o.stages[0], t.items[0])
        for item, (weight, _), stage, refs in zip(self.items[1:], self.order, o.stages[1:], t.items[1:]):
            item.bind(place, t.down_shard if weight == DOWN else i.shards[weight], o.full[weight], stage, refs)
        for pair, out, refs in zip(self.reduces, o.grads, t.reduces):
            for item, own in zip(pair, refs):
                item.bind(place, out, own)
        self.sums.bind(place, o.sums, t.exchange)
        self.direct = to_sibling(place, i.cotangent, o.cot_far, t.direct)

        for item in self.items[:3]:
            item.start()
        self.direct.start()
        for turn in range(-self.extra, 4):
            self.tick(turn)
        self.set_up()
        pl.run_scoped(
            self.attention_phase,
            [weight_space] * 3,
            [square] * 4,
            [pltpu.VMEM((s.width, s.rows), BF16)] * 2,
            pltpu.VMEM((2, 2, s.rows, s.rows), BF16),
            pltpu.VMEM((HEADS * 16, BUCKETS * 16), BF16),
            pltpu.VMEM((s.rows, s.rows), I32),
        )
        pl.run_scoped(
            self.feed_phase,
            [pltpu.VMEM((plan.wide, s.group, s.ff_windows[0][1]), BF16)] * 2,
            pltpu.VMEM((s.ff, s.width), BF16),
            pltpu.VMEM((s.ff, s.rows), BF16),
            pltpu.VMEM((plan.chunks, s.down_group, s.rows), BF16),
            square,
            planes,
            pltpu.VMEM((2, 2, s.rows, TILE), BF16),
            sems(plan.wide),
        )
        pl.run_scoped(
            self.back_phase,
            planes,
            [square] * 3,
            pltpu.VMEM((s.rows, s.width), F32),
            square,
        )


    def tick(self, turn):
        stages, turn = self.small.stages(), turn + self.extra
        for stage in range(stages):
            k = turn - stage
            if 0 <= k < len(self.items):
                self.items[k].step(stage)
        if turn + 3 < len(self.items):
            self.items[turn + 3].start()

    def load(self, weight, window, target):
        k = 1 + self.order.index((weight, window))
        return pltpu.make_async_copy(self.o.full[weight].at[:, :, pl.ds(*window)], target, self.t.load.at[k])

    def pack(self):
        i, t = self.i, self.t
        device = lax.axis_index("wide") * self.plan.narrow + lax.axis_index("narrow")
        source = lax.broadcasted_iota(I32, (LANES, LANES), 0)
        lane = lax.broadcasted_iota(I32, (LANES, LANES), 1)
        row = lax.broadcasted_iota(I32, (16, LANES), 0)
        packed, offset = jnp.zeros((16, LANES), F32), 0
        for k, size in enumerate(self.counts):
            first = lax.rem(device * size, LANES)
            pick = (source == offset + lane - first) & (lane >= first) & (lane < first + size)
            found = matmul(i.vectors[...], pick.astype(F32).astype(BF16))
            packed = jnp.where(row == k, found, packed)
            offset += size
        t.packed[...] = packed.astype(BF16)
        size = i.down_shard.shape[0]
        t.down_shard[...] = jnp.concatenate(
            [i.down_shard[...], jnp.zeros((t.down_shard.shape[0] - size, self.sizes.width), BF16)], axis=0
        )

    def set_up(self):
        i, o, t = self.i, self.o, self.t
        copy = pltpu.make_async_copy(o.small, t.small, t.load.at[0])
        copy.start()
        tokens = pltpu.make_async_copy(i.tokens, t.normed, t.pre.at[7])
        tokens.start()
        patches, rows = i.patch_keep.shape[1], self.sizes.rows
        row = lax.broadcasted_iota(I32, (rows, patches), 0)
        lane = lax.broadcasted_iota(I32, (rows, patches), 1)
        kept = jnp.sum(jnp.where(row == lane, i.patch_keep[...].astype(F32), 0.0), axis=1, keepdims=True)
        t.keep[...] = jnp.where(lax.broadcasted_iota(I32, (rows, 1), 0) >= patches, 1.0, kept)
        t.totals[...] = jnp.zeros_like(t.totals)
        copy.wait()
        embed, gain_one, gain_two, table = unpack_small(self.plan, t.small[...], self.counts)
        t.rows[...] = jnp.concatenate([embed, gain_one, gain_two, jnp.zeros((5, self.sizes.width), F32)], axis=0)
        self.table_row = table
        tokens.wait()

        def body(j):
            block = at(j, 64)
            t.stream[block, :] = jnp.where(
                t.keep[block, :] > 0.5, t.normed[block, :].astype(F32), t.rows[0:1, :]
            )

        loop(0, rows // 64, body)
        self.norm(1)

    def norm(self, gain):
        t = self.t

        def body(j):
            block = at(j, 64)
            x = t.stream[block, :]
            scale = lax.rsqrt(jnp.mean(x * x, axis=-1, keepdims=True) + EPSILON)
            t.normed[block, :] = (x * scale * t.rows[gain : gain + 1, :]).astype(BF16)

        loop(0, self.sizes.rows // 64, body)

    def turn(self, source, target):
        def body(j):
            target[at(j, LANES), :] = source[:, at(j, LANES)].T

        loop(0, self.sizes.width // LANES, body)


    def attention_phase(self, held, qkva, turned, prob, table, buckets):
        o, t, s = self.o, self.t, self.sizes
        bucket_copy = pltpu.make_async_copy(self.i.buckets, buckets, t.pre.at[7])
        bucket_copy.start()
        normed, attended, second, _ = self.swaps
        for swap, source, target, sem in zip(
            self.swaps, (turned[0], turned[1], turned[0]), o.turned, t.swaps
        ):
            swap.bind(self.place, source, target, sem)
        store = [pltpu.make_async_copy(qkva[k], o.qkv[k], t.store.at[k]) for k in range(3)]
        whole = (0, s.width)
        loads = [self.load(weight, whole, held[weight % 3]) for weight in (QUERY, KEY, VALUE, OUT)]
        self.turn(t.normed, turned[0])
        normed.start()
        table[...] = spread_table(self.table_row)
        self.tick(4)
        loads[QUERY].start()
        blocks = s.rows // 16
        bucket_copy.wait()
        self.bias(0, blocks // 2, table, buckets)
        self.tick(5)
        loads[KEY].start()
        loads[QUERY].wait()
        self.project(held[0], qkva[0])
        store[0].start()
        self.bias(blocks // 2, blocks, table, buckets)
        self.tick(6)
        loads[VALUE].start()
        loads[KEY].wait()
        self.project(held[1], qkva[1])
        store[1].start()
        self.tick(7)
        loads[OUT].start()
        loads[VALUE].wait()
        self.project(held[2], qkva[2])
        store[2].start()
        count = HEADS // 2
        self.attend(0, count // 4, qkva, prob)
        self.tick(8)
        self.attend(count // 4, 5 * count // 8, qkva, prob)
        self.tick(9)
        self.attend(5 * count // 8, count, qkva, prob)
        for slot in range(2):
            self.prob_copy(slot, count - 2 + slot, prob).wait()
        loads[OUT].wait()

        def body(j):
            block = held[0][:, :, at(j, TILE)].reshape(s.width, TILE)
            t.stream[:, at(j, TILE)] += matmul(qkva[3][...], block)

        loop(0, s.width // TILE, body)
        self.turn(qkva[3], turned[1])
        attended.start()
        normed.finish()
        self.norm(2)
        self.turn(t.normed, turned[0])
        second.start()
        for copy in store:
            copy.wait()
        attended.finish()
        second.finish()

    def bias(self, low, high, table, buckets):
        i, t = self.i, self.t
        live = lax.broadcasted_iota(I32, (1, self.sizes.rows), 1) < i.patch_keep.shape[1] + i.text_len[0]

        def body(j):
            block = at(j, 16)
            spread = matmul(table[...], bucket_rows(buckets[block, :]))
            spread = jnp.where(live, spread, NEG_FILL).astype(BF16)
            t.big[:, block, :] = spread.reshape(HEADS, 16, spread.shape[-1])

        loop(low, high, body)

    def project(self, weight, target):
        def body(j):
            block = weight[:, :, at(j, TILE)].reshape(self.sizes.width, TILE)
            target[:, at(j, TILE)] = matmul(self.t.normed[...], block).astype(BF16)

        loop(0, self.sizes.width // TILE, body)

    def prob_copy(self, slot, pair, prob):
        return pltpu.make_async_copy(prob.at[slot], self.o.prob.at[pl.ds(2 * pair, 2)], self.t.pair_sem.at[slot])

    def attend(self, low, high, qkva, prob):
        t = self.t
        lane = lax.broadcasted_iota(I32, (1, LANES), 1)

        def body(pair):
            columns, slot = at(pair, LANES), lax.rem(pair, 2)

            @pl.when(pair >= 2)
            def _():
                self.prob_copy(slot, pair, prob).wait()

            q, k, v = (ref[:, columns] for ref in qkva[:3])
            mixed = []
            for e in range(2):
                own = jnp.where((lane < HEAD) == (e == 0), q, jnp.zeros_like(q))
                scores = times_trans(own, k) + t.big[2 * pair + e].astype(F32)
                top = jnp.max(scores, axis=-1, keepdims=True)
                powers = jnp.exp(scores - top)
                total = jnp.sum(powers, axis=-1, keepdims=True)
                weights = (powers * (1.0 / total)).astype(BF16)
                prob[slot, e] = weights
                mixed.append(matmul(weights, v))
            qkva[3][:, columns] = jnp.where(lane < HEAD, mixed[0], mixed[1]).astype(BF16)
            self.prob_copy(slot, pair, prob).start()

        loop(low, high, body)


    def feed_phase(self, held, down, hidden, hidden_far, cot_far, planes, far, sem):
        i, o, t, s = self.i, self.o, self.t, self.sizes
        group, windows = s.down_group, s.ff_windows
        copies = [
            pltpu.make_async_copy(o.full[DOWN].at[k], down.at[pl.ds(k * group, group), :], sem.at[k])
            for k in range(self.plan.wide)
        ]
        for copy in copies:
            copy.start()
        swap = self.swaps[3]
        swap.bind(self.place, hidden, o.hidden_far, t.swaps[3])
        planes_copy = pltpu.make_async_copy(o.turned[2], planes, t.pre.at[0])
        self.tick(10)
        for part, window in enumerate(windows):
            loads = [
                self.load(weight, window, held[k].at[:, :, pl.ds(0, window[1])]) for k, weight in enumerate((GATE, UP))
            ]
            loads[0].start()
            self.tick(11 + 2 * part)
            loads[1].start()
            if part == 0:
                for copy in copies:
                    copy.wait()
            if part > 0:
                self.feed_weights(part - 1, planes, far)
            for copy in loads:
                copy.wait()
            self.feed(part, held, down, hidden)
            for copy in self.ff_copies(part):
                copy.start()
            if part == 0:
                self.swaps[2].wait_recv()
                planes_copy.start()
                planes_copy.wait()
            self.tick(12 + 2 * part)
        swap.start()
        for item in self.items:
            item.finish()
        self.direct.wait()
        cot_copy = pltpu.make_async_copy(o.cot_far, cot_far, t.pre.at[1])
        cot_copy.start()
        self.feed_weights(len(windows) - 1, planes, far)
        swap.wait_recv()
        far_copy = pltpu.make_async_copy(o.hidden_far, hidden_far, t.pre.at[2])
        far_copy.start()
        cot_copy.wait()
        far_copy.wait()
        self.down_gradient(hidden, hidden_far, cot_far)
        self.advance(DOWN)
        self.advance(GATE, (0,))
        self.advance(UP, (0,))
        store = pltpu.make_async_copy(cot_far, o.result, t.pre.at[1])

        def finish(j):
            block = at(j, TILE)
            cot_far[:, block] = (t.stream[:, block] + trans_times(hidden[...], down[:, block])).astype(BF16)

        loop(0, s.width // TILE, finish)
        store.start()
        store.wait()
        swap.finish()

    def near(self, which, j):
        return which * self.sizes.blocks + lax.div(j, 2), at(lax.rem(j, 2), TILE)

    def ff_copies(self, part):
        s, t = self.sizes, self.t
        start, size = s.ff_windows[part]
        copies = []
        for which in range(2):
            for k, first in enumerate(range(start, start + size, BLOCK)):
                block, columns = first // BLOCK, pl.ds(0, min(BLOCK, start + size - first))
                copies.append(
                    to_sibling(
                        self.place,
                        t.big.at[which * s.blocks + block, :, columns],
                        self.o.far_ff.at[which, block, :, columns],
                        t.ff_sem.at[part, which, k],
                    )
                )
        return copies

    def feed(self, part, held, down, hidden):
        i, t, s = self.i, self.t, self.sizes
        start, size = s.ff_windows[part]
        first = start // TILE

        def body(j):
            tile, columns = first + j, at(j, TILE)
            gate = matmul(t.normed[...], held[0][:, :, columns].reshape(s.width, TILE))
            up = matmul(t.normed[...], held[1][:, :, columns].reshape(s.width, TILE))
            grad = times_trans(i.cotangent[...], down[at(tile, TILE), :])
            square = gate * gate
            bend = jnp.tanh(GELU_SCALE * gate * (1.0 + GELU_CUBE * square))
            half = 0.5 * (1.0 + bend)
            act = gate * half
            slope = half + (0.5 * GELU_SCALE) * gate * (1.0 - bend * bend) * (1.0 + (3.0 * GELU_CUBE) * square)
            hidden[at(tile, TILE), :] = (act * up).astype(BF16).T
            for which, value in enumerate((grad * up * slope, grad * act)):
                block, lanes = self.near(which, tile)
                t.big[block, :, lanes] = value.astype(BF16)

        loop(0, size // TILE, body)

    def feed_weights(self, part, planes, far):
        o, t, s = self.o, self.t, self.sizes
        start, size = s.ff_windows[part]
        first, rows = start // TILE, self.plan.chunks * s.group
        for copy in self.ff_copies(part):
            copy.wait_recv()

        def far_copies(slot, j):
            return [
                pltpu.make_async_copy(
                    o.far_ff.at[which, lax.div(first + j, 2), :, self.near(which, first + j)[1]],
                    far.at[slot, which],
                    t.tile_sem.at[slot, which],
                )
                for which in range(2)
            ]

        def body(j, slot):
            left = jnp.concatenate([planes[0].reshape(rows, s.rows), planes[1].reshape(rows, s.rows)], axis=1)
            for which, weight in enumerate((GATE, UP)):
                block, lanes = self.near(which, first + j)
                right = jnp.concatenate([t.big[block, :, lanes], far[slot, which]], axis=0)
                acc = self.reduces[weight][part].acc
                acc[:, :, at(j, TILE)] = matmul(left, right).astype(BF16).reshape(self.plan.chunks, s.group, TILE)

        streamed(0, size // TILE, far_copies, body)
        self.advance(GATE, (part,))
        self.advance(UP, (part,))

    def down_gradient(self, hidden, hidden_far, cot_far):
        i, s = self.i, self.sizes
        for part, (start, size) in enumerate(s.half_windows):
            acc = self.reduces[DOWN][part].acc

            def body(slot, acc=acc, start=start, size=size):
                columns = pl.ds(start, size)
                near = hidden[at(self.place[0] ^ (2 * slot), s.down_group), :]
                left = jnp.concatenate([near, hidden_far[slot]], axis=1)
                right = jnp.concatenate([i.cotangent[:, columns], cot_far[:, columns]], axis=0)
                acc[slot] = matmul(left, right).astype(BF16)

            loop(0, self.plan.chunks, body)


    def advance(self, weight, parts=None):
        for part in range(len(self.reduces[weight])) if parts is None else parts:
            item = self.reduces[weight][part]
            item.step(item.done)
            item.done += 1

    def back_phase(self, planes, qkv, back, grad_attended):
        o, t, s = self.o, self.t, self.sizes
        square = pltpu.VMEM((s.rows, s.width), BF16)
        self.swaps[0].wait_recv()
        loads = [
            pltpu.make_async_copy(source, target, t.pre.at[k])
            for k, (source, target) in enumerate(zip([o.turned[0]] + o.qkv, [planes] + qkv))
        ]
        for copy in loads:
            copy.start()
        pl.run_scoped(
            functools.partial(self.middle, back, grad_attended),
            pltpu.VMEM((self.plan.wide, s.group, s.width), BF16),
            pltpu.VMEM((2, self.plan.chunks, s.group, s.rows), BF16),
            square,
        )
        for copy in loads:
            copy.wait()
        pl.run_scoped(
            functools.partial(self.attention_back, planes, qkv, back, grad_attended),
            [square] * 3,
            pltpu.VMEM((3, s.rows, s.width // 2), BF16),
        )

    def middle(self, back, grad_attended, weight, planes, grad_mid):
        o, t, s = self.o, self.t, self.sizes
        self.swaps[1].wait_recv()
        loads = [
            pltpu.make_async_copy(o.full[OUT], weight, t.pre.at[4]),
            pltpu.make_async_copy(o.turned[1], planes, t.pre.at[5]),
        ]
        for copy in loads:
            copy.start()
        groups = TILE // s.group
        pl.run_scoped(
            functools.partial(self.feed_input, back), pltpu.VMEM((2, 2, groups, s.group, s.ff), BF16)
        )
        for part in range(len(s.ff_windows)):
            for copy in self.ff_copies(part):
                copy.wait_send()
        self.norm_back(2, back, grad_mid)
        out_copy = to_sibling(self.place, grad_mid, o.far_out, t.out_sem)
        out_copy.start()
        self.advance(GATE, (1,))
        self.advance(UP, (1,))
        for copy in loads:
            copy.wait()
        pl.run_scoped(
            functools.partial(self.out_back, out_copy, weight, planes, grad_mid, grad_attended),
            pltpu.VMEM((s.rows, s.width), BF16),
        )
        self.advance(GATE, (0,))
        self.advance(UP, (0,))
        out_copy.wait_send()

    def attention_back(self, planes, qkv, back, grad_attended, grad_qkv, far):
        i, o, t, s, plan = self.i, self.o, self.t, self.sizes, self.plan
        self.grad_qkv = grad_qkv
        prob_space = pltpu.VMEM((2, 2, s.rows, s.rows), BF16)
        half = HEADS // 4
        tokens = pltpu.make_async_copy(i.tokens, t.normed, t.pre.at[7])
        tokens.start()
        pl.run_scoped(functools.partial(self.attend_back, 0, half, qkv, grad_attended), prob_space)
        self.send_attention(0)
        self.advance(GATE, (2,))
        self.advance(UP, (2,))
        self.advance(DOWN)
        self.attention_weights(0, planes, far)
        self.advance(GATE, (0, 1))
        self.advance(UP, (0, 1))
        pl.run_scoped(functools.partial(self.attend_back, half, 2 * half, qkv, grad_attended), prob_space)
        self.send_attention(1)
        self.advance(OUT)
        self.advance(GATE, (2,))
        self.advance(UP, (2,))
        self.advance(DOWN)
        self.attention_weights(1, planes, far)
        for weight in (QUERY, KEY, VALUE):
            self.advance(weight, (0,))
        groups = TILE // s.group
        pl.run_scoped(
            functools.partial(self.attention_input, back), pltpu.VMEM((2, 3, groups, s.group, s.width), BF16)
        )
        self.advance(OUT)
        for weight in (QUERY, KEY, VALUE):
            self.advance(weight, (1,))
        tokens.wait()
        self.norm_back(1, back, None)
        store = pltpu.make_async_copy(t.stream, o.input_grad, t.pre.at[0])
        store.start()
        for weight in (QUERY, KEY, VALUE):
            self.advance(weight, (0,))
        self.table_back()
        self.sums.start(t.totals[...])
        for weight in (QUERY, KEY, VALUE):
            self.advance(weight, (1,))
        turn, last = 0, len(plan.bits) + 1
        left = [(weight, part) for weight in (GATE, UP, DOWN, OUT) for part in range(len(self.reduces[weight]))]
        left += [(weight, part) for part in range(2) for weight in (QUERY, KEY, VALUE)]
        while left:
            for weight, part in list(left):
                if self.reduces[weight][part].done > last:
                    left.remove((weight, part))
                    continue
                self.advance(weight, (part,))
                if turn % 2 == 1 and turn // 2 < len(self.sums.rounds):
                    self.sums.step(turn // 2)
                turn += 1
        for k in range(turn // 2, len(self.sums.rounds)):
            self.sums.step(k)
        store.wait()
        for part in range(2):
            for copy in self.attention_copies(part):
                copy.wait_send()
        for pair in self.reduces:
            for item in pair:
                item.finish()
        self.sums.finish()

    def feed_input(self, back, held):
        o, t, s = self.o, self.t, self.sizes
        groups = TILE // s.group
        last = s.ff - BLOCK * (s.blocks - 1)

        def weight_copies(slot, j):
            return [
                pltpu.make_async_copy(
                    o.full[weight].at[pl.ds(j * groups, groups)], held.at[slot, which], t.tile_sem.at[slot, which]
                )
                for which, weight in enumerate((GATE, UP))
            ]

        def body(j, slot):
            total = None
            for which in range(2):
                first = which * s.blocks
                near = [t.big[first + k] for k in range(s.blocks - 1)]
                near.append(t.big[first + s.blocks - 1, :, pl.ds(0, last)])
                found = times_trans(jnp.concatenate(near, axis=1), held[slot, which].reshape(TILE, s.ff))
                total = found if total is None else total + found
            back[:, at(j, TILE)] = total

        streamed(0, s.width // TILE, weight_copies, body)

    def norm_back(self, which, back, grad_mid):
        i, t, s = self.i, self.t, self.sizes

        def body(j):
            block = at(j, 64)
            kept = t.keep[block, :] > 0.5
            grad = back[block, :]
            if which == 2:
                x = t.stream[block, :]
                before = i.cotangent[block, :].astype(F32)
            else:
                x = jnp.where(kept, t.normed[block, :].astype(F32), t.rows[0:1, :])
                before = t.stream[block, :]
            scale = lax.rsqrt(jnp.mean(x * x, axis=-1, keepdims=True) + EPSILON)
            scaled = x * scale
            u = grad * t.rows[which : which + 1, :]
            inner = jnp.mean(u * scaled, axis=-1, keepdims=True)
            total = before + scale * (u - scaled * inner)
            t.totals[which : which + 1, :] += jnp.sum(grad * scaled, axis=0, keepdims=True)
            if which == 2:
                t.stream[block, :] = total
                grad_mid[block, :] = total.astype(BF16)
            else:
                t.stream[block, :] = jnp.where(kept, total, 0.0)
                t.totals[0:1, :] += jnp.sum(jnp.where(kept, 0.0, total), axis=0, keepdims=True)

        loop(0, s.rows // 64, body)

    def out_back(self, out_copy, weight, planes, grad_mid, grad_attended, far):
        o, t, s = self.o, self.t, self.sizes
        groups = TILE // s.group

        def attended(j):
            block = weight[pl.ds(j * groups, groups)].reshape(TILE, s.width)
            grad_attended[:, at(j, TILE)] = times_trans(grad_mid[...], block).astype(BF16)

        loop(0, s.width // TILE, attended)
        out_copy.wait_recv()
        load = pltpu.make_async_copy(o.far_out, far, t.pre.at[6])
        load.start()
        load.wait()
        rows = self.plan.chunks * s.group
        for part, (start, size) in enumerate(s.half_windows):
            columns = pl.ds(start, size)
            left = jnp.concatenate([planes[0].reshape(rows, s.rows), planes[1].reshape(rows, s.rows)], axis=1)
            right = jnp.concatenate([grad_mid[:, columns], far[:, columns]], axis=0)
            acc = self.reduces[OUT][part].acc
            acc[...] = matmul(left, right).astype(BF16).reshape(acc.shape)
            self.advance(OUT, (part,))

    def attend_back(self, low, high, qkv, grad_attended, prob):
        o, t = self.o, self.t
        lane = lax.broadcasted_iota(I32, (1, LANES), 1)

        def prob_copies(slot, pair):
            return [pltpu.make_async_copy(o.prob.at[pl.ds(2 * pair, 2)], prob.at[slot], t.tile_sem.at[slot, 0])]

        def body(pair, slot):
            columns = at(pair, LANES)
            q, k, v = (ref[:, columns] for ref in qkv)
            grad = grad_attended[:, columns]
            found = [[], [], []]
            for e in range(2):
                own = jnp.where((lane < HEAD) == (e == 0), grad, jnp.zeros_like(grad))
                weights = prob[slot, e]
                wide = weights.astype(F32)
                grad_prob = times_trans(own, v)
                delta = jnp.sum(grad_prob * wide, axis=-1, keepdims=True)
                scores = (wide * (grad_prob - delta)).astype(BF16)
                t.big[2 * pair + e] = scores
                found[0].append(matmul(scores, k))
                found[1].append(trans_times(scores, q))
                found[2].append(trans_times(weights, grad))
            for ref, (first, second) in zip(self.grad_qkv, found):
                ref[:, columns] = jnp.where(lane < HEAD, first, second).astype(BF16)

        streamed(low, high, prob_copies, body)

    def attention_copies(self, part):
        window = pl.ds(*self.sizes.half_windows[part])
        return [
            to_sibling(
                self.place,
                self.grad_qkv[which].at[:, window],
                self.o.far_attn[which].at[:, window],
                self.t.attn_sem.at[part, which],
            )
            for which in range(3)
        ]

    def send_attention(self, part):
        for copy in self.attention_copies(part):
            copy.start()

    def attention_weights(self, part, planes, far):
        o, t, s = self.o, self.t, self.sizes
        columns = pl.ds(*s.half_windows[part])
        rows = self.plan.chunks * s.group
        loads = []
        for which, copy in enumerate(self.attention_copies(part)):
            copy.wait_recv()
            loads.append(pltpu.make_async_copy(o.far_attn[which].at[:, columns], far.at[which], t.pre.at[which]))
            loads[-1].start()
        for which in range(3):
            loads[which].wait()
            left = jnp.concatenate([planes[0].reshape(rows, s.rows), planes[1].reshape(rows, s.rows)], axis=1)
            right = jnp.concatenate([self.grad_qkv[which][:, columns], far[which]], axis=0)
            acc = self.reduces[which][part].acc
            acc[...] = matmul(left, right).astype(BF16).reshape(acc.shape)
            self.advance(which, (part,))

    def attention_input(self, back, held):
        o, t, s = self.o, self.t, self.sizes
        groups = TILE // s.group

        def weight_copies(slot, j):
            return [
                pltpu.make_async_copy(
                    o.full[which].at[pl.ds(j * groups, groups)], held.at[slot, which], t.tile_sem.at[slot, which]
                )
                for which in range(3)
            ]

        def body(j, slot):
            back[:, at(j, TILE)] = sum(
                times_trans(self.grad_qkv[which][...], held[slot, which].reshape(TILE, s.width)) for which in range(3)
            )

        streamed(0, s.width // TILE, weight_copies, body)

    def table_back(self):
        i, t, s = self.i, self.t, self.sizes
        width, step = BUCKETS * HEADS, 4

        def count(total, buckets):
            copy = pltpu.make_async_copy(i.buckets, buckets, t.pre.at[7])
            copy.start()
            total[...] = jnp.zeros_like(total)
            copy.wait()

            def body(j):
                left, right = [], []
                for k in range(step):
                    block = at(j * step + k, 16)
                    left.append(bucket_rows(buckets[block, :]))
                    right.append(t.big[:, block, :].reshape(HEADS * 16, s.rows))
                total[...] += times_trans(jnp.concatenate(left, axis=1), jnp.concatenate(right, axis=1))

            loop(0, s.rows // (16 * step), body)
            found = total[...].T
            row = lax.broadcasted_iota(I32, found.shape, 0)
            lane = lax.broadcasted_iota(I32, found.shape, 1)
            found = jnp.where(row % 16 == lane % 16, found, 0.0)
            by_head = jnp.sum(found.reshape(HEADS, 16, width), axis=1)
            summed = jnp.dot(
                by_head, same_bucket(width), precision=lax.Precision.HIGHEST, preferred_element_type=F32
            )
            head = lax.broadcasted_iota(I32, summed.shape, 0)
            lane = lax.broadcasted_iota(I32, summed.shape, 1)
            t.totals[3:4, :width] = jnp.sum(jnp.where(lane % HEADS == head, summed, 0.0), axis=0, keepdims=True)

        pl.run_scoped(count, pltpu.VMEM((width, HEADS * 16), F32), pltpu.VMEM((s.rows, s.rows), I32))


def per_device(
    plan,
    tokens,
    patch_keep,
    text_len,
    buckets,
    mask_embed,
    norm_attn,
    w_query,
    w_key,
    w_value,
    w_out,
    bias_table,
    norm_ffn,
    w_gate,
    w_up,
    w_down,
    cotangent,
):
    rows, width = tokens.shape
    assert patch_keep.shape[0] == 1
    device = lax.axis_index("wide") * plan.narrow + lax.axis_index("narrow")
    small = (mask_embed, norm_attn, norm_ffn, bias_table)
    counts = [member.shape[0] for member in small]
    vectors = jnp.concatenate(list(small) + [jnp.zeros((LANES - sum(counts),), BF16)]).reshape(1, LANES)
    weights = (w_query, w_key, w_value, w_out, w_gate, w_up, w_down)
    shards = [jnp.pad(weight, ((0, -weight.shape[0] % 16), (0, 0))) for weight in weights[:DOWN]] + [w_down]
    sizes = Sizes(plan, rows, width, w_gate.shape[1], [weight.shape[0] for weight in weights])
    f = Layer(plan, sizes).call(vectors, counts, shards, tokens, patch_keep, text_len, buckets, cotangent)

    def own(row, size):
        return lax.dynamic_slice(f.sums[row], (device * size,), (size,))

    query, key, value, out, gate, up, down = f.grads
    return (
        f.result,
        f.input_grad,
        own(0, mask_embed.shape[0]),
        own(1, norm_attn.shape[0]),
        query,
        key,
        value,
        out,
        own(3, bias_table.shape[0]),
        own(2, norm_ffn.shape[0]),
        gate,
        up,
        down,
    )


def solution(mesh):
    rows, flat = P(("wide", "narrow"), None), P(("wide", "narrow"))
    plan = Plan(mesh.shape["wide"], mesh.shape["narrow"])
    return jax.shard_map(
        functools.partial(per_device, plan),
        mesh=mesh,
        in_specs=(rows, rows, flat, rows, flat, flat, rows, rows, rows, rows, flat, flat, rows, rows, rows, rows),
        out_specs=(rows, rows, flat, flat, rows, rows, rows, rows, flat, flat, rows, rows, rows),
        check_vma=False,
    )
```

```python
import functools
import types

import jax
import jax.numpy as jnp
from jax import lax
from jax.experimental import pallas as pl
from jax.experimental.pallas import tpu as pltpu
from jax.sharding import PartitionSpec as P

MESH = pl.DeviceIdType.MESH
VMEM_LIMIT = 62 << 20
HEADS = 16
HEAD = 64
BUCKETS = 32
EPSILON = 1e-06
NEG_FILL = -1000000000.0
LANES = 128
TILE = 256
CONTRACT_LAST = (((1,), (1,)), ((), ()))
CONTRACT_FIRST = (((0,), (0,)), ((), ()))
BF16, F32, I32 = jnp.bfloat16, jnp.float32, jnp.int32
GELU_SCALE = 0.7978845608028654
GELU_CUBE = 0.044715


def round_up(value, unit):
    return -(-value // unit) * unit


def matmul(left, right):
    return jnp.dot(left, right, preferred_element_type=F32)


def times_trans(left, right):
    return lax.dot_general(left, right, CONTRACT_LAST, preferred_element_type=F32)


def trans_times(left, right):
    return lax.dot_general(left, right, CONTRACT_FIRST, preferred_element_type=F32)


class Plan:
    def __init__(self, wide, narrow):
        self.wide, self.narrow = wide, narrow
        self.bits = [2 << i for i in range(wide.bit_length() - 2)]
        self.chunks = wide // 2
        assert wide == 2 << len(self.bits)


def span(bits):
    out = [0]
    for bit in bits:
        out = out + [member ^ bit for member in out]
    return out


def halves(start, size):
    half = round_up(size // 2, LANES)
    return [(start, half), (start + half, size - half)] if size > 2 * LANES else [(start, size)]


def enter(plan):
    w, n = lax.axis_index("wide"), lax.axis_index("narrow")
    barrier = pltpu.get_barrier_semaphore()
    partners = [(w ^ bit, n) for bit in [1] + plan.bits]
    partners += [(w, lax.rem(n + d, plan.narrow)) for d in range(1, plan.narrow)]
    for partner in partners:
        pl.semaphore_signal(barrier, inc=1, device_id=partner, device_id_type=MESH)
    pl.semaphore_wait(barrier, len(partners))
    return w, n


def loop(low, high, body):
    def step(i, carry):
        body(i)
        return carry

    lax.fori_loop(low, high, step, 0)


def at(index, size):
    return pl.ds(pl.multiple_of(index * size, size), size)


def streamed(low, high, copies, body):
    for copy in copies(lax.rem(low, 2), low):
        copy.start()

    def step(i):
        slot = lax.rem(i, 2)

        @pl.when(i + 1 < high)
        def _():
            for copy in copies(1 - slot, i + 1):
                copy.start()

        for copy in copies(slot, i):
            copy.wait()
        body(i, slot)

    loop(low, high, step)


def run(kernel, inputs, outputs, scratch, resident, scalars, collective_id, name):
    sizes = [len(jax.tree.leaves(tree)) for tree in (inputs, outputs, scratch)]
    forms = [jax.tree.structure(tree) for tree in (inputs, outputs, scratch)]

    def flat(*refs):
        first, second = sizes[0], sizes[0] + sizes[1]
        parts = (refs[:first], refs[first:second], refs[second:])
        kernel(*(types.SimpleNamespace(**form.unflatten(part)) for form, part in zip(forms, parts)))

    def space(key):
        return pltpu.VMEM if key in resident else pltpu.SMEM if key in scalars else pl.ANY

    def specs(tree):
        return jax.tree.leaves(
            {
                key: jax.tree.map(lambda _, key=key: pl.BlockSpec(memory_space=space(key)), value)
                for key, value in tree.items()
            }
        )

    result = pl.pallas_call(
        flat,
        out_shape=jax.tree.leaves(outputs),
        in_specs=specs(inputs),
        out_specs=specs(outputs),
        scratch_shapes=jax.tree.leaves(scratch),
        compiler_params=pltpu.CompilerParams(
            collective_id=collective_id, has_side_effects=collective_id is not None, vmem_limit_bytes=VMEM_LIMIT
        ),
        name=name,
    )(*jax.tree.leaves(inputs))
    return types.SimpleNamespace(**forms[1].unflatten(result))


def sems(*shape):
    return pltpu.SemaphoreType.DMA(shape)


def struct(shape, dtype):
    return jax.ShapeDtypeStruct(shape, dtype)


class Gather:
    def __init__(self, plan, rows, window):
        self.plan, self.rows = plan, rows
        self.start_column, self.columns = window
        self.padded = round_up(self.rows, 16)
        self.aligned = self.padded == self.rows
        self.group = plan.narrow * self.rows
        self.parts = halves(*window)
        self.orders = [plan.bits, plan.bits[::-1]][: len(self.parts)]
        self.chunks = plan.chunks

    def reserve(self):
        count, parts = self.plan.narrow, len(self.parts)
        return [sems(2, count), sems(2, parts, self.chunks), sems(2, parts, self.chunks), sems(2)]

    def stages_out(self):
        return [] if self.aligned else [struct((self.plan.narrow, self.padded, self.columns), BF16)]

    def bind(self, place, shard, out, stage, refs):
        self.w, self.n = place
        self.shard, self.out = shard, out
        self.zsem, self.bsem, self.csem, self.lsem = refs
        if not self.aligned:
            self.stage = stage[0]

    def window(self):
        return pl.ds(self.start_column, self.columns)

    def own_slot(self):
        if self.aligned:
            rows = pl.ds(pl.multiple_of(self.n * self.rows, self.rows), self.rows)
            return self.out.at[self.w, rows, self.window()]
        return self.stage.at[self.n]

    def z_copy(self, d):
        return pltpu.make_async_remote_copy(
            src_ref=self.shard.at[:, self.window()],
            dst_ref=self.own_slot(),
            send_sem=self.zsem.at[0, d],
            recv_sem=self.zsem.at[1, d],
            device_id=(self.w, lax.rem(self.n + d, self.plan.narrow)),
            device_id_type=MESH,
        )

    def place_copy(self):
        return pltpu.make_async_copy(self.shard.at[:, self.window()], self.own_slot(), self.lsem.at[0])

    def pack_group(self, stage, compact):
        copy = pltpu.make_async_copy(self.stage, stage, self.lsem.at[1])
        copy.start()
        copy.wait()
        size, wide = self.group, self.plan.narrow * self.padded
        row = lax.broadcasted_iota(I32, (size, wide), 0)
        column = lax.broadcasted_iota(I32, (size, wide), 1)
        pick = column == (row // self.rows) * self.padded + row % self.rows
        compact[...] = matmul(pick.astype(F32).astype(BF16), stage[...].reshape(wide, self.columns)).astype(BF16)
        copy = pltpu.make_async_copy(compact, self.out.at[self.w, :, self.window()], self.lsem.at[1])
        copy.start()
        copy.wait()

    def start(self):
        for d in range(1, self.plan.narrow):
            self.z_copy(d).start()
        self.place_copy().start()

    def hop(self, sems, part, mask, bit, slot):
        start, size = self.parts[part]
        target = self.out.at[self.w ^ mask, :, pl.ds(start, size)]
        return pltpu.make_async_remote_copy(
            src_ref=target,
            dst_ref=target,
            send_sem=sems.at[0, part, slot],
            recv_sem=sems.at[1, part, slot],
            device_id=(self.w ^ bit, self.n),
            device_id_type=MESH,
        )

    def hops(self, part, stage):
        order = self.orders[part]
        masks = span(order[:stage])
        return [self.hop(self.bsem, part, mask, order[stage], len(masks) + i - 1) for i, mask in enumerate(masks)]

    def core_hops(self, part, stage):
        masks = span(self.orders[part])
        low, high = (0, 1) if stage == 0 else (1 << (stage - 1), 1 << stage)
        return [self.hop(self.csem, part, masks[i], 1, i) for i in range(low, high)]

    def stages(self):
        return len(self.plan.bits) + 2

    def step(self, stage):
        bits, parts = len(self.plan.bits), range(len(self.parts))
        if stage == 0:
            for d in range(1, self.plan.narrow):
                self.z_copy(d).wait_recv()
            self.place_copy().wait()
            if not self.aligned:
                pl.run_scoped(
                    self.pack_group,
                    pltpu.VMEM((self.plan.narrow, self.padded, self.columns), BF16),
                    pltpu.VMEM((self.group, self.columns), BF16),
                )
        elif stage <= bits:
            for part in parts:
                for copy in self.hops(part, stage - 1):
                    copy.wait_recv()
        else:
            for part in parts:
                for s in range(bits + 1):
                    for copy in self.core_hops(part, s):
                        copy.wait_recv()
        if stage < bits:
            for part in parts:
                for copy in self.hops(part, stage):
                    copy.start()
        if stage <= bits:
            for part in parts:
                for copy in self.core_hops(part, stage):
                    copy.start()

    def finish(self):
        for d in range(1, self.plan.narrow):
            self.z_copy(d).wait_send()
        for part in range(len(self.parts)):
            for s in range(len(self.plan.bits)):
                for copy in self.hops(part, s):
                    copy.wait_send()
            for s in range(len(self.plan.bits) + 1):
                for copy in self.core_hops(part, s):
                    copy.wait_send()


class Swap:
    def __init__(self, plan):
        self.plan = plan

    def reserve(self):
        return sems(3, self.plan.chunks)

    def bind(self, place, source, out, sem):
        self.w, self.n = place
        self.source, self.out, self.sem = source, out, sem
        self.both = len(out.shape) == 4
        self.group = source.shape[0] // self.plan.wide

    def chunk(self, index):
        return self.source.at[pl.ds(pl.multiple_of(index * self.group, self.group), self.group), :]

    def local(self, slot):
        return pltpu.make_async_copy(self.chunk(self.w ^ (2 * slot)), self.out.at[0, slot], self.sem.at[2, slot])

    def landing(self, slot):
        return self.out.at[1, slot] if self.both else self.out.at[slot]

    def remote(self, slot, source):
        return pltpu.make_async_remote_copy(
            src_ref=source,
            dst_ref=self.landing(slot),
            send_sem=self.sem.at[0, slot],
            recv_sem=self.sem.at[1, slot],
            device_id=(self.w ^ 1, self.n),
            device_id_type=MESH,
        )

    def send(self, slot):
        return self.remote(slot, self.chunk(self.w ^ 1 ^ (2 * slot)))

    def start(self):
        for slot in range(self.plan.chunks):
            self.send(slot).start()
            if self.both:
                self.local(slot).start()

    def wait_recv(self):
        for slot in range(self.plan.chunks):
            self.remote(slot, self.landing(slot)).wait_recv()

    def finish(self):
        for slot in range(self.plan.chunks):
            self.send(slot).wait_send()
            if self.both:
                self.local(slot).wait()


def to_sibling(place, source, target, sem):
    return pltpu.make_async_remote_copy(
        src_ref=source,
        dst_ref=target,
        send_sem=sem.at[0],
        recv_sem=sem.at[1],
        device_id=(place[0] ^ 1, place[1]),
        device_id_type=MESH,
    )


def column_of(row):
    eye = lax.broadcasted_iota(I32, (LANES, LANES), 0) == lax.broadcasted_iota(I32, (LANES, LANES), 1)
    pieces = [
        jnp.sum(jnp.where(eye, row[:, start : start + LANES], 0.0), axis=1, keepdims=True)
        for start in range(0, row.shape[1], LANES)
    ]
    return jnp.concatenate(pieces, axis=0)


def unpack_small(plan, packed, sizes):
    summed = jnp.sum(packed.astype(F32).reshape(plan.wide, plan.narrow, 16, LANES), axis=1)
    rows = []
    for i, size in enumerate(sizes):
        each = LANES // (size * plan.narrow)
        blocks = [
            sum(summed[first + j, i : i + 1, :] for j in range(each))
            for first in range(0, plan.wide, each)
        ]
        rows.append(jnp.concatenate(blocks, axis=1))
    return rows


def same_bucket(width):
    row = lax.broadcasted_iota(I32, (width, width), 0) // HEADS
    column = lax.broadcasted_iota(I32, (width, width), 1) // HEADS
    return (row == column).astype(F32)


def spread_table(table_row):
    width = BUCKETS * HEADS
    lane = lax.broadcasted_iota(I32, (HEADS, width), 1)
    head = lax.broadcasted_iota(I32, (HEADS, width), 0)
    same = lane % HEADS == head
    picked = jnp.where(same, table_row, 0.0).astype(BF16)
    spread = matmul(picked, same_bucket(width).astype(BF16))
    return jnp.concatenate(
        [jnp.where(same, spread[h : h + 1, :], 0.0).astype(BF16) for h in range(HEADS)], axis=0
    )


def bucket_rows(bucket):
    small = bucket.astype(F32).astype(BF16)
    one, zero = jnp.ones_like(small), jnp.zeros_like(small)
    return jnp.concatenate(
        [jnp.where(small == jnp.asarray(j, BF16), one, zero) for j in range(BUCKETS)], axis=0
    )


class Reduce:
    def __init__(self, plan, rows, window, order):
        self.plan, self.rows = plan, rows
        self.start_column, self.columns = window
        self.padded = round_up(rows, 16)
        self.aligned = self.padded == rows
        self.group = plan.narrow * rows
        self.order = order
        self.chunks = plan.chunks

    def reserve(self):
        count, columns = self.plan.narrow, self.columns
        shapes = [
            sems(2, self.chunks),
            sems(2, count),
            pltpu.VMEM((self.chunks, self.group, columns), BF16),
            pltpu.VMEM((self.chunks - 1, self.group, columns), BF16),
            pltpu.VMEM((count - 1, self.padded, columns), BF16),
        ]
        if not self.aligned:
            shapes.append(pltpu.VMEM((count, self.padded, columns), BF16))
        return shapes

    def bind(self, place, out, refs):
        self.w, self.n = place
        self.out, self.done = out, 0
        self.bsem, self.zsem, self.acc, self.received, self.zreceived = refs[:5]
        if not self.aligned:
            self.stage = refs[5]

    def hops(self, stage):
        bit, masks = self.order[stage], span(self.order[stage + 1 :])
        base = self.chunks - 2 * len(masks)
        return [
            (
                mask >> 1,
                base + k,
                pltpu.make_async_remote_copy(
                    src_ref=self.acc.at[(bit ^ mask) >> 1],
                    dst_ref=self.received.at[base + k],
                    send_sem=self.bsem.at[0, base + k],
                    recv_sem=self.bsem.at[1, base + k],
                    device_id=(self.w ^ bit, self.n),
                    device_id_type=MESH,
                ),
            )
            for k, mask in enumerate(masks)
        ]

    def z_copy(self, d):
        peer = lax.rem(self.n + d, self.plan.narrow)
        source = self.acc.at[0, at(peer, self.rows), :] if self.aligned else self.stage.at[peer]
        return pltpu.make_async_remote_copy(
            src_ref=source,
            dst_ref=self.zreceived.at[d - 1],
            send_sem=self.zsem.at[0, d],
            recv_sem=self.zsem.at[1, d],
            device_id=(self.w, peer),
            device_id_type=MESH,
        )

    def step(self, stage):
        bits = len(self.order)
        if 1 <= stage <= bits:
            for slot, k, copy in self.hops(stage - 1):
                copy.wait_recv()

                def body(j, slot=slot, k=k):
                    block = at(j, 16)
                    self.acc[slot, block, :] += self.received[k, block, :]

                loop(0, self.group // 16, body)
        if stage < bits:
            for _, _, copy in self.hops(stage):
                copy.start()
        elif stage == bits:
            if not self.aligned:
                size, wide = self.group, self.plan.narrow * self.padded
                row = lax.broadcasted_iota(I32, (wide, size), 0)
                column = lax.broadcasted_iota(I32, (wide, size), 1)
                pick = row == (column // self.rows) * self.padded + column % self.rows
                self.stage[...] = (
                    matmul(pick.astype(F32).astype(BF16), self.acc[0]).astype(BF16).reshape(self.stage.shape)
                )
            for d in range(1, self.plan.narrow):
                self.z_copy(d).start()
        else:
            total = self.acc[0, at(self.n, self.rows), :] if self.aligned else self.stage[self.n]
            total = total.astype(F32)
            for d in range(1, self.plan.narrow):
                self.z_copy(d).wait_recv()
                total = total + self.zreceived[d - 1].astype(F32)
            self.out[:, pl.ds(self.start_column, self.columns)] = total[: self.rows]

    def finish(self):
        for stage in range(len(self.order)):
            for _, _, copy in self.hops(stage):
                copy.wait_send()
        for d in range(1, self.plan.narrow):
            self.z_copy(d).wait_send()


class SumAll:
    def __init__(self, plan, shape):
        self.shape = shape
        self.rounds = [(bit, 0) for bit in [1] + plan.bits]
        self.rounds += [(0, 1 << k) for k in range(plan.narrow.bit_length() - 1)]

    def reserve(self):
        count = len(self.rounds)
        return [sems(2, count)] + [pltpu.VMEM((count, *self.shape), F32)] * 2

    def bind(self, place, out, refs):
        self.w, self.n = place
        self.out = out
        self.sem, self.held, self.received = refs

    def copy(self, turn):
        bit, other = self.rounds[turn]
        return pltpu.make_async_remote_copy(
            src_ref=self.held.at[turn],
            dst_ref=self.received.at[turn],
            send_sem=self.sem.at[0, turn],
            recv_sem=self.sem.at[1, turn],
            device_id=(self.w ^ bit, self.n ^ other),
            device_id_type=MESH,
        )

    def start(self, value):
        self.held[0] = value
        self.copy(0).start()

    def step(self, turn):
        self.copy(turn).wait_recv()
        total = self.held[turn] + self.received[turn]
        if turn + 1 < len(self.rounds):
            self.held[turn + 1] = total
            self.copy(turn + 1).start()
        else:
            self.out[...] = total

    def finish(self):
        for turn in range(len(self.rounds)):
            self.copy(turn).wait_send()


class Sizes:
    def __init__(self, plan, rows, width, ff, shards):
        self.plan, self.rows, self.width, self.ff = plan, rows, width, ff
        self.shards = shards
        self.group = plan.narrow * shards[0]
        self.down_group = plan.narrow * shards[DOWN]
        step = round_up(ff // 3, BLOCK)
        self.ff_windows = [(start, min(step, ff - start)) for start in range(0, ff, step)]
        self.half_windows = [(0, width // 2), (width // 2, width // 2)]
        self.blocks = round_up(ff, BLOCK) // BLOCK

    def full(self):
        wide = self.plan.wide
        return (
            [(wide, self.group, self.width)] * 4
            + [(wide, self.group, self.ff)] * 2
            + [(wide, self.down_group, self.width)]
        )


QUERY, KEY, VALUE, OUT, GATE, UP, DOWN = range(7)
BLOCK = 512


class Layer:
    def __init__(self, plan, sizes):
        self.plan, self.sizes = plan, sizes
        whole = (0, sizes.width)
        wide = [(weight, window) for window in sizes.ff_windows for weight in (GATE, UP)]
        down = [(DOWN, window) for window in sizes.half_windows]
        self.order = [(weight, whole) for weight in (QUERY, KEY, VALUE, OUT)] + down + wide
        self.small = Gather(plan, 16, (0, LANES))
        self.items = [self.small] + [Gather(plan, sizes.shards[weight], window) for weight, window in self.order]
        self.swaps = [Swap(plan) for _ in range(4)]
        self.extra = self.small.stages() - 4
        ways = [plan.bits, plan.bits[::-1]]
        self.reduces = []
        for weight in range(7):
            turn = 1 if weight in (UP, KEY, OUT) else 0
            pairs = enumerate(sizes.half_windows)
            if weight in (GATE, UP):
                pairs = [(0, window) for window in sizes.ff_windows]
            self.reduces.append([Reduce(plan, sizes.shards[weight], window, ways[k ^ turn]) for k, window in pairs])
        self.sums = SumAll(plan, (8, sizes.width))

    def call(self, vectors, counts, shards, tokens, patch_keep, text_len, buckets, cotangent):
        plan, s = self.plan, self.sizes
        self.counts = counts
        rows, width, chunks = s.rows, s.width, plan.chunks
        row_block = struct((rows, width), BF16)
        inputs = dict(
            vectors=vectors,
            shards=shards[:DOWN],
            down_shard=shards[DOWN],
            tokens=tokens,
            patch_keep=patch_keep,
            text_len=text_len,
            buckets=buckets,
            cotangent=cotangent,
        )
        outputs = dict(
            small=struct((plan.wide, plan.narrow * 16, LANES), BF16),
            full=[struct(shape, BF16) for shape in s.full()],
            stages=[item.stages_out() for item in self.items],
            qkv=[row_block] * 3,
            prob=struct((HEADS, rows, rows), BF16),
            turned=[struct((2, chunks, s.group, rows), BF16)] * 3,
            hidden_far=struct((chunks, s.down_group, rows), BF16),
            cot_far=row_block,
            far_ff=struct((2, s.blocks, rows, BLOCK), BF16),
            far_out=row_block,
            far_attn=[row_block] * 3,
            result=row_block,
            input_grad=struct((rows, width), F32),
            grads=[
                struct((size, s.ff if weight in (GATE, UP) else width), F32) for weight, size in enumerate(s.shards)
            ],
            sums=struct((8, width), F32),
        )
        square = pltpu.VMEM((rows, width), BF16)
        down_rows = round_up(s.shards[DOWN], 16)
        scratch = dict(
            items=[item.reserve() for item in self.items],
            swaps=[swap.reserve() for swap in self.swaps],
            reduces=[[item.reserve() for item in pair] for pair in self.reduces],
            exchange=self.sums.reserve(),
            direct=sems(2),
            load=sems(len(self.items)),
            pre=sems(8),
            packed=pltpu.VMEM((16, LANES), BF16),
            small=pltpu.VMEM((plan.wide, plan.narrow * 16, LANES), BF16),
            down_shard=pltpu.VMEM((down_rows, width), BF16),
            rows=pltpu.VMEM((8, width), F32),
            keep=pltpu.VMEM((rows, 1), F32),
            big=pltpu.VMEM((HEADS, rows, rows), BF16),
            stream=pltpu.VMEM((rows, width), F32),
            normed=square,
            totals=pltpu.VMEM((8, width), F32),
            pair_sem=sems(2),
            tile_sem=sems(2, 3),
            ff_sem=sems(len(s.ff_windows), 2, 2, 2),
            out_sem=sems(2),
            attn_sem=sems(2, 3, 2),
            store=sems(6),
        )
        return run(
            self.kernel,
            inputs,
            outputs,
            scratch,
            {"vectors", "down_shard", "patch_keep", "cotangent", "grads", "sums"},
            {"text_len"},
            0,
            "layer",
        )

    def kernel(self, i, o, t):
        self.i, self.o, self.t = i, o, t
        plan, s = self.plan, self.sizes
        square = pltpu.VMEM((s.rows, s.width), BF16)
        planes = pltpu.VMEM((2, plan.chunks, s.group, s.rows), BF16)
        weight_space = pltpu.VMEM((plan.wide, s.group, s.width), BF16)
        self.pack()
        self.place = place = enter(plan)
        self.small.bind(place, t.packed, o.small, o.stages[0], t.items[0])
        for item, (weight, _), stage, refs in zip(self.items[1:], self.order, o.stages[1:], t.items[1:]):
            item.bind(place, t.down_shard if weight == DOWN else i.shards[weight], o.full[weight], stage, refs)
        for pair, out, refs in zip(self.reduces, o.grads, t.reduces):
            for item, own in zip(pair, refs):
                item.bind(place, out, own)
        self.sums.bind(place, o.sums, t.exchange)
        self.direct = to_sibling(place, i.cotangent, o.cot_far, t.direct)

        for item in self.items[:3]:
            item.start()
        self.direct.start()
        for turn in range(-self.extra, 4):
            self.tick(turn)
        self.set_up()
        pl.run_scoped(
            self.attention_phase,
            [weight_space] * 3,
            [square] * 4,
            [pltpu.VMEM((s.width, s.rows), BF16)] * 2,
            pltpu.VMEM((2, 2, s.rows, s.rows), BF16),
            pltpu.VMEM((HEADS * 16, BUCKETS * 16), BF16),
            pltpu.VMEM((s.rows, s.rows), I32),
        )
        pl.run_scoped(
            self.feed_phase,
            [pltpu.VMEM((plan.wide, s.group, s.ff_windows[0][1]), BF16)] * 2,
            pltpu.VMEM((s.ff, s.width), BF16),
            pltpu.VMEM((s.ff, s.rows), BF16),
            pltpu.VMEM((plan.chunks, s.down_group, s.rows), BF16),
            square,
            planes,
            pltpu.VMEM((2, 2, s.rows, TILE), BF16),
            sems(plan.wide),
        )
        pl.run_scoped(
            self.back_phase,
            planes,
            [square] * 3,
            pltpu.VMEM((s.rows, s.width), F32),
            square,
        )


    def tick(self, turn):
        stages, turn = self.small.stages(), turn + self.extra
        for stage in range(stages):
            k = turn - stage
            if 0 <= k < len(self.items):
                self.items[k].step(stage)
        if turn + 3 < len(self.items):
            self.items[turn + 3].start()

    def load(self, weight, window, target):
        k = 1 + self.order.index((weight, window))
        return pltpu.make_async_copy(self.o.full[weight].at[:, :, pl.ds(*window)], target, self.t.load.at[k])

    def pack(self):
        i, t = self.i, self.t
        device = lax.axis_index("wide") * self.plan.narrow + lax.axis_index("narrow")
        source = lax.broadcasted_iota(I32, (LANES, LANES), 0)
        lane = lax.broadcasted_iota(I32, (LANES, LANES), 1)
        row = lax.broadcasted_iota(I32, (16, LANES), 0)
        packed, offset = jnp.zeros((16, LANES), F32), 0
        for k, size in enumerate(self.counts):
            first = lax.rem(device * size, LANES)
            pick = (source == offset + lane - first) & (lane >= first) & (lane < first + size)
            found = matmul(i.vectors[...], pick.astype(F32).astype(BF16))
            packed = jnp.where(row == k, found, packed)
            offset += size
        t.packed[...] = packed.astype(BF16)
        size = i.down_shard.shape[0]
        t.down_shard[...] = jnp.concatenate(
            [i.down_shard[...], jnp.zeros((t.down_shard.shape[0] - size, self.sizes.width), BF16)], axis=0
        )

    def set_up(self):
        i, o, t = self.i, self.o, self.t
        copy = pltpu.make_async_copy(o.small, t.small, t.load.at[0])
        copy.start()
        tokens = pltpu.make_async_copy(i.tokens, t.normed, t.pre.at[7])
        tokens.start()
        patches, rows = i.patch_keep.shape[1], self.sizes.rows
        row = lax.broadcasted_iota(I32, (rows, patches), 0)
        lane = lax.broadcasted_iota(I32, (rows, patches), 1)
        kept = jnp.sum(jnp.where(row == lane, i.patch_keep[...].astype(F32), 0.0), axis=1, keepdims=True)
        t.keep[...] = jnp.where(lax.broadcasted_iota(I32, (rows, 1), 0) >= patches, 1.0, kept)
        t.totals[...] = jnp.zeros_like(t.totals)
        copy.wait()
        embed, gain_one, gain_two, table = unpack_small(self.plan, t.small[...], self.counts)
        t.rows[...] = jnp.concatenate([embed, gain_one, gain_two, jnp.zeros((5, self.sizes.width), F32)], axis=0)
        self.table_row = table
        tokens.wait()

        def body(j):
            block = at(j, 64)
            t.stream[block, :] = jnp.where(
                t.keep[block, :] > 0.5, t.normed[block, :].astype(F32), t.rows[0:1, :]
            )

        loop(0, rows // 64, body)
        self.norm(1)

    def norm(self, gain):
        t = self.t

        def body(j):
            block = at(j, 64)
            x = t.stream[block, :]
            scale = lax.rsqrt(jnp.mean(x * x, axis=-1, keepdims=True) + EPSILON)
            t.normed[block, :] = (x * scale * t.rows[gain : gain + 1, :]).astype(BF16)

        loop(0, self.sizes.rows // 64, body)

    def turn(self, source, target):
        def body(j):
            target[at(j, LANES), :] = source[:, at(j, LANES)].T

        loop(0, self.sizes.width // LANES, body)


    def attention_phase(self, held, qkva, turned, prob, table, buckets):
        o, t, s = self.o, self.t, self.sizes
        bucket_copy = pltpu.make_async_copy(self.i.buckets, buckets, t.pre.at[7])
        bucket_copy.start()
        normed, attended, second, _ = self.swaps
        for swap, source, target, sem in zip(
            self.swaps, (turned[0], turned[1], turned[0]), o.turned, t.swaps
        ):
            swap.bind(self.place, source, target, sem)
        store = [pltpu.make_async_copy(qkva[k], o.qkv[k], t.store.at[k]) for k in range(3)]
        whole = (0, s.width)
        loads = [self.load(weight, whole, held[weight % 3]) for weight in (QUERY, KEY, VALUE, OUT)]
        self.turn(t.normed, turned[0])
        normed.start()
        table[...] = spread_table(self.table_row)
        self.tick(4)
        loads[QUERY].start()
        blocks = s.rows // 16
        bucket_copy.wait()
        self.bias(0, blocks // 2, table, buckets)
        self.tick(5)
        loads[KEY].start()
        loads[QUERY].wait()
        self.project(held[0], qkva[0])
        store[0].start()
        self.bias(blocks // 2, blocks, table, buckets)
        self.tick(6)
        loads[VALUE].start()
        loads[KEY].wait()
        self.project(held[1], qkva[1])
        store[1].start()
        self.tick(7)
        loads[OUT].start()
        loads[VALUE].wait()
        self.project(held[2], qkva[2])
        store[2].start()
        count = HEADS // 2
        self.attend(0, 3 * count // 8, qkva, prob)
        self.tick(8)
        self.attend(3 * count // 8, 6 * count // 8, qkva, prob)
        self.tick(9)
        self.attend(6 * count // 8, count, qkva, prob)
        for slot in range(2):
            self.prob_copy(slot, count - 2 + slot, prob).wait()
        loads[OUT].wait()

        def body(j):
            block = held[0][:, :, at(j, TILE)].reshape(s.width, TILE)
            t.stream[:, at(j, TILE)] += matmul(qkva[3][...], block)

        loop(0, s.width // TILE, body)
        self.turn(qkva[3], turned[1])
        attended.start()
        normed.finish()
        self.norm(2)
        self.turn(t.normed, turned[0])
        second.start()
        for copy in store:
            copy.wait()
        attended.finish()
        second.finish()

    def bias(self, low, high, table, buckets):
        i, t = self.i, self.t
        live = lax.broadcasted_iota(I32, (1, self.sizes.rows), 1) < i.patch_keep.shape[1] + i.text_len[0]

        def body(j):
            block = at(j, 16)
            spread = matmul(table[...], bucket_rows(buckets[block, :]))
            spread = jnp.where(live, spread, NEG_FILL).astype(BF16)
            t.big[:, block, :] = spread.reshape(HEADS, 16, spread.shape[-1])

        loop(low, high, body)

    def project(self, weight, target):
        def body(j):
            block = weight[:, :, at(j, TILE)].reshape(self.sizes.width, TILE)
            target[:, at(j, TILE)] = matmul(self.t.normed[...], block).astype(BF16)

        loop(0, self.sizes.width // TILE, body)

    def prob_copy(self, slot, pair, prob):
        return pltpu.make_async_copy(prob.at[slot], self.o.prob.at[pl.ds(2 * pair, 2)], self.t.pair_sem.at[slot])

    def attend(self, low, high, qkva, prob):
        t = self.t
        lane = lax.broadcasted_iota(I32, (1, LANES), 1)

        def body(pair):
            columns, slot = at(pair, LANES), lax.rem(pair, 2)

            @pl.when(pair >= 2)
            def _():
                self.prob_copy(slot, pair, prob).wait()

            q, k, v = (ref[:, columns] for ref in qkva[:3])
            mixed = []
            for e in range(2):
                own = jnp.where((lane < HEAD) == (e == 0), q, jnp.zeros_like(q))
                scores = times_trans(own, k) + t.big[2 * pair + e].astype(F32)
                top = jnp.max(scores, axis=-1, keepdims=True)
                powers = jnp.exp(scores - top)
                total = jnp.sum(powers, axis=-1, keepdims=True)
                weights = (powers * (1.0 / total)).astype(BF16)
                prob[slot, e] = weights
                mixed.append(matmul(weights, v))
            qkva[3][:, columns] = jnp.where(lane < HEAD, mixed[0], mixed[1]).astype(BF16)
            self.prob_copy(slot, pair, prob).start()

        loop(low, high, body)


    def feed_phase(self, held, down, hidden, hidden_far, cot_far, planes, far, sem):
        i, o, t, s = self.i, self.o, self.t, self.sizes
        group, windows = s.down_group, s.ff_windows
        copies = [
            pltpu.make_async_copy(o.full[DOWN].at[k], down.at[pl.ds(k * group, group), :], sem.at[k])
            for k in range(self.plan.wide)
        ]
        for copy in copies:
            copy.start()
        swap = self.swaps[3]
        swap.bind(self.place, hidden, o.hidden_far, t.swaps[3])
        planes_copy = pltpu.make_async_copy(o.turned[2], planes, t.pre.at[0])
        self.tick(10)
        for part, window in enumerate(windows):
            loads = [
                self.load(weight, window, held[k].at[:, :, pl.ds(0, window[1])]) for k, weight in enumerate((GATE, UP))
            ]
            loads[0].start()
            self.tick(11 + 2 * part)
            loads[1].start()
            if part == 0:
                for copy in copies:
                    copy.wait()
            if part > 0:
                self.feed_weights(part - 1, planes, far)
            for copy in loads:
                copy.wait()
            self.feed(part, held, down, hidden)
            for copy in self.ff_copies(part):
                copy.start()
            if part == 0:
                self.swaps[2].wait_recv()
                planes_copy.start()
                planes_copy.wait()
            self.tick(12 + 2 * part)
        swap.start()
        for item in self.items:
            item.finish()
        self.direct.wait()
        cot_copy = pltpu.make_async_copy(o.cot_far, cot_far, t.pre.at[1])
        cot_copy.start()
        self.feed_weights(len(windows) - 1, planes, far)
        swap.wait_recv()
        far_copy = pltpu.make_async_copy(o.hidden_far, hidden_far, t.pre.at[2])
        far_copy.start()
        cot_copy.wait()
        far_copy.wait()
        self.down_gradient(hidden, hidden_far, cot_far)
        self.advance(DOWN)
        self.advance(GATE, (0,))
        self.advance(UP, (0,))
        store = pltpu.make_async_copy(cot_far, o.result, t.pre.at[1])

        def finish(j):
            block = at(j, TILE)
            cot_far[:, block] = (t.stream[:, block] + trans_times(hidden[...], down[:, block])).astype(BF16)

        loop(0, s.width // TILE, finish)
        store.start()
        store.wait()
        swap.finish()

    def near(self, which, j):
        return which * self.sizes.blocks + lax.div(j, 2), at(lax.rem(j, 2), TILE)

    def ff_copies(self, part):
        s, t = self.sizes, self.t
        start, size = s.ff_windows[part]
        copies = []
        for which in range(2):
            for k, first in enumerate(range(start, start + size, BLOCK)):
                block, columns = first // BLOCK, pl.ds(0, min(BLOCK, start + size - first))
                copies.append(
                    to_sibling(
                        self.place,
                        t.big.at[which * s.blocks + block, :, columns],
                        self.o.far_ff.at[which, block, :, columns],
                        t.ff_sem.at[part, which, k],
                    )
                )
        return copies

    def feed(self, part, held, down, hidden):
        i, t, s = self.i, self.t, self.sizes
        start, size = s.ff_windows[part]
        first = start // TILE

        def body(j):
            tile, columns = first + j, at(j, TILE)
            gate = matmul(t.normed[...], held[0][:, :, columns].reshape(s.width, TILE))
            up = matmul(t.normed[...], held[1][:, :, columns].reshape(s.width, TILE))
            grad = times_trans(i.cotangent[...], down[at(tile, TILE), :])
            square = gate * gate
            bend = jnp.tanh(GELU_SCALE * gate * (1.0 + GELU_CUBE * square))
            half = 0.5 * (1.0 + bend)
            act = gate * half
            slope = half + (0.5 * GELU_SCALE) * gate * (1.0 - bend * bend) * (1.0 + (3.0 * GELU_CUBE) * square)
            hidden[at(tile, TILE), :] = (act * up).astype(BF16).T
            for which, value in enumerate((grad * up * slope, grad * act)):
                block, lanes = self.near(which, tile)
                t.big[block, :, lanes] = value.astype(BF16)

        loop(0, size // TILE, body)

    def feed_weights(self, part, planes, far):
        o, t, s = self.o, self.t, self.sizes
        start, size = s.ff_windows[part]
        first, rows = start // TILE, self.plan.chunks * s.group
        for copy in self.ff_copies(part):
            copy.wait_recv()

        def far_copies(slot, j):
            return [
                pltpu.make_async_copy(
                    o.far_ff.at[which, lax.div(first + j, 2), :, self.near(which, first + j)[1]],
                    far.at[slot, which],
                    t.tile_sem.at[slot, which],
                )
                for which in range(2)
            ]

        def body(j, slot):
            left = jnp.concatenate([planes[0].reshape(rows, s.rows), planes[1].reshape(rows, s.rows)], axis=1)
            for which, weight in enumerate((GATE, UP)):
                block, lanes = self.near(which, first + j)
                right = jnp.concatenate([t.big[block, :, lanes], far[slot, which]], axis=0)
                acc = self.reduces[weight][part].acc
                acc[:, :, at(j, TILE)] = matmul(left, right).astype(BF16).reshape(self.plan.chunks, s.group, TILE)

        streamed(0, size // TILE, far_copies, body)
        self.advance(GATE, (part,))
        self.advance(UP, (part,))

    def down_gradient(self, hidden, hidden_far, cot_far):
        i, s = self.i, self.sizes
        for part, (start, size) in enumerate(s.half_windows):
            acc = self.reduces[DOWN][part].acc

            def body(slot, acc=acc, start=start, size=size):
                columns = pl.ds(start, size)
                near = hidden[at(self.place[0] ^ (2 * slot), s.down_group), :]
                left = jnp.concatenate([near, hidden_far[slot]], axis=1)
                right = jnp.concatenate([i.cotangent[:, columns], cot_far[:, columns]], axis=0)
                acc[slot] = matmul(left, right).astype(BF16)

            loop(0, self.plan.chunks, body)


    def advance(self, weight, parts=None):
        for part in range(len(self.reduces[weight])) if parts is None else parts:
            item = self.reduces[weight][part]
            item.step(item.done)
            item.done += 1

    def back_phase(self, planes, qkv, back, grad_attended):
        o, t, s = self.o, self.t, self.sizes
        square = pltpu.VMEM((s.rows, s.width), BF16)
        self.swaps[0].wait_recv()
        loads = [
            pltpu.make_async_copy(source, target, t.pre.at[k])
            for k, (source, target) in enumerate(zip([o.turned[0]] + o.qkv, [planes] + qkv))
        ]
        for copy in loads:
            copy.start()
        pl.run_scoped(
            functools.partial(self.middle, back, grad_attended),
            pltpu.VMEM((self.plan.wide, s.group, s.width), BF16),
            pltpu.VMEM((2, self.plan.chunks, s.group, s.rows), BF16),
            square,
        )
        for copy in loads:
            copy.wait()
        pl.run_scoped(
            functools.partial(self.attention_back, planes, qkv, back, grad_attended),
            [square] * 3,
            pltpu.VMEM((3, s.rows, s.width // 2), BF16),
        )

    def middle(self, back, grad_attended, weight, planes, grad_mid):
        o, t, s = self.o, self.t, self.sizes
        self.swaps[1].wait_recv()
        loads = [
            pltpu.make_async_copy(o.full[OUT], weight, t.pre.at[4]),
            pltpu.make_async_copy(o.turned[1], planes, t.pre.at[5]),
        ]
        for copy in loads:
            copy.start()
        groups = TILE // s.group
        pl.run_scoped(
            functools.partial(self.feed_input, back), pltpu.VMEM((2, 2, groups, s.group, s.ff), BF16)
        )
        for part in range(len(s.ff_windows)):
            for copy in self.ff_copies(part):
                copy.wait_send()
        self.norm_back(2, back, grad_mid)
        out_copy = to_sibling(self.place, grad_mid, o.far_out, t.out_sem)
        out_copy.start()
        self.advance(GATE, (1,))
        self.advance(UP, (1,))
        for copy in loads:
            copy.wait()
        pl.run_scoped(
            functools.partial(self.out_back, out_copy, weight, planes, grad_mid, grad_attended),
            pltpu.VMEM((s.rows, s.width), BF16),
        )
        self.advance(GATE, (0,))
        self.advance(UP, (0,))
        out_copy.wait_send()

    def attention_back(self, planes, qkv, back, grad_attended, grad_qkv, far):
        i, o, t, s, plan = self.i, self.o, self.t, self.sizes, self.plan
        self.grad_qkv = grad_qkv
        prob_space = pltpu.VMEM((2, 2, s.rows, s.rows), BF16)
        half = HEADS // 4
        tokens = pltpu.make_async_copy(i.tokens, t.normed, t.pre.at[7])
        tokens.start()
        pl.run_scoped(functools.partial(self.attend_back, 0, half, qkv, grad_attended), prob_space)
        self.send_attention(0)
        self.advance(GATE, (2,))
        self.advance(UP, (2,))
        self.advance(DOWN)
        self.attention_weights(0, planes, far)
        self.advance(GATE, (0, 1))
        self.advance(UP, (0, 1))
        pl.run_scoped(functools.partial(self.attend_back, half, 2 * half, qkv, grad_attended), prob_space)
        self.send_attention(1)
        self.advance(OUT)
        self.advance(GATE, (2,))
        self.advance(UP, (2,))
        self.advance(DOWN)
        self.attention_weights(1, planes, far)
        for weight in (QUERY, KEY, VALUE):
            self.advance(weight, (0,))
        groups = TILE // s.group
        pl.run_scoped(
            functools.partial(self.attention_input, back), pltpu.VMEM((2, 3, groups, s.group, s.width), BF16)
        )
        self.advance(OUT)
        for weight in (QUERY, KEY, VALUE):
            self.advance(weight, (1,))
        tokens.wait()
        self.norm_back(1, back, None)
        store = pltpu.make_async_copy(t.stream, o.input_grad, t.pre.at[0])
        store.start()
        for weight in (QUERY, KEY, VALUE):
            self.advance(weight, (0,))
        self.table_back()
        self.sums.start(t.totals[...])
        for weight in (QUERY, KEY, VALUE):
            self.advance(weight, (1,))
        turn, last = 0, len(plan.bits) + 1
        left = [(weight, part) for weight in (GATE, UP, DOWN, OUT) for part in range(len(self.reduces[weight]))]
        left += [(weight, part) for part in range(2) for weight in (QUERY, KEY, VALUE)]
        while left:
            for weight, part in list(left):
                if self.reduces[weight][part].done > last:
                    left.remove((weight, part))
                    continue
                self.advance(weight, (part,))
                if turn % 2 == 1 and turn // 2 < len(self.sums.rounds):
                    self.sums.step(turn // 2)
                turn += 1
        for k in range(turn // 2, len(self.sums.rounds)):
            self.sums.step(k)
        store.wait()
        for part in range(2):
            for copy in self.attention_copies(part):
                copy.wait_send()
        for pair in self.reduces:
            for item in pair:
                item.finish()
        self.sums.finish()

    def feed_input(self, back, held):
        o, t, s = self.o, self.t, self.sizes
        groups = TILE // s.group
        last = s.ff - BLOCK * (s.blocks - 1)

        def weight_copies(slot, j):
            return [
                pltpu.make_async_copy(
                    o.full[weight].at[pl.ds(j * groups, groups)], held.at[slot, which], t.tile_sem.at[slot, which]
                )
                for which, weight in enumerate((GATE, UP))
            ]

        def body(j, slot):
            total = None
            for which in range(2):
                first = which * s.blocks
                near = [t.big[first + k] for k in range(s.blocks - 1)]
                near.append(t.big[first + s.blocks - 1, :, pl.ds(0, last)])
                found = times_trans(jnp.concatenate(near, axis=1), held[slot, which].reshape(TILE, s.ff))
                total = found if total is None else total + found
            back[:, at(j, TILE)] = total

        streamed(0, s.width // TILE, weight_copies, body)

    def norm_back(self, which, back, grad_mid):
        i, t, s = self.i, self.t, self.sizes

        def body(j):
            block = at(j, 64)
            kept = t.keep[block, :] > 0.5
            grad = back[block, :]
            if which == 2:
                x = t.stream[block, :]
                before = i.cotangent[block, :].astype(F32)
            else:
                x = jnp.where(kept, t.normed[block, :].astype(F32), t.rows[0:1, :])
                before = t.stream[block, :]
            scale = lax.rsqrt(jnp.mean(x * x, axis=-1, keepdims=True) + EPSILON)
            scaled = x * scale
            u = grad * t.rows[which : which + 1, :]
            inner = jnp.mean(u * scaled, axis=-1, keepdims=True)
            total = before + scale * (u - scaled * inner)
            t.totals[which : which + 1, :] += jnp.sum(grad * scaled, axis=0, keepdims=True)
            if which == 2:
                t.stream[block, :] = total
                grad_mid[block, :] = total.astype(BF16)
            else:
                t.stream[block, :] = jnp.where(kept, total, 0.0)
                t.totals[0:1, :] += jnp.sum(jnp.where(kept, 0.0, total), axis=0, keepdims=True)

        loop(0, s.rows // 64, body)

    def out_back(self, out_copy, weight, planes, grad_mid, grad_attended, far):
        o, t, s = self.o, self.t, self.sizes
        groups = TILE // s.group

        def attended(j):
            block = weight[pl.ds(j * groups, groups)].reshape(TILE, s.width)
            grad_attended[:, at(j, TILE)] = times_trans(grad_mid[...], block).astype(BF16)

        loop(0, s.width // TILE, attended)
        out_copy.wait_recv()
        load = pltpu.make_async_copy(o.far_out, far, t.pre.at[6])
        load.start()
        load.wait()
        rows = self.plan.chunks * s.group
        for part, (start, size) in enumerate(s.half_windows):
            columns = pl.ds(start, size)
            left = jnp.concatenate([planes[0].reshape(rows, s.rows), planes[1].reshape(rows, s.rows)], axis=1)
            right = jnp.concatenate([grad_mid[:, columns], far[:, columns]], axis=0)
            acc = self.reduces[OUT][part].acc
            acc[...] = matmul(left, right).astype(BF16).reshape(acc.shape)
            self.advance(OUT, (part,))

    def attend_back(self, low, high, qkv, grad_attended, prob):
        o, t = self.o, self.t
        lane = lax.broadcasted_iota(I32, (1, LANES), 1)

        def prob_copies(slot, pair):
            return [pltpu.make_async_copy(o.prob.at[pl.ds(2 * pair, 2)], prob.at[slot], t.tile_sem.at[slot, 0])]

        def body(pair, slot):
            columns = at(pair, LANES)
            q, k, v = (ref[:, columns] for ref in qkv)
            grad = grad_attended[:, columns]
            found = [[], [], []]
            for e in range(2):
                own = jnp.where((lane < HEAD) == (e == 0), grad, jnp.zeros_like(grad))
                weights = prob[slot, e]
                wide = weights.astype(F32)
                grad_prob = times_trans(own, v)
                delta = jnp.sum(grad_prob * wide, axis=-1, keepdims=True)
                scores = (wide * (grad_prob - delta)).astype(BF16)
                t.big[2 * pair + e] = scores
                found[0].append(matmul(scores, k))
                found[1].append(trans_times(scores, q))
                found[2].append(trans_times(weights, grad))
            for ref, (first, second) in zip(self.grad_qkv, found):
                ref[:, columns] = jnp.where(lane < HEAD, first, second).astype(BF16)

        streamed(low, high, prob_copies, body)

    def attention_copies(self, part):
        window = pl.ds(*self.sizes.half_windows[part])
        return [
            to_sibling(
                self.place,
                self.grad_qkv[which].at[:, window],
                self.o.far_attn[which].at[:, window],
                self.t.attn_sem.at[part, which],
            )
            for which in range(3)
        ]

    def send_attention(self, part):
        for copy in self.attention_copies(part):
            copy.start()

    def attention_weights(self, part, planes, far):
        o, t, s = self.o, self.t, self.sizes
        columns = pl.ds(*s.half_windows[part])
        rows = self.plan.chunks * s.group
        loads = []
        for which, copy in enumerate(self.attention_copies(part)):
            copy.wait_recv()
            loads.append(pltpu.make_async_copy(o.far_attn[which].at[:, columns], far.at[which], t.pre.at[which]))
            loads[-1].start()
        for which in range(3):
            loads[which].wait()
            left = jnp.concatenate([planes[0].reshape(rows, s.rows), planes[1].reshape(rows, s.rows)], axis=1)
            right = jnp.concatenate([self.grad_qkv[which][:, columns], far[which]], axis=0)
            acc = self.reduces[which][part].acc
            acc[...] = matmul(left, right).astype(BF16).reshape(acc.shape)
            self.advance(which, (part,))

    def attention_input(self, back, held):
        o, t, s = self.o, self.t, self.sizes
        groups = TILE // s.group

        def weight_copies(slot, j):
            return [
                pltpu.make_async_copy(
                    o.full[which].at[pl.ds(j * groups, groups)], held.at[slot, which], t.tile_sem.at[slot, which]
                )
                for which in range(3)
            ]

        def body(j, slot):
            back[:, at(j, TILE)] = sum(
                times_trans(self.grad_qkv[which][...], held[slot, which].reshape(TILE, s.width)) for which in range(3)
            )

        streamed(0, s.width // TILE, weight_copies, body)

    def table_back(self):
        i, t, s = self.i, self.t, self.sizes
        width, step = BUCKETS * HEADS, 4

        def count(total, buckets):
            copy = pltpu.make_async_copy(i.buckets, buckets, t.pre.at[7])
            copy.start()
            total[...] = jnp.zeros_like(total)
            copy.wait()

            def body(j):
                left, right = [], []
                for k in range(step):
                    block = at(j * step + k, 16)
                    left.append(bucket_rows(buckets[block, :]))
                    right.append(t.big[:, block, :].reshape(HEADS * 16, s.rows))
                total[...] += times_trans(jnp.concatenate(left, axis=1), jnp.concatenate(right, axis=1))

            loop(0, s.rows // (16 * step), body)
            found = total[...].T
            row = lax.broadcasted_iota(I32, found.shape, 0)
            lane = lax.broadcasted_iota(I32, found.shape, 1)
            found = jnp.where(row % 16 == lane % 16, found, 0.0)
            by_head = jnp.sum(found.reshape(HEADS, 16, width), axis=1)
            summed = jnp.dot(
                by_head, same_bucket(width), precision=lax.Precision.HIGHEST, preferred_element_type=F32
            )
            head = lax.broadcasted_iota(I32, summed.shape, 0)
            lane = lax.broadcasted_iota(I32, summed.shape, 1)
            t.totals[3:4, :width] = jnp.sum(jnp.where(lane % HEADS == head, summed, 0.0), axis=0, keepdims=True)

        pl.run_scoped(count, pltpu.VMEM((width, HEADS * 16), F32), pltpu.VMEM((s.rows, s.rows), I32))


def hand_out(plan, large, sums, counts):
    def kernel(i, o, t):
        takes = [pltpu.make_async_copy(*pair, t.take.at[k]) for k, pair in enumerate(zip(i.large, t.held))]
        gives = [pltpu.make_async_copy(*pair, t.give.at[k]) for k, pair in enumerate(zip(t.held, o.large))]
        for copy in takes:
            copy.start()
        device = lax.axis_index("wide") * plan.narrow + lax.axis_index("narrow")
        width = i.sums.shape[1]
        source = lax.broadcasted_iota(I32, (width, LANES), 0)
        lane = lax.broadcasted_iota(I32, (width, LANES), 1)
        for row, (size, target) in enumerate(zip(counts, o.owned)):
            pick = (source == device * size + lane).astype(F32)
            found = jnp.dot(
                i.sums[...], pick, precision=lax.Precision.HIGHEST, preferred_element_type=F32
            )
            target[...] = found[row : row + 1, :size]
        for take, give in zip(takes, gives):
            take.wait()
            give.start()
        for copy in gives:
            copy.wait()

    done = run(
        kernel,
        dict(large=large, sums=sums),
        dict(large=[struct(x.shape, x.dtype) for x in large], owned=[struct((1, size), F32) for size in counts]),
        dict(take=sems(len(large)), give=sems(len(large)), held=[pltpu.VMEM(x.shape, x.dtype) for x in large]),
        {"sums", "owned"},
        set(),
        None,
        "hand_out",
    )
    return done.large, done.owned


def per_device(
    plan,
    tokens,
    patch_keep,
    text_len,
    buckets,
    mask_embed,
    norm_attn,
    w_query,
    w_key,
    w_value,
    w_out,
    bias_table,
    norm_ffn,
    w_gate,
    w_up,
    w_down,
    cotangent,
):
    rows, width = tokens.shape
    assert patch_keep.shape[0] == 1
    device = lax.axis_index("wide") * plan.narrow + lax.axis_index("narrow")
    small = (mask_embed, norm_attn, norm_ffn, bias_table)
    counts = [member.shape[0] for member in small]
    starts = [sum(counts[:k]) for k in range(len(counts))]
    vectors = sum(
        jnp.pad(member.reshape(1, -1), ((0, 0), (start, LANES - start - member.shape[0])))
        for start, member in zip(starts, small)
    )
    weights = (w_query, w_key, w_value, w_out, w_gate, w_up, w_down)
    shards = [jnp.pad(weight, ((0, -weight.shape[0] % 16), (0, 0))) for weight in weights[:DOWN]] + [w_down]
    sizes = Sizes(plan, rows, width, w_gate.shape[1], [weight.shape[0] for weight in weights])
    f = Layer(plan, sizes).call(vectors, counts, shards, tokens, patch_keep, text_len, buckets, cotangent)

    large = [f.result, f.input_grad] + f.grads
    (result, input_grad, query, key, value, out, gate, up, down), owned = hand_out(plan, large, f.sums, counts)
    embed, gain_one, gain_two, table = (part.reshape(-1) for part in owned)
    return (
        result,
        input_grad,
        embed,
        gain_one,
        query,
        key,
        value,
        out,
        table,
        gain_two,
        gate,
        up,
        down,
    )


def solution(mesh):
    rows, flat = P(("wide", "narrow"), None), P(("wide", "narrow"))
    plan = Plan(mesh.shape["wide"], mesh.shape["narrow"])
    return jax.shard_map(
        functools.partial(per_device, plan),
        mesh=mesh,
        in_specs=(rows, rows, flat, rows, flat, flat, rows, rows, rows, rows, flat, flat, rows, rows, rows, rows),
        out_specs=(rows, rows, flat, flat, rows, rows, rows, rows, flat, flat, rows, rows, rows),
        check_vma=False,
    )
```

```python
import functools
import types

import jax
import jax.numpy as jnp
from jax import lax
from jax.experimental import pallas as pl
from jax.experimental.pallas import tpu as pltpu
from jax.sharding import PartitionSpec as P

MESH = pl.DeviceIdType.MESH
VMEM_LIMIT = 62 << 20
HEADS = 16
HEAD = 64
BUCKETS = 32
EPSILON = 1e-06
NEG_FILL = -1000000000.0
LANES = 128
TILE = 256
CONTRACT_LAST = (((1,), (1,)), ((), ()))
CONTRACT_FIRST = (((0,), (0,)), ((), ()))
BF16, F32, I32 = jnp.bfloat16, jnp.float32, jnp.int32
GELU_SCALE = 0.7978845608028654
GELU_CUBE = 0.044715


def round_up(value, unit):
    return -(-value // unit) * unit


def matmul(left, right):
    return jnp.dot(left, right, preferred_element_type=F32)


def times_trans(left, right):
    return lax.dot_general(left, right, CONTRACT_LAST, preferred_element_type=F32)


def trans_times(left, right):
    return lax.dot_general(left, right, CONTRACT_FIRST, preferred_element_type=F32)


class Plan:
    def __init__(self, wide, narrow):
        self.wide, self.narrow = wide, narrow
        self.bits = [2 << i for i in range(wide.bit_length() - 2)]
        self.chunks = wide // 2
        assert wide == 2 << len(self.bits)


def span(bits):
    out = [0]
    for bit in bits:
        out = out + [member ^ bit for member in out]
    return out


def halves(start, size):
    half = round_up(size // 2, LANES)
    return [(start, half), (start + half, size - half)] if size > 2 * LANES else [(start, size)]


def enter(plan):
    w, n = lax.axis_index("wide"), lax.axis_index("narrow")
    barrier = pltpu.get_barrier_semaphore()
    partners = [(w ^ bit, n) for bit in [1] + plan.bits]
    partners += [(w, lax.rem(n + d, plan.narrow)) for d in range(1, plan.narrow)]
    for partner in partners:
        pl.semaphore_signal(barrier, inc=1, device_id=partner, device_id_type=MESH)
    pl.semaphore_wait(barrier, len(partners))
    return w, n


def loop(low, high, body):
    def step(i, carry):
        body(i)
        return carry

    lax.fori_loop(low, high, step, 0)


def at(index, size):
    return pl.ds(pl.multiple_of(index * size, size), size)


def streamed(low, high, copies, body, first=None, last=None):
    first, last = low if first is None else first, high if last is None else last
    if low == first:
        for copy in copies(lax.rem(low, 2), low):
            copy.start()

    def step(i):
        slot = lax.rem(i, 2)

        @pl.when(i + 1 < last)
        def _():
            for copy in copies(1 - slot, i + 1):
                copy.start()

        for copy in copies(slot, i):
            copy.wait()
        body(i, slot)

    loop(low, high, step)


def run(kernel, inputs, outputs, scratch, resident, scalars, collective_id, name):
    sizes = [len(jax.tree.leaves(tree)) for tree in (inputs, outputs, scratch)]
    forms = [jax.tree.structure(tree) for tree in (inputs, outputs, scratch)]

    def flat(*refs):
        first, second = sizes[0], sizes[0] + sizes[1]
        parts = (refs[:first], refs[first:second], refs[second:])
        kernel(*(types.SimpleNamespace(**form.unflatten(part)) for form, part in zip(forms, parts)))

    def space(key):
        return pltpu.VMEM if key in resident else pltpu.SMEM if key in scalars else pl.ANY

    def specs(tree):
        return jax.tree.leaves(
            {
                key: jax.tree.map(lambda _, key=key: pl.BlockSpec(memory_space=space(key)), value)
                for key, value in tree.items()
            }
        )

    result = pl.pallas_call(
        flat,
        out_shape=jax.tree.leaves(outputs),
        in_specs=specs(inputs),
        out_specs=specs(outputs),
        scratch_shapes=jax.tree.leaves(scratch),
        compiler_params=pltpu.CompilerParams(
            collective_id=collective_id, has_side_effects=collective_id is not None, vmem_limit_bytes=VMEM_LIMIT
        ),
        name=name,
    )(*jax.tree.leaves(inputs))
    return types.SimpleNamespace(**forms[1].unflatten(result))


def sems(*shape):
    return pltpu.SemaphoreType.DMA(shape)


def struct(shape, dtype):
    return jax.ShapeDtypeStruct(shape, dtype)


class Gather:
    def __init__(self, plan, rows, window):
        self.plan, self.rows = plan, rows
        self.start_column, self.columns = window
        self.padded = round_up(self.rows, 16)
        self.aligned = self.padded == self.rows
        self.group = plan.narrow * self.rows
        self.parts = halves(*window)
        self.orders = [plan.bits, plan.bits[::-1]][: len(self.parts)]
        self.chunks = plan.chunks

    def reserve(self):
        count, parts = self.plan.narrow, len(self.parts)
        return [sems(2, count), sems(2, parts, self.chunks), sems(2, parts, self.chunks), sems(2)]

    def stages_out(self):
        return [] if self.aligned else [struct((self.plan.narrow, self.padded, self.columns), BF16)]

    def bind(self, place, shard, out, stage, refs):
        self.w, self.n = place
        self.shard, self.out = shard, out
        self.zsem, self.bsem, self.csem, self.lsem = refs
        if not self.aligned:
            self.stage = stage[0]

    def window(self):
        return pl.ds(self.start_column, self.columns)

    def own_slot(self):
        if self.aligned:
            rows = pl.ds(pl.multiple_of(self.n * self.rows, self.rows), self.rows)
            return self.out.at[self.w, rows, self.window()]
        return self.stage.at[self.n]

    def z_copy(self, d):
        return pltpu.make_async_remote_copy(
            src_ref=self.shard.at[:, self.window()],
            dst_ref=self.own_slot(),
            send_sem=self.zsem.at[0, d],
            recv_sem=self.zsem.at[1, d],
            device_id=(self.w, lax.rem(self.n + d, self.plan.narrow)),
            device_id_type=MESH,
        )

    def place_copy(self):
        return pltpu.make_async_copy(self.shard.at[:, self.window()], self.own_slot(), self.lsem.at[0])

    def pack_group(self, stage, compact):
        copy = pltpu.make_async_copy(self.stage, stage, self.lsem.at[1])
        copy.start()
        copy.wait()
        size, wide = self.group, self.plan.narrow * self.padded
        row = lax.broadcasted_iota(I32, (size, wide), 0)
        column = lax.broadcasted_iota(I32, (size, wide), 1)
        pick = column == (row // self.rows) * self.padded + row % self.rows
        compact[...] = matmul(pick.astype(F32).astype(BF16), stage[...].reshape(wide, self.columns)).astype(BF16)
        copy = pltpu.make_async_copy(compact, self.out.at[self.w, :, self.window()], self.lsem.at[1])
        copy.start()
        copy.wait()

    def start(self):
        for d in range(1, self.plan.narrow):
            self.z_copy(d).start()
        self.place_copy().start()

    def hop(self, sems, part, mask, bit, slot):
        start, size = self.parts[part]
        target = self.out.at[self.w ^ mask, :, pl.ds(start, size)]
        return pltpu.make_async_remote_copy(
            src_ref=target,
            dst_ref=target,
            send_sem=sems.at[0, part, slot],
            recv_sem=sems.at[1, part, slot],
            device_id=(self.w ^ bit, self.n),
            device_id_type=MESH,
        )

    def hops(self, part, stage):
        order = self.orders[part]
        masks = span(order[:stage])
        return [self.hop(self.bsem, part, mask, order[stage], len(masks) + i - 1) for i, mask in enumerate(masks)]

    def core_hops(self, part, stage):
        masks = span(self.orders[part])
        low, high = (0, 1) if stage == 0 else (1 << (stage - 1), 1 << stage)
        return [self.hop(self.csem, part, masks[i], 1, i) for i in range(low, high)]

    def stages(self):
        return len(self.plan.bits) + 2

    def step(self, stage):
        bits, parts = len(self.plan.bits), range(len(self.parts))
        if stage == 0:
            for d in range(1, self.plan.narrow):
                self.z_copy(d).wait_recv()
            self.place_copy().wait()
            if not self.aligned:
                pl.run_scoped(
                    self.pack_group,
                    pltpu.VMEM((self.plan.narrow, self.padded, self.columns), BF16),
                    pltpu.VMEM((self.group, self.columns), BF16),
                )
        elif stage <= bits:
            for part in parts:
                for copy in self.hops(part, stage - 1):
                    copy.wait_recv()
        else:
            for part in parts:
                for s in range(bits + 1):
                    for copy in self.core_hops(part, s):
                        copy.wait_recv()
        if stage < bits:
            for part in parts:
                for copy in self.hops(part, stage):
                    copy.start()
        if stage <= bits:
            for part in parts:
                for copy in self.core_hops(part, stage):
                    copy.start()

    def finish(self):
        for d in range(1, self.plan.narrow):
            self.z_copy(d).wait_send()
        for part in range(len(self.parts)):
            for s in range(len(self.plan.bits)):
                for copy in self.hops(part, s):
                    copy.wait_send()
            for s in range(len(self.plan.bits) + 1):
                for copy in self.core_hops(part, s):
                    copy.wait_send()


class Swap:
    def __init__(self, plan):
        self.plan = plan

    def reserve(self):
        return sems(3, self.plan.chunks)

    def bind(self, place, source, out, sem):
        self.w, self.n = place
        self.source, self.out, self.sem = source, out, sem
        self.both = len(out.shape) == 4
        self.group = source.shape[0] // self.plan.wide

    def chunk(self, index):
        return self.source.at[pl.ds(pl.multiple_of(index * self.group, self.group), self.group), :]

    def local(self, slot):
        return pltpu.make_async_copy(self.chunk(self.w ^ (2 * slot)), self.out.at[0, slot], self.sem.at[2, slot])

    def landing(self, slot):
        return self.out.at[1, slot] if self.both else self.out.at[slot]

    def remote(self, slot, source):
        return pltpu.make_async_remote_copy(
            src_ref=source,
            dst_ref=self.landing(slot),
            send_sem=self.sem.at[0, slot],
            recv_sem=self.sem.at[1, slot],
            device_id=(self.w ^ 1, self.n),
            device_id_type=MESH,
        )

    def send(self, slot):
        return self.remote(slot, self.chunk(self.w ^ 1 ^ (2 * slot)))

    def start(self):
        for slot in range(self.plan.chunks):
            self.send(slot).start()
            if self.both:
                self.local(slot).start()

    def wait_recv(self):
        for slot in range(self.plan.chunks):
            self.remote(slot, self.landing(slot)).wait_recv()

    def finish(self):
        for slot in range(self.plan.chunks):
            self.send(slot).wait_send()
            if self.both:
                self.local(slot).wait()


def to_sibling(place, source, target, sem):
    return pltpu.make_async_remote_copy(
        src_ref=source,
        dst_ref=target,
        send_sem=sem.at[0],
        recv_sem=sem.at[1],
        device_id=(place[0] ^ 1, place[1]),
        device_id_type=MESH,
    )


def column_of(row):
    eye = lax.broadcasted_iota(I32, (LANES, LANES), 0) == lax.broadcasted_iota(I32, (LANES, LANES), 1)
    pieces = [
        jnp.sum(jnp.where(eye, row[:, start : start + LANES], 0.0), axis=1, keepdims=True)
        for start in range(0, row.shape[1], LANES)
    ]
    return jnp.concatenate(pieces, axis=0)


def unpack_small(plan, packed, sizes):
    summed = jnp.sum(packed.astype(F32).reshape(plan.wide, plan.narrow, 16, LANES), axis=1)
    rows = []
    for i, size in enumerate(sizes):
        each = LANES // (size * plan.narrow)
        blocks = [
            sum(summed[first + j, i : i + 1, :] for j in range(each))
            for first in range(0, plan.wide, each)
        ]
        rows.append(jnp.concatenate(blocks, axis=1))
    return rows


def same_bucket(width):
    row = lax.broadcasted_iota(I32, (width, width), 0) // HEADS
    column = lax.broadcasted_iota(I32, (width, width), 1) // HEADS
    return (row == column).astype(F32)


def spread_table(table_row):
    width = BUCKETS * HEADS
    lane = lax.broadcasted_iota(I32, (HEADS, width), 1)
    head = lax.broadcasted_iota(I32, (HEADS, width), 0)
    same = lane % HEADS == head
    picked = jnp.where(same, table_row, 0.0).astype(BF16)
    spread = matmul(picked, same_bucket(width).astype(BF16))
    return jnp.concatenate(
        [jnp.where(same, spread[h : h + 1, :], 0.0).astype(BF16) for h in range(HEADS)], axis=0
    )


def bucket_rows(bucket):
    small = bucket.astype(F32).astype(BF16)
    one, zero = jnp.ones_like(small), jnp.zeros_like(small)
    return jnp.concatenate(
        [jnp.where(small == jnp.asarray(j, BF16), one, zero) for j in range(BUCKETS)], axis=0
    )


class Reduce:
    def __init__(self, plan, rows, window, order):
        self.plan, self.rows = plan, rows
        self.start_column, self.columns = window
        self.padded = round_up(rows, 16)
        self.aligned = self.padded == rows
        self.group = plan.narrow * rows
        self.order = order
        self.chunks = plan.chunks

    def reserve(self):
        count, columns = self.plan.narrow, self.columns
        shapes = [
            sems(2, self.chunks),
            sems(2, count),
            pltpu.VMEM((self.chunks, self.group, columns), BF16),
            pltpu.VMEM((self.chunks - 1, self.group, columns), BF16),
            pltpu.VMEM((count - 1, self.padded, columns), BF16),
        ]
        if not self.aligned:
            shapes.append(pltpu.VMEM((count, self.padded, columns), BF16))
        return shapes

    def bind(self, place, out, refs):
        self.w, self.n = place
        self.out, self.done = out, 0
        self.bsem, self.zsem, self.acc, self.received, self.zreceived = refs[:5]
        if not self.aligned:
            self.stage = refs[5]

    def hops(self, stage):
        bit, masks = self.order[stage], span(self.order[stage + 1 :])
        base = self.chunks - 2 * len(masks)
        return [
            (
                mask >> 1,
                base + k,
                pltpu.make_async_remote_copy(
                    src_ref=self.acc.at[(bit ^ mask) >> 1],
                    dst_ref=self.received.at[base + k],
                    send_sem=self.bsem.at[0, base + k],
                    recv_sem=self.bsem.at[1, base + k],
                    device_id=(self.w ^ bit, self.n),
                    device_id_type=MESH,
                ),
            )
            for k, mask in enumerate(masks)
        ]

    def z_copy(self, d):
        peer = lax.rem(self.n + d, self.plan.narrow)
        source = self.acc.at[0, at(peer, self.rows), :] if self.aligned else self.stage.at[peer]
        return pltpu.make_async_remote_copy(
            src_ref=source,
            dst_ref=self.zreceived.at[d - 1],
            send_sem=self.zsem.at[0, d],
            recv_sem=self.zsem.at[1, d],
            device_id=(self.w, peer),
            device_id_type=MESH,
        )

    def step(self, stage):
        bits = len(self.order)
        if 1 <= stage <= bits:
            for slot, k, copy in self.hops(stage - 1):
                copy.wait_recv()

                def body(j, slot=slot, k=k):
                    block = at(j, 16)
                    self.acc[slot, block, :] += self.received[k, block, :]

                loop(0, self.group // 16, body)
        if stage < bits:
            for _, _, copy in self.hops(stage):
                copy.start()
        elif stage == bits:
            if not self.aligned:
                size, wide = self.group, self.plan.narrow * self.padded
                row = lax.broadcasted_iota(I32, (wide, size), 0)
                column = lax.broadcasted_iota(I32, (wide, size), 1)
                pick = row == (column // self.rows) * self.padded + column % self.rows
                self.stage[...] = (
                    matmul(pick.astype(F32).astype(BF16), self.acc[0]).astype(BF16).reshape(self.stage.shape)
                )
            for d in range(1, self.plan.narrow):
                self.z_copy(d).start()
        else:
            total = self.acc[0, at(self.n, self.rows), :] if self.aligned else self.stage[self.n]
            total = total.astype(F32)
            for d in range(1, self.plan.narrow):
                self.z_copy(d).wait_recv()
                total = total + self.zreceived[d - 1].astype(F32)
            self.out[:, pl.ds(self.start_column, self.columns)] = total[: self.rows]

    def finish(self):
        for stage in range(len(self.order)):
            for _, _, copy in self.hops(stage):
                copy.wait_send()
        for d in range(1, self.plan.narrow):
            self.z_copy(d).wait_send()


class SumAll:
    def __init__(self, plan, shape):
        self.shape = shape
        self.rounds = [(bit, 0) for bit in [1] + plan.bits]
        self.rounds += [(0, 1 << k) for k in range(plan.narrow.bit_length() - 1)]

    def reserve(self):
        count = len(self.rounds)
        return [sems(2, count)] + [pltpu.VMEM((count, *self.shape), F32)] * 2

    def bind(self, place, out, refs):
        self.w, self.n = place
        self.out = out
        self.sem, self.held, self.received = refs

    def copy(self, turn):
        bit, other = self.rounds[turn]
        return pltpu.make_async_remote_copy(
            src_ref=self.held.at[turn],
            dst_ref=self.received.at[turn],
            send_sem=self.sem.at[0, turn],
            recv_sem=self.sem.at[1, turn],
            device_id=(self.w ^ bit, self.n ^ other),
            device_id_type=MESH,
        )

    def start(self, value):
        self.held[0] = value
        self.copy(0).start()

    def step(self, turn):
        self.copy(turn).wait_recv()
        total = self.held[turn] + self.received[turn]
        if turn + 1 < len(self.rounds):
            self.held[turn + 1] = total
            self.copy(turn + 1).start()
        else:
            self.out[...] = total

    def finish(self):
        for turn in range(len(self.rounds)):
            self.copy(turn).wait_send()


class Sizes:
    def __init__(self, plan, rows, width, ff, shards):
        self.plan, self.rows, self.width, self.ff = plan, rows, width, ff
        self.shards = shards
        self.group = plan.narrow * shards[0]
        self.down_group = plan.narrow * shards[DOWN]
        step = round_up(ff // 3, BLOCK)
        self.ff_windows = [(start, min(step, ff - start)) for start in range(0, ff, step)]
        self.half_windows = [(0, width // 2), (width // 2, width // 2)]
        self.blocks = round_up(ff, BLOCK) // BLOCK

    def full(self):
        wide = self.plan.wide
        return (
            [(wide, self.group, self.width)] * 4
            + [(wide, self.group, self.ff)] * 2
            + [(wide, self.down_group, self.width)]
        )


QUERY, KEY, VALUE, OUT, GATE, UP, DOWN = range(7)
BLOCK = 512


class Layer:
    def __init__(self, plan, sizes):
        self.plan, self.sizes = plan, sizes
        whole = (0, sizes.width)
        wide = [(weight, window) for window in sizes.ff_windows for weight in (GATE, UP)]
        down = [(DOWN, window) for window in sizes.half_windows]
        self.order = [(weight, whole) for weight in (QUERY, KEY, VALUE, OUT)] + down + wide
        self.small = Gather(plan, 16, (0, LANES))
        self.items = [self.small] + [Gather(plan, sizes.shards[weight], window) for weight, window in self.order]
        self.swaps = [Swap(plan) for _ in range(4)]
        self.extra = self.small.stages() - 4
        ways = [plan.bits, plan.bits[::-1]]
        self.reduces = []
        for weight in range(7):
            turn = 1 if weight in (UP, KEY, OUT) else 0
            pairs = enumerate(sizes.half_windows)
            if weight in (GATE, UP):
                pairs = [(0, window) for window in sizes.ff_windows]
            self.reduces.append([Reduce(plan, sizes.shards[weight], window, ways[k ^ turn]) for k, window in pairs])
        self.sums = SumAll(plan, (8, sizes.width))

    def call(self, vectors, counts, shards, tokens, patch_keep, text_len, buckets, cotangent):
        plan, s = self.plan, self.sizes
        self.counts = counts
        rows, width, chunks = s.rows, s.width, plan.chunks
        row_block = struct((rows, width), BF16)
        inputs = dict(
            vectors=vectors,
            shards=shards[:DOWN],
            down_shard=shards[DOWN],
            tokens=tokens,
            patch_keep=patch_keep,
            text_len=text_len,
            buckets=buckets,
            cotangent=cotangent,
        )
        outputs = dict(
            small=struct((plan.wide, plan.narrow * 16, LANES), BF16),
            full=[struct(shape, BF16) for shape in s.full()],
            stages=[item.stages_out() for item in self.items],
            qkv=[row_block] * 3,
            prob=struct((HEADS, rows, rows), BF16),
            turned=[struct((2, chunks, s.group, rows), BF16)] * 3,
            hidden_far=struct((chunks, s.down_group, rows), BF16),
            cot_far=row_block,
            far_ff=struct((2, s.blocks, rows, BLOCK), BF16),
            far_out=row_block,
            far_attn=[row_block] * 3,
            result=row_block,
            input_grad=struct((rows, width), F32),
            grads=[
                struct((size, s.ff if weight in (GATE, UP) else width), F32) for weight, size in enumerate(s.shards)
            ],
            sums=struct((8, width), F32),
        )
        square = pltpu.VMEM((rows, width), BF16)
        down_rows = round_up(s.shards[DOWN], 16)
        scratch = dict(
            items=[item.reserve() for item in self.items],
            swaps=[swap.reserve() for swap in self.swaps],
            reduces=[[item.reserve() for item in pair] for pair in self.reduces],
            exchange=self.sums.reserve(),
            direct=sems(2),
            load=sems(len(self.items)),
            pre=sems(8),
            packed=pltpu.VMEM((16, LANES), BF16),
            small=pltpu.VMEM((plan.wide, plan.narrow * 16, LANES), BF16),
            down_shard=pltpu.VMEM((down_rows, width), BF16),
            rows=pltpu.VMEM((8, width), F32),
            keep=pltpu.VMEM((rows, 1), F32),
            big=pltpu.VMEM((HEADS, rows, rows), BF16),
            stream=pltpu.VMEM((rows, width), F32),
            normed=square,
            totals=pltpu.VMEM((8, width), F32),
            pair_sem=sems(2),
            tile_sem=sems(2, 3),
            ff_sem=sems(len(s.ff_windows), 2, 2, 2),
            out_sem=sems(2),
            attn_sem=sems(2, 3, 2),
            store=sems(6),
        )
        return run(
            self.kernel,
            inputs,
            outputs,
            scratch,
            {"vectors", "down_shard", "patch_keep", "cotangent", "grads", "sums"},
            {"text_len"},
            0,
            "layer",
        )

    def kernel(self, i, o, t):
        self.i, self.o, self.t = i, o, t
        plan, s = self.plan, self.sizes
        square = pltpu.VMEM((s.rows, s.width), BF16)
        planes = pltpu.VMEM((2, plan.chunks, s.group, s.rows), BF16)
        weight_space = pltpu.VMEM((plan.wide, s.group, s.width), BF16)
        self.pack()
        self.place = place = enter(plan)
        self.small.bind(place, t.packed, o.small, o.stages[0], t.items[0])
        for item, (weight, _), stage, refs in zip(self.items[1:], self.order, o.stages[1:], t.items[1:]):
            item.bind(place, t.down_shard if weight == DOWN else i.shards[weight], o.full[weight], stage, refs)
        for pair, out, refs in zip(self.reduces, o.grads, t.reduces):
            for item, own in zip(pair, refs):
                item.bind(place, out, own)
        self.sums.bind(place, o.sums, t.exchange)
        self.direct = to_sibling(place, i.cotangent, o.cot_far, t.direct)

        for item in self.items[:2]:
            item.start()
        self.direct.start()
        for turn in range(-self.extra, 4):
            self.tick(turn)
        self.set_up()
        pl.run_scoped(
            self.attention_phase,
            [weight_space] * 3,
            [square] * 4,
            [pltpu.VMEM((s.width, s.rows), BF16)] * 2,
            pltpu.VMEM((2, 2, s.rows, s.rows), BF16),
            pltpu.VMEM((HEADS * 16, BUCKETS * 16), BF16),
            pltpu.VMEM((s.rows, s.rows), I32),
        )
        pl.run_scoped(
            self.feed_phase,
            [pltpu.VMEM((plan.wide, s.group, s.ff_windows[0][1]), BF16)] * 2,
            pltpu.VMEM((s.ff, s.width), BF16),
            pltpu.VMEM((s.ff, s.rows), BF16),
            pltpu.VMEM((plan.chunks, s.down_group, s.rows), BF16),
            square,
            planes,
            pltpu.VMEM((2, 2, s.rows, TILE), BF16),
            sems(plan.wide),
        )
        pl.run_scoped(
            self.back_phase,
            planes,
            [square] * 3,
            pltpu.VMEM((s.rows, s.width), F32),
            square,
        )


    def tick(self, turn):
        stages, turn = self.small.stages(), turn + self.extra
        for stage in range(stages):
            k = turn - stage
            if 0 <= k < len(self.items):
                self.items[k].step(stage)
        if turn + 2 < len(self.items):
            self.items[turn + 2].start()

    def load(self, weight, window, target):
        k = 1 + self.order.index((weight, window))
        return pltpu.make_async_copy(self.o.full[weight].at[:, :, pl.ds(*window)], target, self.t.load.at[k])

    def pack(self):
        i, t = self.i, self.t
        device = lax.axis_index("wide") * self.plan.narrow + lax.axis_index("narrow")
        source = lax.broadcasted_iota(I32, (LANES, LANES), 0)
        lane = lax.broadcasted_iota(I32, (LANES, LANES), 1)
        row = lax.broadcasted_iota(I32, (16, LANES), 0)
        packed, offset = jnp.zeros((16, LANES), F32), 0
        for k, size in enumerate(self.counts):
            first = lax.rem(device * size, LANES)
            pick = (source == offset + lane - first) & (lane >= first) & (lane < first + size)
            found = matmul(i.vectors[...], pick.astype(F32).astype(BF16))
            packed = jnp.where(row == k, found, packed)
            offset += size
        t.packed[...] = packed.astype(BF16)
        size = i.down_shard.shape[0]
        t.down_shard[...] = jnp.concatenate(
            [i.down_shard[...], jnp.zeros((t.down_shard.shape[0] - size, self.sizes.width), BF16)], axis=0
        )

    def set_up(self):
        i, o, t = self.i, self.o, self.t
        copy = pltpu.make_async_copy(o.small, t.small, t.load.at[0])
        copy.start()
        tokens = pltpu.make_async_copy(i.tokens, t.normed, t.pre.at[7])
        tokens.start()
        patches, rows = i.patch_keep.shape[1], self.sizes.rows
        row = lax.broadcasted_iota(I32, (rows, patches), 0)
        lane = lax.broadcasted_iota(I32, (rows, patches), 1)
        kept = jnp.sum(jnp.where(row == lane, i.patch_keep[...].astype(F32), 0.0), axis=1, keepdims=True)
        t.keep[...] = jnp.where(lax.broadcasted_iota(I32, (rows, 1), 0) >= patches, 1.0, kept)
        t.totals[...] = jnp.zeros_like(t.totals)
        copy.wait()
        embed, gain_one, gain_two, table = unpack_small(self.plan, t.small[...], self.counts)
        t.rows[...] = jnp.concatenate([embed, gain_one, gain_two, jnp.zeros((5, self.sizes.width), F32)], axis=0)
        self.table_row = table
        tokens.wait()

        def body(j):
            block = at(j, 64)
            t.stream[block, :] = jnp.where(
                t.keep[block, :] > 0.5, t.normed[block, :].astype(F32), t.rows[0:1, :]
            )

        loop(0, rows // 64, body)
        self.norm(1)

    def norm(self, gain):
        t = self.t

        def body(j):
            block = at(j, 64)
            x = t.stream[block, :]
            scale = lax.rsqrt(jnp.mean(x * x, axis=-1, keepdims=True) + EPSILON)
            t.normed[block, :] = (x * scale * t.rows[gain : gain + 1, :]).astype(BF16)

        loop(0, self.sizes.rows // 64, body)

    def turn(self, source, target):
        def body(j):
            target[at(j, LANES), :] = source[:, at(j, LANES)].T

        loop(0, self.sizes.width // LANES, body)


    def attention_phase(self, held, qkva, turned, prob, table, buckets):
        o, t, s = self.o, self.t, self.sizes
        bucket_copy = pltpu.make_async_copy(self.i.buckets, buckets, t.pre.at[7])
        bucket_copy.start()
        normed, attended, second, _ = self.swaps
        for swap, source, target, sem in zip(
            self.swaps, (turned[0], turned[1], turned[0]), o.turned, t.swaps
        ):
            swap.bind(self.place, source, target, sem)
        store = [pltpu.make_async_copy(qkva[k], o.qkv[k], t.store.at[k]) for k in range(3)]
        whole = (0, s.width)
        loads = [self.load(weight, whole, held[weight % 3]) for weight in (QUERY, KEY, VALUE, OUT)]
        self.turn(t.normed, turned[0])
        normed.start()
        table[...] = spread_table(self.table_row)
        self.tick(4)
        loads[QUERY].start()
        blocks = s.rows // 16
        bucket_copy.wait()
        self.bias(0, blocks // 2, table, buckets)
        self.tick(5)
        loads[KEY].start()
        loads[QUERY].wait()
        self.project(held[0], qkva[0])
        store[0].start()
        self.bias(blocks // 2, blocks, table, buckets)
        self.tick(6)
        loads[VALUE].start()
        loads[KEY].wait()
        self.project(held[1], qkva[1])
        store[1].start()
        self.tick(7)
        loads[OUT].start()
        loads[VALUE].wait()
        self.project(held[2], qkva[2])
        store[2].start()
        count = HEADS // 2
        self.attend(0, 3 * count // 8, qkva, prob)
        self.tick(8)
        self.attend(3 * count // 8, 6 * count // 8, qkva, prob)
        self.tick(9)
        self.attend(6 * count // 8, count, qkva, prob)
        for slot in range(2):
            self.prob_copy(slot, count - 2 + slot, prob).wait()
        loads[OUT].wait()

        def body(j):
            block = held[0][:, :, at(j, TILE)].reshape(s.width, TILE)
            t.stream[:, at(j, TILE)] += matmul(qkva[3][...], block)

        loop(0, s.width // TILE, body)
        self.tick(10)
        self.turn(qkva[3], turned[1])
        attended.start()
        normed.finish()
        self.norm(2)
        self.turn(t.normed, turned[0])
        second.start()
        for copy in store:
            copy.wait()
        attended.finish()
        second.finish()

    def bias(self, low, high, table, buckets):
        i, t = self.i, self.t
        live = lax.broadcasted_iota(I32, (1, self.sizes.rows), 1) < i.patch_keep.shape[1] + i.text_len[0]

        def body(j):
            block = at(j, 16)
            spread = matmul(table[...], bucket_rows(buckets[block, :]))
            spread = jnp.where(live, spread, NEG_FILL).astype(BF16)
            t.big[:, block, :] = spread.reshape(HEADS, 16, spread.shape[-1])

        loop(low, high, body)

    def project(self, weight, target):
        def body(j):
            block = weight[:, :, at(j, TILE)].reshape(self.sizes.width, TILE)
            target[:, at(j, TILE)] = matmul(self.t.normed[...], block).astype(BF16)

        loop(0, self.sizes.width // TILE, body)

    def prob_copy(self, slot, pair, prob):
        return pltpu.make_async_copy(prob.at[slot], self.o.prob.at[pl.ds(2 * pair, 2)], self.t.pair_sem.at[slot])

    def attend(self, low, high, qkva, prob):
        t = self.t
        lane = lax.broadcasted_iota(I32, (1, LANES), 1)

        def body(pair):
            columns, slot = at(pair, LANES), lax.rem(pair, 2)

            @pl.when(pair >= 2)
            def _():
                self.prob_copy(slot, pair, prob).wait()

            q, k, v = (ref[:, columns] for ref in qkva[:3])
            mixed = []
            for e in range(2):
                own = jnp.where((lane < HEAD) == (e == 0), q, jnp.zeros_like(q))
                scores = times_trans(own, k) + t.big[2 * pair + e].astype(F32)
                top = jnp.max(scores, axis=-1, keepdims=True)
                powers = jnp.exp(scores - top)
                total = jnp.sum(powers, axis=-1, keepdims=True)
                weights = (powers * (1.0 / total)).astype(BF16)
                prob[slot, e] = weights
                mixed.append(matmul(weights, v))
            qkva[3][:, columns] = jnp.where(lane < HEAD, mixed[0], mixed[1]).astype(BF16)
            self.prob_copy(slot, pair, prob).start()

        loop(low, high, body)


    def feed_phase(self, held, down, hidden, hidden_far, cot_far, planes, far, sem):
        i, o, t, s = self.i, self.o, self.t, self.sizes
        group, windows = s.down_group, s.ff_windows
        copies = [
            pltpu.make_async_copy(o.full[DOWN].at[k], down.at[pl.ds(k * group, group), :], sem.at[k])
            for k in range(self.plan.wide)
        ]
        for copy in copies:
            copy.start()
        swap = self.swaps[3]
        swap.bind(self.place, hidden, o.hidden_far, t.swaps[3])
        planes_copy = pltpu.make_async_copy(o.turned[2], planes, t.pre.at[0])
        for part, window in enumerate(windows):
            loads = [
                self.load(weight, window, held[k].at[:, :, pl.ds(0, window[1])]) for k, weight in enumerate((GATE, UP))
            ]
            loads[0].start()
            self.tick(11 + 2 * part)
            loads[1].start()
            if part == 0:
                for copy in copies:
                    copy.wait()
            if part > 0:
                self.feed_weights(part - 1, planes, far)
            for copy in loads:
                copy.wait()
            self.feed(part, held, down, hidden)
            for copy in self.ff_copies(part):
                copy.start()
            if part == 0:
                self.swaps[2].wait_recv()
                planes_copy.start()
                planes_copy.wait()
            self.tick(12 + 2 * part)
        swap.start()
        for item in self.items:
            item.finish()
        self.direct.wait()
        cot_copy = pltpu.make_async_copy(o.cot_far, cot_far, t.pre.at[1])
        cot_copy.start()
        self.feed_weights(len(windows) - 1, planes, far)
        swap.wait_recv()
        far_copy = pltpu.make_async_copy(o.hidden_far, hidden_far, t.pre.at[2])
        far_copy.start()
        cot_copy.wait()
        far_copy.wait()
        self.down_gradient(hidden, hidden_far, cot_far)
        self.advance(DOWN)
        self.advance(GATE, (0,))
        self.advance(UP, (0,))
        store = pltpu.make_async_copy(cot_far, o.result, t.pre.at[1])

        def finish(j):
            block = at(j, TILE)
            cot_far[:, block] = (t.stream[:, block] + trans_times(hidden[...], down[:, block])).astype(BF16)

        loop(0, s.width // TILE, finish)
        store.start()
        store.wait()
        swap.finish()

    def near(self, which, j):
        return which * self.sizes.blocks + lax.div(j, 2), at(lax.rem(j, 2), TILE)

    def ff_copies(self, part):
        s, t = self.sizes, self.t
        start, size = s.ff_windows[part]
        copies = []
        for which in range(2):
            for k, first in enumerate(range(start, start + size, BLOCK)):
                block, columns = first // BLOCK, pl.ds(0, min(BLOCK, start + size - first))
                copies.append(
                    to_sibling(
                        self.place,
                        t.big.at[which * s.blocks + block, :, columns],
                        self.o.far_ff.at[which, block, :, columns],
                        t.ff_sem.at[part, which, k],
                    )
                )
        return copies

    def feed(self, part, held, down, hidden):
        i, t, s = self.i, self.t, self.sizes
        start, size = s.ff_windows[part]
        first = start // TILE

        def body(j):
            tile, columns = first + j, at(j, TILE)
            gate = matmul(t.normed[...], held[0][:, :, columns].reshape(s.width, TILE))
            up = matmul(t.normed[...], held[1][:, :, columns].reshape(s.width, TILE))
            grad = times_trans(i.cotangent[...], down[at(tile, TILE), :])
            square = gate * gate
            bend = jnp.tanh(GELU_SCALE * gate * (1.0 + GELU_CUBE * square))
            half = 0.5 * (1.0 + bend)
            act = gate * half
            slope = half + (0.5 * GELU_SCALE) * gate * (1.0 - bend * bend) * (1.0 + (3.0 * GELU_CUBE) * square)
            hidden[at(tile, TILE), :] = (act * up).astype(BF16).T
            for which, value in enumerate((grad * up * slope, grad * act)):
                block, lanes = self.near(which, tile)
                t.big[block, :, lanes] = value.astype(BF16)

        loop(0, size // TILE, body)

    def feed_weights(self, part, planes, far):
        o, t, s = self.o, self.t, self.sizes
        start, size = s.ff_windows[part]
        first, rows = start // TILE, self.plan.chunks * s.group
        for copy in self.ff_copies(part):
            copy.wait_recv()

        def far_copies(slot, j):
            return [
                pltpu.make_async_copy(
                    o.far_ff.at[which, lax.div(first + j, 2), :, self.near(which, first + j)[1]],
                    far.at[slot, which],
                    t.tile_sem.at[slot, which],
                )
                for which in range(2)
            ]

        def body(j, slot):
            left = jnp.concatenate([planes[0].reshape(rows, s.rows), planes[1].reshape(rows, s.rows)], axis=1)
            for which, weight in enumerate((GATE, UP)):
                block, lanes = self.near(which, first + j)
                right = jnp.concatenate([t.big[block, :, lanes], far[slot, which]], axis=0)
                acc = self.reduces[weight][part].acc
                acc[:, :, at(j, TILE)] = matmul(left, right).astype(BF16).reshape(self.plan.chunks, s.group, TILE)

        streamed(0, size // TILE, far_copies, body)
        self.advance(GATE, (part,))
        self.advance(UP, (part,))

    def down_gradient(self, hidden, hidden_far, cot_far):
        i, s = self.i, self.sizes
        for part, (start, size) in enumerate(s.half_windows):
            acc = self.reduces[DOWN][part].acc

            def body(slot, acc=acc, start=start, size=size):
                columns = pl.ds(start, size)
                near = hidden[at(self.place[0] ^ (2 * slot), s.down_group), :]
                left = jnp.concatenate([near, hidden_far[slot]], axis=1)
                right = jnp.concatenate([i.cotangent[:, columns], cot_far[:, columns]], axis=0)
                acc[slot] = matmul(left, right).astype(BF16)

            loop(0, self.plan.chunks, body)


    def advance(self, weight, parts=None):
        for part in range(len(self.reduces[weight])) if parts is None else parts:
            item = self.reduces[weight][part]
            item.step(item.done)
            item.done += 1

    def back_phase(self, planes, qkv, back, grad_attended):
        o, t, s = self.o, self.t, self.sizes
        square = pltpu.VMEM((s.rows, s.width), BF16)
        self.swaps[0].wait_recv()
        loads = [
            pltpu.make_async_copy(source, target, t.pre.at[k])
            for k, (source, target) in enumerate(zip([o.turned[0]] + o.qkv, [planes] + qkv))
        ]
        pl.run_scoped(
            functools.partial(self.middle, loads, back, grad_attended),
            pltpu.VMEM((self.plan.wide, s.group, s.width), BF16),
            pltpu.VMEM((2, self.plan.chunks, s.group, s.rows), BF16),
            square,
        )
        for copy in loads:
            copy.wait()
        pl.run_scoped(
            functools.partial(self.attention_back, planes, qkv, back, grad_attended),
            [square] * 3,
            pltpu.VMEM((3, s.rows, s.width // 2), BF16),
        )

    def middle(self, later, back, grad_attended, weight, planes, grad_mid):
        o, t, s = self.o, self.t, self.sizes
        self.swaps[1].wait_recv()
        loads = [
            pltpu.make_async_copy(o.full[OUT], weight, t.pre.at[4]),
            pltpu.make_async_copy(o.turned[1], planes, t.pre.at[5]),
        ]
        groups = TILE // s.group
        pl.run_scoped(
            functools.partial(self.feed_input, loads + later, back), pltpu.VMEM((2, 2, groups, s.group, s.ff), BF16)
        )
        for part in range(len(s.ff_windows)):
            for copy in self.ff_copies(part):
                copy.wait_send()
        self.norm_back(2, back, grad_mid)
        out_copy = to_sibling(self.place, grad_mid, o.far_out, t.out_sem)
        out_copy.start()
        self.advance(GATE, (1,))
        self.advance(UP, (1,))
        for copy in loads:
            copy.wait()
        pl.run_scoped(
            functools.partial(self.out_back, out_copy, weight, planes, grad_mid, grad_attended),
            pltpu.VMEM((s.rows, s.width), BF16),
        )
        self.advance(GATE, (0,))
        self.advance(UP, (0,))
        out_copy.wait_send()

    def attention_back(self, planes, qkv, back, grad_attended, grad_qkv, far):
        i, o, t, s, plan = self.i, self.o, self.t, self.sizes, self.plan
        self.grad_qkv = grad_qkv
        prob_space = pltpu.VMEM((2, 2, s.rows, s.rows), BF16)
        half = HEADS // 4
        tokens = pltpu.make_async_copy(i.tokens, t.normed, t.pre.at[7])
        tokens.start()
        pl.run_scoped(functools.partial(self.attend_back, 0, half, qkv, grad_attended), prob_space)
        self.send_attention(0)
        self.advance(GATE, (2,))
        self.advance(UP, (2,))
        self.advance(DOWN)
        self.attention_weights(0, planes, far)
        self.advance(GATE, (0, 1))
        self.advance(UP, (0, 1))
        pl.run_scoped(functools.partial(self.attend_back, half, 2 * half, qkv, grad_attended), prob_space)
        self.send_attention(1)
        self.advance(OUT)
        self.advance(GATE, (2,))
        self.advance(UP, (2,))
        self.advance(DOWN)
        self.attention_weights(1, planes, far)
        for weight in (QUERY, KEY, VALUE):
            self.advance(weight, (0,))
        groups = TILE // s.group
        pl.run_scoped(
            functools.partial(self.attention_input, back), pltpu.VMEM((2, 3, groups, s.group, s.width), BF16)
        )
        self.advance(OUT)
        for weight in (QUERY, KEY, VALUE):
            self.advance(weight, (1,))
        tokens.wait()
        self.norm_back(1, back, None)
        store = pltpu.make_async_copy(t.stream, o.input_grad, t.pre.at[0])
        store.start()
        for weight in (QUERY, KEY, VALUE):
            self.advance(weight, (0,))
        self.table_back()
        self.sums.start(t.totals[...])
        for weight in (QUERY, KEY, VALUE):
            self.advance(weight, (1,))
        turn, last = 0, len(plan.bits) + 1
        left = [(weight, part) for weight in (GATE, UP, DOWN, OUT) for part in range(len(self.reduces[weight]))]
        left += [(weight, part) for part in range(2) for weight in (QUERY, KEY, VALUE)]
        while left:
            for weight, part in list(left):
                if self.reduces[weight][part].done > last:
                    left.remove((weight, part))
                    continue
                self.advance(weight, (part,))
                if turn % 2 == 1 and turn // 2 < len(self.sums.rounds):
                    self.sums.step(turn // 2)
                turn += 1
        for k in range(turn // 2, len(self.sums.rounds)):
            self.sums.step(k)
        store.wait()
        for part in range(2):
            for copy in self.attention_copies(part):
                copy.wait_send()
        for pair in self.reduces:
            for item in pair:
                item.finish()
        self.sums.finish()

    def feed_input(self, loads, back, held):
        o, t, s = self.o, self.t, self.sizes
        groups = TILE // s.group
        last = s.ff - BLOCK * (s.blocks - 1)

        def weight_copies(slot, j):
            return [
                pltpu.make_async_copy(
                    o.full[weight].at[pl.ds(j * groups, groups)], held.at[slot, which], t.tile_sem.at[slot, which]
                )
                for which, weight in enumerate((GATE, UP))
            ]

        def body(j, slot):
            total = None
            for which in range(2):
                first = which * s.blocks
                near = [t.big[first + k] for k in range(s.blocks - 1)]
                near.append(t.big[first + s.blocks - 1, :, pl.ds(0, last)])
                found = times_trans(jnp.concatenate(near, axis=1), held[slot, which].reshape(TILE, s.ff))
                total = found if total is None else total + found
            back[:, at(j, TILE)] = total

        for copy in weight_copies(0, 0) + loads:
            copy.start()
        streamed(0, s.width // TILE, weight_copies, body, first=-1)

    def norm_back(self, which, back, grad_mid):
        i, t, s = self.i, self.t, self.sizes

        def body(j):
            block = at(j, 64)
            kept = t.keep[block, :] > 0.5
            grad = back[block, :]
            if which == 2:
                x = t.stream[block, :]
                before = i.cotangent[block, :].astype(F32)
            else:
                x = jnp.where(kept, t.normed[block, :].astype(F32), t.rows[0:1, :])
                before = t.stream[block, :]
            scale = lax.rsqrt(jnp.mean(x * x, axis=-1, keepdims=True) + EPSILON)
            scaled = x * scale
            u = grad * t.rows[which : which + 1, :]
            inner = jnp.mean(u * scaled, axis=-1, keepdims=True)
            total = before + scale * (u - scaled * inner)
            t.totals[which : which + 1, :] += jnp.sum(grad * scaled, axis=0, keepdims=True)
            if which == 2:
                t.stream[block, :] = total
                grad_mid[block, :] = total.astype(BF16)
            else:
                t.stream[block, :] = jnp.where(kept, total, 0.0)
                t.totals[0:1, :] += jnp.sum(jnp.where(kept, 0.0, total), axis=0, keepdims=True)

        loop(0, s.rows // 64, body)

    def out_back(self, out_copy, weight, planes, grad_mid, grad_attended, far):
        o, t, s = self.o, self.t, self.sizes
        groups = TILE // s.group

        def attended(j):
            block = weight[pl.ds(j * groups, groups)].reshape(TILE, s.width)
            grad_attended[:, at(j, TILE)] = times_trans(grad_mid[...], block).astype(BF16)

        loop(0, s.width // TILE, attended)
        out_copy.wait_recv()
        load = pltpu.make_async_copy(o.far_out, far, t.pre.at[6])
        load.start()
        load.wait()
        rows = self.plan.chunks * s.group
        for part, (start, size) in enumerate(s.half_windows):
            columns = pl.ds(start, size)
            left = jnp.concatenate([planes[0].reshape(rows, s.rows), planes[1].reshape(rows, s.rows)], axis=1)
            right = jnp.concatenate([grad_mid[:, columns], far[:, columns]], axis=0)
            acc = self.reduces[OUT][part].acc
            acc[...] = matmul(left, right).astype(BF16).reshape(acc.shape)
            self.advance(OUT, (part,))

    def attend_back(self, low, high, qkv, grad_attended, prob):
        o, t = self.o, self.t
        lane = lax.broadcasted_iota(I32, (1, LANES), 1)

        def prob_copies(slot, pair):
            return [pltpu.make_async_copy(o.prob.at[pl.ds(2 * pair, 2)], prob.at[slot], t.tile_sem.at[slot, 0])]

        def body(pair, slot):
            columns = at(pair, LANES)
            q, k, v = (ref[:, columns] for ref in qkv)
            grad = grad_attended[:, columns]
            found = [[], [], []]
            for e in range(2):
                own = jnp.where((lane < HEAD) == (e == 0), grad, jnp.zeros_like(grad))
                weights = prob[slot, e]
                wide = weights.astype(F32)
                grad_prob = times_trans(own, v)
                delta = jnp.sum(grad_prob * wide, axis=-1, keepdims=True)
                scores = (wide * (grad_prob - delta)).astype(BF16)
                t.big[2 * pair + e] = scores
                found[0].append(matmul(scores, k))
                found[1].append(trans_times(scores, q))
                found[2].append(trans_times(weights, grad))
            for ref, (first, second) in zip(self.grad_qkv, found):
                ref[:, columns] = jnp.where(lane < HEAD, first, second).astype(BF16)

        streamed(low, high, prob_copies, body)

    def attention_copies(self, part):
        window = pl.ds(*self.sizes.half_windows[part])
        return [
            to_sibling(
                self.place,
                self.grad_qkv[which].at[:, window],
                self.o.far_attn[which].at[:, window],
                self.t.attn_sem.at[part, which],
            )
            for which in range(3)
        ]

    def send_attention(self, part):
        for copy in self.attention_copies(part):
            copy.start()

    def attention_weights(self, part, planes, far):
        o, t, s = self.o, self.t, self.sizes
        columns = pl.ds(*s.half_windows[part])
        rows = self.plan.chunks * s.group
        loads = []
        for which, copy in enumerate(self.attention_copies(part)):
            copy.wait_recv()
            loads.append(pltpu.make_async_copy(o.far_attn[which].at[:, columns], far.at[which], t.pre.at[which]))
            loads[-1].start()
        for which in range(3):
            loads[which].wait()
            left = jnp.concatenate([planes[0].reshape(rows, s.rows), planes[1].reshape(rows, s.rows)], axis=1)
            right = jnp.concatenate([self.grad_qkv[which][:, columns], far[which]], axis=0)
            acc = self.reduces[which][part].acc
            acc[...] = matmul(left, right).astype(BF16).reshape(acc.shape)
            self.advance(which, (part,))

    def attention_input(self, back, held):
        o, t, s = self.o, self.t, self.sizes
        groups = TILE // s.group

        def weight_copies(slot, j):
            return [
                pltpu.make_async_copy(
                    o.full[which].at[pl.ds(j * groups, groups)], held.at[slot, which], t.tile_sem.at[slot, which]
                )
                for which in range(3)
            ]

        def body(j, slot):
            back[:, at(j, TILE)] = sum(
                times_trans(self.grad_qkv[which][...], held[slot, which].reshape(TILE, s.width)) for which in range(3)
            )

        streamed(0, s.width // TILE, weight_copies, body)

    def table_back(self):
        i, t, s = self.i, self.t, self.sizes
        width, step = BUCKETS * HEADS, 4

        def count(total, buckets):
            copy = pltpu.make_async_copy(i.buckets, buckets, t.pre.at[7])
            copy.start()
            total[...] = jnp.zeros_like(total)
            copy.wait()

            def body(j):
                left, right = [], []
                for k in range(step):
                    block = at(j * step + k, 16)
                    left.append(bucket_rows(buckets[block, :]))
                    right.append(t.big[:, block, :].reshape(HEADS * 16, s.rows))
                total[...] += times_trans(jnp.concatenate(left, axis=1), jnp.concatenate(right, axis=1))

            loop(0, s.rows // (16 * step), body)
            found = total[...].T
            row = lax.broadcasted_iota(I32, found.shape, 0)
            lane = lax.broadcasted_iota(I32, found.shape, 1)
            found = jnp.where(row % 16 == lane % 16, found, 0.0)
            by_head = jnp.sum(found.reshape(HEADS, 16, width), axis=1)
            summed = jnp.dot(
                by_head, same_bucket(width), precision=lax.Precision.HIGHEST, preferred_element_type=F32
            )
            head = lax.broadcasted_iota(I32, summed.shape, 0)
            lane = lax.broadcasted_iota(I32, summed.shape, 1)
            t.totals[3:4, :width] = jnp.sum(jnp.where(lane % HEADS == head, summed, 0.0), axis=0, keepdims=True)

        pl.run_scoped(count, pltpu.VMEM((width, HEADS * 16), F32), pltpu.VMEM((s.rows, s.rows), I32))


def hand_out(plan, large, sums, counts):
    def kernel(i, o, t):
        takes = [pltpu.make_async_copy(*pair, t.take.at[k]) for k, pair in enumerate(zip(i.large, t.held))]
        gives = [pltpu.make_async_copy(*pair, t.give.at[k]) for k, pair in enumerate(zip(t.held, o.large))]
        for copy in takes:
            copy.start()
        device = lax.axis_index("wide") * plan.narrow + lax.axis_index("narrow")
        width = i.sums.shape[1]
        source = lax.broadcasted_iota(I32, (width, LANES), 0)
        lane = lax.broadcasted_iota(I32, (width, LANES), 1)
        for row, (size, target) in enumerate(zip(counts, o.owned)):
            pick = (source == device * size + lane).astype(F32)
            found = jnp.dot(
                i.sums[...], pick, precision=lax.Precision.HIGHEST, preferred_element_type=F32
            )
            target[...] = found[row : row + 1, :size]
        for take, give in zip(takes, gives):
            take.wait()
            give.start()
        for copy in gives:
            copy.wait()

    done = run(
        kernel,
        dict(large=large, sums=sums),
        dict(large=[struct(x.shape, x.dtype) for x in large], owned=[struct((1, size), F32) for size in counts]),
        dict(take=sems(len(large)), give=sems(len(large)), held=[pltpu.VMEM(x.shape, x.dtype) for x in large]),
        {"sums", "owned"},
        set(),
        None,
        "hand_out",
    )
    return done.large, done.owned


def per_device(
    plan,
    tokens,
    patch_keep,
    text_len,
    buckets,
    mask_embed,
    norm_attn,
    w_query,
    w_key,
    w_value,
    w_out,
    bias_table,
    norm_ffn,
    w_gate,
    w_up,
    w_down,
    cotangent,
):
    rows, width = tokens.shape
    assert patch_keep.shape[0] == 1
    device = lax.axis_index("wide") * plan.narrow + lax.axis_index("narrow")
    small = (mask_embed, norm_attn, norm_ffn, bias_table)
    counts = [member.shape[0] for member in small]
    starts = [sum(counts[:k]) for k in range(len(counts))]
    vectors = sum(
        jnp.pad(member.reshape(1, -1), ((0, 0), (start, LANES - start - member.shape[0])))
        for start, member in zip(starts, small)
    )
    weights = (w_query, w_key, w_value, w_out, w_gate, w_up, w_down)
    shards = [jnp.pad(weight, ((0, -weight.shape[0] % 16), (0, 0))) for weight in weights[:DOWN]] + [w_down]
    sizes = Sizes(plan, rows, width, w_gate.shape[1], [weight.shape[0] for weight in weights])
    f = Layer(plan, sizes).call(vectors, counts, shards, tokens, patch_keep, text_len, buckets, cotangent)

    large = [f.result, f.input_grad] + f.grads
    (result, input_grad, query, key, value, out, gate, up, down), owned = hand_out(plan, large, f.sums, counts)
    embed, gain_one, gain_two, table = (part.reshape(-1) for part in owned)
    return (
        result,
        input_grad,
        embed,
        gain_one,
        query,
        key,
        value,
        out,
        table,
        gain_two,
        gate,
        up,
        down,
    )


def solution(mesh):
    rows, flat = P(("wide", "narrow"), None), P(("wide", "narrow"))
    plan = Plan(mesh.shape["wide"], mesh.shape["narrow"])
    return jax.shard_map(
        functools.partial(per_device, plan),
        mesh=mesh,
        in_specs=(rows, rows, flat, rows, flat, flat, rows, rows, rows, rows, flat, flat, rows, rows, rows, rows),
        out_specs=(rows, rows, flat, flat, rows, rows, rows, rows, flat, flat, rows, rows, rows),
        check_vma=False,
    )
```

```python
import functools
import types

import jax
import jax.numpy as jnp
from jax import lax
from jax.experimental import pallas as pl
from jax.experimental.pallas import tpu as pltpu
from jax.sharding import PartitionSpec as P

MESH = pl.DeviceIdType.MESH
VMEM_LIMIT = 62 << 20
HEADS = 16
HEAD = 64
BUCKETS = 32
EPSILON = 1e-06
NEG_FILL = -1000000000.0
LANES = 128
TILE = 256
CONTRACT_LAST = (((1,), (1,)), ((), ()))
CONTRACT_FIRST = (((0,), (0,)), ((), ()))
BF16, F32, I32 = jnp.bfloat16, jnp.float32, jnp.int32
GELU_SCALE = 0.7978845608028654
GELU_CUBE = 0.044715


def round_up(value, unit):
    return -(-value // unit) * unit


def matmul(left, right):
    return jnp.dot(left, right, preferred_element_type=F32)


def times_trans(left, right):
    return lax.dot_general(left, right, CONTRACT_LAST, preferred_element_type=F32)


def trans_times(left, right):
    return lax.dot_general(left, right, CONTRACT_FIRST, preferred_element_type=F32)


class Plan:
    def __init__(self, wide, narrow):
        self.wide, self.narrow = wide, narrow
        self.bits = [2 << i for i in range(wide.bit_length() - 2)]
        self.chunks = wide // 2
        assert wide == 2 << len(self.bits)


def span(bits):
    out = [0]
    for bit in bits:
        out = out + [member ^ bit for member in out]
    return out


def halves(start, size):
    half = round_up(size // 2, LANES)
    return [(start, half), (start + half, size - half)] if size > 2 * LANES else [(start, size)]


def enter(plan):
    w, n = lax.axis_index("wide"), lax.axis_index("narrow")
    barrier = pltpu.get_barrier_semaphore()
    partners = [(w ^ bit, n) for bit in [1] + plan.bits]
    partners += [(w, lax.rem(n + d, plan.narrow)) for d in range(1, plan.narrow)]
    for partner in partners:
        pl.semaphore_signal(barrier, inc=1, device_id=partner, device_id_type=MESH)
    pl.semaphore_wait(barrier, len(partners))
    return w, n


def loop(low, high, body):
    def step(i, carry):
        body(i)
        return carry

    lax.fori_loop(low, high, step, 0)


def at(index, size):
    return pl.ds(pl.multiple_of(index * size, size), size)


def streamed(low, high, copies, body, first=None, last=None):
    first, last = low if first is None else first, high if last is None else last
    if low == first:
        for copy in copies(lax.rem(low, 2), low):
            copy.start()

    def step(i):
        slot = lax.rem(i, 2)

        @pl.when(i + 1 < last)
        def _():
            for copy in copies(1 - slot, i + 1):
                copy.start()

        for copy in copies(slot, i):
            copy.wait()
        body(i, slot)

    loop(low, high, step)


def run(kernel, inputs, outputs, scratch, resident, scalars, collective_id, name):
    sizes = [len(jax.tree.leaves(tree)) for tree in (inputs, outputs, scratch)]
    forms = [jax.tree.structure(tree) for tree in (inputs, outputs, scratch)]

    def flat(*refs):
        first, second = sizes[0], sizes[0] + sizes[1]
        parts = (refs[:first], refs[first:second], refs[second:])
        kernel(*(types.SimpleNamespace(**form.unflatten(part)) for form, part in zip(forms, parts)))

    def space(key):
        return pltpu.VMEM if key in resident else pltpu.SMEM if key in scalars else pl.ANY

    def specs(tree):
        return jax.tree.leaves(
            {
                key: jax.tree.map(lambda _, key=key: pl.BlockSpec(memory_space=space(key)), value)
                for key, value in tree.items()
            }
        )

    result = pl.pallas_call(
        flat,
        out_shape=jax.tree.leaves(outputs),
        in_specs=specs(inputs),
        out_specs=specs(outputs),
        scratch_shapes=jax.tree.leaves(scratch),
        compiler_params=pltpu.CompilerParams(
            collective_id=collective_id, has_side_effects=collective_id is not None, vmem_limit_bytes=VMEM_LIMIT
        ),
        name=name,
    )(*jax.tree.leaves(inputs))
    return types.SimpleNamespace(**forms[1].unflatten(result))


def sems(*shape):
    return pltpu.SemaphoreType.DMA(shape)


def struct(shape, dtype):
    return jax.ShapeDtypeStruct(shape, dtype)


class Gather:
    def __init__(self, plan, rows, window):
        self.plan, self.rows = plan, rows
        self.start_column, self.columns = window
        self.padded = round_up(self.rows, 16)
        self.aligned = self.padded == self.rows
        self.group = plan.narrow * self.rows
        self.parts = halves(*window)
        self.orders = [plan.bits, plan.bits[::-1]][: len(self.parts)]
        self.chunks = plan.chunks

    def reserve(self):
        count, parts = self.plan.narrow, len(self.parts)
        return [sems(2, count), sems(2, parts, self.chunks), sems(2, parts, self.chunks), sems(2)]

    def stages_out(self):
        return [] if self.aligned else [struct((self.plan.narrow, self.padded, self.columns), BF16)]

    def bind(self, place, shard, out, stage, refs):
        self.w, self.n = place
        self.shard, self.out = shard, out
        self.zsem, self.bsem, self.csem, self.lsem = refs
        if not self.aligned:
            self.stage = stage[0]

    def window(self):
        return pl.ds(self.start_column, self.columns)

    def own_slot(self):
        if self.aligned:
            rows = pl.ds(pl.multiple_of(self.n * self.rows, self.rows), self.rows)
            return self.out.at[self.w, rows, self.window()]
        return self.stage.at[self.n]

    def z_copy(self, d):
        return pltpu.make_async_remote_copy(
            src_ref=self.shard.at[:, self.window()],
            dst_ref=self.own_slot(),
            send_sem=self.zsem.at[0, d],
            recv_sem=self.zsem.at[1, d],
            device_id=(self.w, lax.rem(self.n + d, self.plan.narrow)),
            device_id_type=MESH,
        )

    def place_copy(self):
        return pltpu.make_async_copy(self.shard.at[:, self.window()], self.own_slot(), self.lsem.at[0])

    def pack_group(self, stage, compact):
        copy = pltpu.make_async_copy(self.stage, stage, self.lsem.at[1])
        copy.start()
        copy.wait()
        size, wide = self.group, self.plan.narrow * self.padded
        row = lax.broadcasted_iota(I32, (size, wide), 0)
        column = lax.broadcasted_iota(I32, (size, wide), 1)
        pick = column == (row // self.rows) * self.padded + row % self.rows
        compact[...] = matmul(pick.astype(F32).astype(BF16), stage[...].reshape(wide, self.columns)).astype(BF16)
        copy = pltpu.make_async_copy(compact, self.out.at[self.w, :, self.window()], self.lsem.at[1])
        copy.start()
        copy.wait()

    def start(self):
        for d in range(1, self.plan.narrow):
            self.z_copy(d).start()
        self.place_copy().start()

    def hop(self, sems, part, mask, bit, slot):
        start, size = self.parts[part]
        target = self.out.at[self.w ^ mask, :, pl.ds(start, size)]
        return pltpu.make_async_remote_copy(
            src_ref=target,
            dst_ref=target,
            send_sem=sems.at[0, part, slot],
            recv_sem=sems.at[1, part, slot],
            device_id=(self.w ^ bit, self.n),
            device_id_type=MESH,
        )

    def hops(self, part, stage):
        order = self.orders[part]
        masks = span(order[:stage])
        return [self.hop(self.bsem, part, mask, order[stage], len(masks) + i - 1) for i, mask in enumerate(masks)]

    def core_hops(self, part, stage):
        masks = span(self.orders[part])
        low, high = (0, 1) if stage == 0 else (1 << (stage - 1), 1 << stage)
        return [self.hop(self.csem, part, masks[i], 1, i) for i in range(low, high)]

    def stages(self):
        return len(self.plan.bits) + 2

    def step(self, stage):
        bits, parts = len(self.plan.bits), range(len(self.parts))
        if stage == 0:
            for d in range(1, self.plan.narrow):
                self.z_copy(d).wait_recv()
            self.place_copy().wait()
            if not self.aligned:
                pl.run_scoped(
                    self.pack_group,
                    pltpu.VMEM((self.plan.narrow, self.padded, self.columns), BF16),
                    pltpu.VMEM((self.group, self.columns), BF16),
                )
        elif stage <= bits:
            for part in parts:
                for copy in self.hops(part, stage - 1):
                    copy.wait_recv()
        else:
            for part in parts:
                for s in range(bits + 1):
                    for copy in self.core_hops(part, s):
                        copy.wait_recv()
        if stage < bits:
            for part in parts:
                for copy in self.hops(part, stage):
                    copy.start()
        if stage <= bits:
            for part in parts:
                for copy in self.core_hops(part, stage):
                    copy.start()

    def finish(self):
        for d in range(1, self.plan.narrow):
            self.z_copy(d).wait_send()
        for part in range(len(self.parts)):
            for s in range(len(self.plan.bits)):
                for copy in self.hops(part, s):
                    copy.wait_send()
            for s in range(len(self.plan.bits) + 1):
                for copy in self.core_hops(part, s):
                    copy.wait_send()


class Swap:
    def __init__(self, plan):
        self.plan = plan

    def reserve(self):
        return sems(3, self.plan.chunks)

    def bind(self, place, source, out, sem):
        self.w, self.n = place
        self.source, self.out, self.sem = source, out, sem
        self.both = len(out.shape) == 4
        self.group = source.shape[0] // self.plan.wide

    def chunk(self, index):
        return self.source.at[pl.ds(pl.multiple_of(index * self.group, self.group), self.group), :]

    def local(self, slot):
        return pltpu.make_async_copy(self.chunk(self.w ^ (2 * slot)), self.out.at[0, slot], self.sem.at[2, slot])

    def landing(self, slot):
        return self.out.at[1, slot] if self.both else self.out.at[slot]

    def remote(self, slot, source):
        return pltpu.make_async_remote_copy(
            src_ref=source,
            dst_ref=self.landing(slot),
            send_sem=self.sem.at[0, slot],
            recv_sem=self.sem.at[1, slot],
            device_id=(self.w ^ 1, self.n),
            device_id_type=MESH,
        )

    def send(self, slot):
        return self.remote(slot, self.chunk(self.w ^ 1 ^ (2 * slot)))

    def start(self):
        for slot in range(self.plan.chunks):
            self.send(slot).start()
            if self.both:
                self.local(slot).start()

    def wait_recv(self):
        for slot in range(self.plan.chunks):
            self.remote(slot, self.landing(slot)).wait_recv()

    def finish(self):
        for slot in range(self.plan.chunks):
            self.send(slot).wait_send()
            if self.both:
                self.local(slot).wait()


def to_sibling(place, source, target, sem):
    return pltpu.make_async_remote_copy(
        src_ref=source,
        dst_ref=target,
        send_sem=sem.at[0],
        recv_sem=sem.at[1],
        device_id=(place[0] ^ 1, place[1]),
        device_id_type=MESH,
    )


def column_of(row):
    eye = lax.broadcasted_iota(I32, (LANES, LANES), 0) == lax.broadcasted_iota(I32, (LANES, LANES), 1)
    pieces = [
        jnp.sum(jnp.where(eye, row[:, start : start + LANES], 0.0), axis=1, keepdims=True)
        for start in range(0, row.shape[1], LANES)
    ]
    return jnp.concatenate(pieces, axis=0)


def unpack_small(plan, packed, sizes):
    summed = jnp.sum(packed.astype(F32).reshape(plan.wide, plan.narrow, 16, LANES), axis=1)
    rows = []
    for i, size in enumerate(sizes):
        each = LANES // (size * plan.narrow)
        blocks = [
            sum(summed[first + j, i : i + 1, :] for j in range(each))
            for first in range(0, plan.wide, each)
        ]
        rows.append(jnp.concatenate(blocks, axis=1))
    return rows


def same_bucket(width):
    row = lax.broadcasted_iota(I32, (width, width), 0) // HEADS
    column = lax.broadcasted_iota(I32, (width, width), 1) // HEADS
    return (row == column).astype(F32)


def spread_table(table_row):
    width = BUCKETS * HEADS
    lane = lax.broadcasted_iota(I32, (HEADS, width), 1)
    head = lax.broadcasted_iota(I32, (HEADS, width), 0)
    same = lane % HEADS == head
    picked = jnp.where(same, table_row, 0.0).astype(BF16)
    spread = matmul(picked, same_bucket(width).astype(BF16))
    return jnp.concatenate(
        [jnp.where(same, spread[h : h + 1, :], 0.0).astype(BF16) for h in range(HEADS)], axis=0
    )


def bucket_rows(bucket):
    small = bucket.astype(F32).astype(BF16)
    one, zero = jnp.ones_like(small), jnp.zeros_like(small)
    return jnp.concatenate(
        [jnp.where(small == jnp.asarray(j, BF16), one, zero) for j in range(BUCKETS)], axis=0
    )


class Reduce:
    def __init__(self, plan, rows, window, order):
        self.plan, self.rows = plan, rows
        self.start_column, self.columns = window
        self.padded = round_up(rows, 16)
        self.aligned = self.padded == rows
        self.group = plan.narrow * rows
        self.order = order
        self.chunks = plan.chunks

    def reserve(self):
        count, columns = self.plan.narrow, self.columns
        shapes = [
            sems(2, self.chunks),
            sems(2, count),
            pltpu.VMEM((self.chunks, self.group, columns), BF16),
            pltpu.VMEM((self.chunks - 1, self.group, columns), BF16),
            pltpu.VMEM((count - 1, self.padded, columns), BF16),
        ]
        if not self.aligned:
            shapes.append(pltpu.VMEM((count, self.padded, columns), BF16))
        return shapes

    def bind(self, place, out, refs):
        self.w, self.n = place
        self.out, self.done = out, 0
        self.bsem, self.zsem, self.acc, self.received, self.zreceived = refs[:5]
        if not self.aligned:
            self.stage = refs[5]

    def hops(self, stage):
        bit, masks = self.order[stage], span(self.order[stage + 1 :])
        base = self.chunks - 2 * len(masks)
        return [
            (
                mask >> 1,
                base + k,
                pltpu.make_async_remote_copy(
                    src_ref=self.acc.at[(bit ^ mask) >> 1],
                    dst_ref=self.received.at[base + k],
                    send_sem=self.bsem.at[0, base + k],
                    recv_sem=self.bsem.at[1, base + k],
                    device_id=(self.w ^ bit, self.n),
                    device_id_type=MESH,
                ),
            )
            for k, mask in enumerate(masks)
        ]

    def z_copy(self, d):
        peer = lax.rem(self.n + d, self.plan.narrow)
        source = self.acc.at[0, at(peer, self.rows), :] if self.aligned else self.stage.at[peer]
        return pltpu.make_async_remote_copy(
            src_ref=source,
            dst_ref=self.zreceived.at[d - 1],
            send_sem=self.zsem.at[0, d],
            recv_sem=self.zsem.at[1, d],
            device_id=(self.w, peer),
            device_id_type=MESH,
        )

    def step(self, stage):
        bits = len(self.order)
        if 1 <= stage <= bits:
            for slot, k, copy in self.hops(stage - 1):
                copy.wait_recv()

                def body(j, slot=slot, k=k):
                    block = at(j, 16)
                    self.acc[slot, block, :] += self.received[k, block, :]

                loop(0, self.group // 16, body)
        if stage < bits:
            for _, _, copy in self.hops(stage):
                copy.start()
        elif stage == bits:
            if not self.aligned:
                size, wide = self.group, self.plan.narrow * self.padded
                row = lax.broadcasted_iota(I32, (wide, size), 0)
                column = lax.broadcasted_iota(I32, (wide, size), 1)
                pick = row == (column // self.rows) * self.padded + column % self.rows
                self.stage[...] = (
                    matmul(pick.astype(F32).astype(BF16), self.acc[0]).astype(BF16).reshape(self.stage.shape)
                )
            for d in range(1, self.plan.narrow):
                self.z_copy(d).start()
        else:
            total = self.acc[0, at(self.n, self.rows), :] if self.aligned else self.stage[self.n]
            total = total.astype(F32)
            for d in range(1, self.plan.narrow):
                self.z_copy(d).wait_recv()
                total = total + self.zreceived[d - 1].astype(F32)
            self.out[:, pl.ds(self.start_column, self.columns)] = total[: self.rows]

    def finish(self):
        for stage in range(len(self.order)):
            for _, _, copy in self.hops(stage):
                copy.wait_send()
        for d in range(1, self.plan.narrow):
            self.z_copy(d).wait_send()


class SumAll:
    def __init__(self, plan, shape):
        self.shape = shape
        self.rounds = [(bit, 0) for bit in [1] + plan.bits]
        self.rounds += [(0, 1 << k) for k in range(plan.narrow.bit_length() - 1)]

    def reserve(self):
        count = len(self.rounds)
        return [sems(2, count)] + [pltpu.VMEM((count, *self.shape), F32)] * 2

    def bind(self, place, out, refs):
        self.w, self.n = place
        self.out = out
        self.sem, self.held, self.received = refs

    def copy(self, turn):
        bit, other = self.rounds[turn]
        return pltpu.make_async_remote_copy(
            src_ref=self.held.at[turn],
            dst_ref=self.received.at[turn],
            send_sem=self.sem.at[0, turn],
            recv_sem=self.sem.at[1, turn],
            device_id=(self.w ^ bit, self.n ^ other),
            device_id_type=MESH,
        )

    def start(self, value):
        self.held[0] = value
        self.copy(0).start()

    def step(self, turn):
        self.copy(turn).wait_recv()
        total = self.held[turn] + self.received[turn]
        if turn + 1 < len(self.rounds):
            self.held[turn + 1] = total
            self.copy(turn + 1).start()
        else:
            self.out[...] = total

    def finish(self):
        for turn in range(len(self.rounds)):
            self.copy(turn).wait_send()


class Sizes:
    def __init__(self, plan, rows, width, ff, shards):
        self.plan, self.rows, self.width, self.ff = plan, rows, width, ff
        self.shards = shards
        self.group = plan.narrow * shards[0]
        self.down_group = plan.narrow * shards[DOWN]
        step = round_up(ff // 3, BLOCK)
        self.ff_windows = [(start, min(step, ff - start)) for start in range(0, ff, step)]
        self.half_windows = [(0, width // 2), (width // 2, width // 2)]
        self.blocks = round_up(ff, BLOCK) // BLOCK

    def full(self):
        wide = self.plan.wide
        return (
            [(wide, self.group, self.width)] * 4
            + [(wide, self.group, self.ff)] * 2
            + [(wide, self.down_group, self.width)]
        )


QUERY, KEY, VALUE, OUT, GATE, UP, DOWN = range(7)
BLOCK = 512


class Layer:
    def __init__(self, plan, sizes):
        self.plan, self.sizes = plan, sizes
        whole = (0, sizes.width)
        wide = [(weight, window) for window in sizes.ff_windows for weight in (GATE, UP)]
        down = [(DOWN, window) for window in sizes.half_windows]
        self.order = [(weight, whole) for weight in (QUERY, KEY, VALUE, OUT)] + down + wide
        self.small = Gather(plan, 16, (0, LANES))
        self.items = [self.small] + [Gather(plan, sizes.shards[weight], window) for weight, window in self.order]
        self.swaps = [Swap(plan) for _ in range(4)]
        self.extra = self.small.stages() - 4
        ways = [plan.bits, plan.bits[::-1]]
        self.reduces = []
        for weight in range(7):
            turn = 1 if weight in (UP, KEY, OUT) else 0
            pairs = enumerate(sizes.half_windows)
            if weight in (GATE, UP):
                pairs = [(0, window) for window in sizes.ff_windows]
            self.reduces.append([Reduce(plan, sizes.shards[weight], window, ways[k ^ turn]) for k, window in pairs])
        self.sums = SumAll(plan, (8, sizes.width))

    def call(self, vectors, counts, shards, tokens, patch_keep, text_len, buckets, cotangent):
        plan, s = self.plan, self.sizes
        self.counts = counts
        rows, width, chunks = s.rows, s.width, plan.chunks
        row_block = struct((rows, width), BF16)
        inputs = dict(
            vectors=vectors,
            shards=shards[:DOWN],
            down_shard=shards[DOWN],
            tokens=tokens,
            patch_keep=patch_keep,
            text_len=text_len,
            buckets=buckets,
            cotangent=cotangent,
        )
        outputs = dict(
            small=struct((plan.wide, plan.narrow * 16, LANES), BF16),
            full=[struct(shape, BF16) for shape in s.full()],
            stages=[item.stages_out() for item in self.items],
            qkv=[row_block] * 3,
            prob=struct((HEADS, rows, rows), BF16),
            turned=[struct((2, chunks, s.group, rows), BF16)] * 3,
            hidden_far=struct((chunks, s.down_group, rows), BF16),
            cot_far=row_block,
            far_ff=struct((2, s.blocks, rows, BLOCK), BF16),
            far_out=row_block,
            far_attn=[row_block] * 3,
            result=row_block,
            input_grad=struct((rows, width), F32),
            grads=[
                struct((size, s.ff if weight in (GATE, UP) else width), F32) for weight, size in enumerate(s.shards)
            ],
            sums=struct((8, width), F32),
        )
        square = pltpu.VMEM((rows, width), BF16)
        down_rows = round_up(s.shards[DOWN], 16)
        scratch = dict(
            items=[item.reserve() for item in self.items],
            swaps=[swap.reserve() for swap in self.swaps],
            reduces=[[item.reserve() for item in pair] for pair in self.reduces],
            exchange=self.sums.reserve(),
            direct=sems(2),
            load=sems(len(self.items)),
            pre=sems(8),
            packed=pltpu.VMEM((16, LANES), BF16),
            small=pltpu.VMEM((plan.wide, plan.narrow * 16, LANES), BF16),
            down_shard=pltpu.VMEM((down_rows, width), BF16),
            rows=pltpu.VMEM((8, width), F32),
            keep=pltpu.VMEM((rows, 1), F32),
            big=pltpu.VMEM((HEADS, rows, rows), BF16),
            stream=pltpu.VMEM((rows, width), F32),
            normed=square,
            totals=pltpu.VMEM((8, width), F32),
            pair_sem=sems(2),
            tile_sem=sems(2, 3),
            ff_sem=sems(len(s.ff_windows), 2, 2, 2),
            out_sem=sems(2),
            attn_sem=sems(2, 3, 2),
            store=sems(6),
        )
        return run(
            self.kernel,
            inputs,
            outputs,
            scratch,
            {"vectors", "down_shard", "patch_keep", "cotangent", "grads", "sums"},
            {"text_len"},
            0,
            "layer",
        )

    def kernel(self, i, o, t):
        self.i, self.o, self.t = i, o, t
        plan, s = self.plan, self.sizes
        square = pltpu.VMEM((s.rows, s.width), BF16)
        planes = pltpu.VMEM((2, plan.chunks, s.group, s.rows), BF16)
        weight_space = pltpu.VMEM((plan.wide, s.group, s.width), BF16)
        self.pack()
        self.place = place = enter(plan)
        self.small.bind(place, t.packed, o.small, o.stages[0], t.items[0])
        for item, (weight, _), stage, refs in zip(self.items[1:], self.order, o.stages[1:], t.items[1:]):
            item.bind(place, t.down_shard if weight == DOWN else i.shards[weight], o.full[weight], stage, refs)
        for pair, out, refs in zip(self.reduces, o.grads, t.reduces):
            for item, own in zip(pair, refs):
                item.bind(place, out, own)
        self.sums.bind(place, o.sums, t.exchange)
        self.direct = to_sibling(place, i.cotangent, o.cot_far, t.direct)

        for item in self.items[:2]:
            item.start()
        self.direct.start()
        for turn in range(-self.extra, 4):
            self.tick(turn)
        self.set_up()
        pl.run_scoped(
            self.attention_phase,
            [weight_space] * 3,
            [square] * 4,
            [pltpu.VMEM((s.width, s.rows), BF16)] * 2,
            pltpu.VMEM((2, 2, s.rows, s.rows), BF16),
            pltpu.VMEM((HEADS * 16, BUCKETS * 16), BF16),
            pltpu.VMEM((s.rows, s.rows), I32),
        )
        pl.run_scoped(
            self.feed_phase,
            [pltpu.VMEM((plan.wide, s.group, s.ff_windows[0][1]), BF16)] * 2,
            pltpu.VMEM((s.ff, s.width), BF16),
            pltpu.VMEM((s.ff, s.rows), BF16),
            pltpu.VMEM((plan.chunks, s.down_group, s.rows), BF16),
            square,
            planes,
            pltpu.VMEM((2, 2, s.rows, TILE), BF16),
            sems(plan.wide),
        )
        pl.run_scoped(
            self.back_phase,
            planes,
            [square] * 3,
            pltpu.VMEM((s.rows, s.width), F32),
            square,
        )


    def tick(self, turn):
        stages, turn = self.small.stages(), turn + self.extra
        for stage in range(stages):
            k = turn - stage
            if 0 <= k < len(self.items):
                self.items[k].step(stage)
        if turn + 2 < len(self.items):
            self.items[turn + 2].start()

    def load(self, weight, window, target):
        k = 1 + self.order.index((weight, window))
        return pltpu.make_async_copy(self.o.full[weight].at[:, :, pl.ds(*window)], target, self.t.load.at[k])

    def pack(self):
        i, t = self.i, self.t
        device = lax.axis_index("wide") * self.plan.narrow + lax.axis_index("narrow")
        source = lax.broadcasted_iota(I32, (LANES, LANES), 0)
        lane = lax.broadcasted_iota(I32, (LANES, LANES), 1)
        row = lax.broadcasted_iota(I32, (16, LANES), 0)
        packed, offset = jnp.zeros((16, LANES), F32), 0
        for k, size in enumerate(self.counts):
            first = lax.rem(device * size, LANES)
            pick = (source == offset + lane - first) & (lane >= first) & (lane < first + size)
            found = matmul(i.vectors[...], pick.astype(F32).astype(BF16))
            packed = jnp.where(row == k, found, packed)
            offset += size
        t.packed[...] = packed.astype(BF16)
        size = i.down_shard.shape[0]
        t.down_shard[...] = jnp.concatenate(
            [i.down_shard[...], jnp.zeros((t.down_shard.shape[0] - size, self.sizes.width), BF16)], axis=0
        )

    def set_up(self):
        i, o, t = self.i, self.o, self.t
        copy = pltpu.make_async_copy(o.small, t.small, t.load.at[0])
        copy.start()
        tokens = pltpu.make_async_copy(i.tokens, t.normed, t.pre.at[7])
        tokens.start()
        patches, rows = i.patch_keep.shape[1], self.sizes.rows
        row = lax.broadcasted_iota(I32, (rows, patches), 0)
        lane = lax.broadcasted_iota(I32, (rows, patches), 1)
        kept = jnp.sum(jnp.where(row == lane, i.patch_keep[...].astype(F32), 0.0), axis=1, keepdims=True)
        t.keep[...] = jnp.where(lax.broadcasted_iota(I32, (rows, 1), 0) >= patches, 1.0, kept)
        t.totals[...] = jnp.zeros_like(t.totals)
        copy.wait()
        embed, gain_one, gain_two, table = unpack_small(self.plan, t.small[...], self.counts)
        t.rows[...] = jnp.concatenate([embed, gain_one, gain_two, jnp.zeros((5, self.sizes.width), F32)], axis=0)
        self.table_row = table
        tokens.wait()

        def body(j):
            block = at(j, 64)
            t.stream[block, :] = jnp.where(
                t.keep[block, :] > 0.5, t.normed[block, :].astype(F32), t.rows[0:1, :]
            )

        loop(0, rows // 64, body)
        self.norm(1)

    def norm(self, gain):
        t = self.t

        def body(j):
            block = at(j, 64)
            x = t.stream[block, :]
            scale = lax.rsqrt(jnp.mean(x * x, axis=-1, keepdims=True) + EPSILON)
            t.normed[block, :] = (x * scale * t.rows[gain : gain + 1, :]).astype(BF16)

        loop(0, self.sizes.rows // 64, body)

    def turn(self, source, target):
        def body(j):
            target[at(j, LANES), :] = source[:, at(j, LANES)].T

        loop(0, self.sizes.width // LANES, body)


    def attention_phase(self, held, qkva, turned, prob, table, buckets):
        o, t, s = self.o, self.t, self.sizes
        bucket_copy = pltpu.make_async_copy(self.i.buckets, buckets, t.pre.at[7])
        bucket_copy.start()
        normed, attended, second, _ = self.swaps
        for swap, source, target, sem in zip(
            self.swaps, (turned[0], turned[1], turned[0]), o.turned, t.swaps
        ):
            swap.bind(self.place, source, target, sem)
        store = [pltpu.make_async_copy(qkva[k], o.qkv[k], t.store.at[k]) for k in range(3)]
        whole = (0, s.width)
        loads = [self.load(weight, whole, held[weight % 3]) for weight in (QUERY, KEY, VALUE, OUT)]
        self.turn(t.normed, turned[0])
        normed.start()
        table[...] = spread_table(self.table_row)
        self.tick(4)
        loads[QUERY].start()
        blocks = s.rows // 16
        bucket_copy.wait()
        self.bias(0, blocks // 2, table, buckets)
        self.tick(5)
        loads[KEY].start()
        loads[QUERY].wait()
        self.project(held[0], qkva[0])
        store[0].start()
        self.bias(blocks // 2, blocks, table, buckets)
        self.tick(6)
        loads[VALUE].start()
        loads[KEY].wait()
        self.project(held[1], qkva[1])
        store[1].start()
        self.tick(7)
        loads[OUT].start()
        loads[VALUE].wait()
        self.project(held[2], qkva[2])
        store[2].start()
        count = HEADS // 2
        self.attend(0, 3 * count // 8, qkva, prob)
        self.tick(8)
        self.attend(3 * count // 8, 6 * count // 8, qkva, prob)
        self.tick(9)
        self.attend(6 * count // 8, count, qkva, prob)
        for slot in range(2):
            self.prob_copy(slot, count - 2 + slot, prob).wait()
        loads[OUT].wait()

        def body(j):
            block = held[0][:, :, at(j, TILE)].reshape(s.width, TILE)
            t.stream[:, at(j, TILE)] += matmul(qkva[3][...], block)

        loop(0, s.width // TILE, body)
        self.tick(10)
        self.turn(qkva[3], turned[1])
        attended.start()
        normed.finish()
        self.norm(2)
        self.turn(t.normed, turned[0])
        second.start()
        for copy in store:
            copy.wait()
        attended.finish()
        second.finish()

    def bias(self, low, high, table, buckets):
        i, t = self.i, self.t
        live = lax.broadcasted_iota(I32, (1, self.sizes.rows), 1) < i.patch_keep.shape[1] + i.text_len[0]

        def body(j):
            block = at(j, 16)
            spread = matmul(table[...], bucket_rows(buckets[block, :]))
            spread = jnp.where(live, spread, NEG_FILL).astype(BF16)
            t.big[:, block, :] = spread.reshape(HEADS, 16, spread.shape[-1])

        loop(low, high, body)

    def project(self, weight, target):
        def body(j):
            block = weight[:, :, at(j, TILE)].reshape(self.sizes.width, TILE)
            target[:, at(j, TILE)] = matmul(self.t.normed[...], block).astype(BF16)

        loop(0, self.sizes.width // TILE, body)

    def prob_copy(self, slot, pair, prob):
        return pltpu.make_async_copy(prob.at[slot], self.o.prob.at[pl.ds(2 * pair, 2)], self.t.pair_sem.at[slot])

    def attend(self, low, high, qkva, prob):
        t = self.t
        lane = lax.broadcasted_iota(I32, (1, LANES), 1)

        def body(pair):
            columns, slot = at(pair, LANES), lax.rem(pair, 2)

            @pl.when(pair >= 2)
            def _():
                self.prob_copy(slot, pair, prob).wait()

            q, k, v = (ref[:, columns] for ref in qkva[:3])
            mixed = []
            for e in range(2):
                own = jnp.where((lane < HEAD) == (e == 0), q, jnp.zeros_like(q))
                scores = times_trans(own, k) + t.big[2 * pair + e].astype(F32)
                top = jnp.max(scores, axis=-1, keepdims=True)
                powers = jnp.exp(scores - top)
                total = jnp.sum(powers, axis=-1, keepdims=True)
                weights = (powers * (1.0 / total)).astype(BF16)
                prob[slot, e] = weights
                mixed.append(matmul(weights, v))
            qkva[3][:, columns] = jnp.where(lane < HEAD, mixed[0], mixed[1]).astype(BF16)
            self.prob_copy(slot, pair, prob).start()

        loop(low, high, body)


    def feed_phase(self, held, down, hidden, hidden_far, cot_far, planes, far, sem):
        i, o, t, s = self.i, self.o, self.t, self.sizes
        group, windows = s.down_group, s.ff_windows
        copies = [
            pltpu.make_async_copy(o.full[DOWN].at[k], down.at[pl.ds(k * group, group), :], sem.at[k])
            for k in range(self.plan.wide)
        ]
        for copy in copies:
            copy.start()
        swap = self.swaps[3]
        swap.bind(self.place, hidden, o.hidden_far, t.swaps[3])
        planes_copy = pltpu.make_async_copy(o.turned[2], planes, t.pre.at[0])
        for part, window in enumerate(windows):
            loads = [
                self.load(weight, window, held[k].at[:, :, pl.ds(0, window[1])]) for k, weight in enumerate((GATE, UP))
            ]
            loads[0].start()
            self.tick(11 + 2 * part)
            loads[1].start()
            if part == 0:
                for copy in copies:
                    copy.wait()
            if part > 0:
                self.feed_weights(part - 1, planes, far)
            for copy in loads:
                copy.wait()
            self.feed(part, held, down, hidden)
            for copy in self.ff_copies(part):
                copy.start()
            if part == 0:
                self.swaps[2].wait_recv()
                planes_copy.start()
                planes_copy.wait()
            self.tick(12 + 2 * part)
        swap.start()
        for item in self.items:
            item.finish()
        self.direct.wait()
        cot_copy = pltpu.make_async_copy(o.cot_far, cot_far, t.pre.at[1])
        cot_copy.start()
        self.feed_weights(len(windows) - 1, planes, far)
        swap.wait_recv()
        far_copy = pltpu.make_async_copy(o.hidden_far, hidden_far, t.pre.at[2])
        far_copy.start()
        cot_copy.wait()
        far_copy.wait()
        self.down_gradient(hidden, hidden_far, cot_far)
        self.advance(DOWN)
        self.advance(GATE, (0,))
        self.advance(UP, (0,))
        store = pltpu.make_async_copy(cot_far, o.result, t.pre.at[1])

        def finish(j):
            block = at(j, TILE)
            cot_far[:, block] = (t.stream[:, block] + trans_times(hidden[...], down[:, block])).astype(BF16)

        loop(0, s.width // TILE, finish)
        store.start()
        store.wait()
        swap.finish()

    def near(self, which, j):
        return which * self.sizes.blocks + lax.div(j, 2), at(lax.rem(j, 2), TILE)

    def ff_copies(self, part):
        s, t = self.sizes, self.t
        start, size = s.ff_windows[part]
        copies = []
        for which in range(2):
            for k, first in enumerate(range(start, start + size, BLOCK)):
                block, columns = first // BLOCK, pl.ds(0, min(BLOCK, start + size - first))
                copies.append(
                    to_sibling(
                        self.place,
                        t.big.at[which * s.blocks + block, :, columns],
                        self.o.far_ff.at[which, block, :, columns],
                        t.ff_sem.at[part, which, k],
                    )
                )
        return copies

    def feed(self, part, held, down, hidden):
        i, t, s = self.i, self.t, self.sizes
        start, size = s.ff_windows[part]
        first = start // TILE

        def body(j):
            tile, columns = first + j, at(j, TILE)
            gate = matmul(t.normed[...], held[0][:, :, columns].reshape(s.width, TILE))
            up = matmul(t.normed[...], held[1][:, :, columns].reshape(s.width, TILE))
            grad = times_trans(i.cotangent[...], down[at(tile, TILE), :])
            square = gate * gate
            bend = jnp.tanh(GELU_SCALE * gate * (1.0 + GELU_CUBE * square))
            half = 0.5 * (1.0 + bend)
            act = gate * half
            slope = half + (0.5 * GELU_SCALE) * gate * (1.0 - bend * bend) * (1.0 + (3.0 * GELU_CUBE) * square)
            hidden[at(tile, TILE), :] = (act * up).astype(BF16).T
            for which, value in enumerate((grad * up * slope, grad * act)):
                block, lanes = self.near(which, tile)
                t.big[block, :, lanes] = value.astype(BF16)

        loop(0, size // TILE, body)

    def feed_weights(self, part, planes, far):
        o, t, s = self.o, self.t, self.sizes
        start, size = s.ff_windows[part]
        first, rows = start // TILE, self.plan.chunks * s.group
        for copy in self.ff_copies(part):
            copy.wait_recv()

        def far_copies(slot, j):
            return [
                pltpu.make_async_copy(
                    o.far_ff.at[which, lax.div(first + j, 2), :, self.near(which, first + j)[1]],
                    far.at[slot, which],
                    t.tile_sem.at[slot, which],
                )
                for which in range(2)
            ]

        def body(j, slot):
            left = jnp.concatenate([planes[0].reshape(rows, s.rows), planes[1].reshape(rows, s.rows)], axis=1)
            for which, weight in enumerate((GATE, UP)):
                block, lanes = self.near(which, first + j)
                right = jnp.concatenate([t.big[block, :, lanes], far[slot, which]], axis=0)
                acc = self.reduces[weight][part].acc
                acc[:, :, at(j, TILE)] = matmul(left, right).astype(BF16).reshape(self.plan.chunks, s.group, TILE)

        streamed(0, size // TILE, far_copies, body)
        self.advance(GATE, (part,))
        self.advance(UP, (part,))

    def down_gradient(self, hidden, hidden_far, cot_far):
        i, s = self.i, self.sizes
        for part, (start, size) in enumerate(s.half_windows):
            acc = self.reduces[DOWN][part].acc

            def body(slot, acc=acc, start=start, size=size):
                columns = pl.ds(start, size)
                near = hidden[at(self.place[0] ^ (2 * slot), s.down_group), :]
                left = jnp.concatenate([near, hidden_far[slot]], axis=1)
                right = jnp.concatenate([i.cotangent[:, columns], cot_far[:, columns]], axis=0)
                acc[slot] = matmul(left, right).astype(BF16)

            loop(0, self.plan.chunks, body)


    def advance(self, weight, parts=None):
        for part in range(len(self.reduces[weight])) if parts is None else parts:
            item = self.reduces[weight][part]
            item.step(item.done)
            item.done += 1

    def back_phase(self, planes, qkv, back, grad_attended):
        o, t, s = self.o, self.t, self.sizes
        square = pltpu.VMEM((s.rows, s.width), BF16)
        self.swaps[0].wait_recv()
        loads = [
            pltpu.make_async_copy(source, target, t.pre.at[k])
            for k, (source, target) in enumerate(zip([o.turned[0]] + o.qkv, [planes] + qkv))
        ]
        pl.run_scoped(
            functools.partial(self.middle, loads, back, grad_attended),
            pltpu.VMEM((self.plan.wide, s.group, s.width), BF16),
            pltpu.VMEM((2, self.plan.chunks, s.group, s.rows), BF16),
            square,
        )
        for copy in loads:
            copy.wait()
        pl.run_scoped(
            functools.partial(self.attention_back, planes, qkv, back, grad_attended),
            [square] * 3,
            pltpu.VMEM((3, s.rows, s.width // 2), BF16),
        )

    def middle(self, later, back, grad_attended, weight, planes, grad_mid):
        o, t, s = self.o, self.t, self.sizes
        self.swaps[1].wait_recv()
        loads = [
            pltpu.make_async_copy(o.full[OUT], weight, t.pre.at[4]),
            pltpu.make_async_copy(o.turned[1], planes, t.pre.at[5]),
        ]
        groups = TILE // s.group
        pl.run_scoped(
            functools.partial(self.feed_input, loads + later, back), pltpu.VMEM((2, 2, groups, s.group, s.ff), BF16)
        )
        for part in range(len(s.ff_windows)):
            for copy in self.ff_copies(part):
                copy.wait_send()
        self.norm_back(2, back, grad_mid)
        out_copy = to_sibling(self.place, grad_mid, o.far_out, t.out_sem)
        out_copy.start()
        self.advance(GATE, (1,))
        self.advance(UP, (1,))
        for copy in loads:
            copy.wait()
        pl.run_scoped(
            functools.partial(self.out_back, out_copy, weight, planes, grad_mid, grad_attended),
            pltpu.VMEM((s.rows, s.width), BF16),
        )
        self.advance(GATE, (0,))
        self.advance(UP, (0,))
        out_copy.wait_send()

    def attention_back(self, planes, qkv, back, grad_attended, grad_qkv, far):
        i, o, t, s, plan = self.i, self.o, self.t, self.sizes, self.plan
        self.grad_qkv = grad_qkv
        prob_space = pltpu.VMEM((2, 2, s.rows, s.rows), BF16)
        half = HEADS // 4
        tokens = pltpu.make_async_copy(i.tokens, t.normed, t.pre.at[7])
        tokens.start()
        pl.run_scoped(functools.partial(self.attend_back, 0, half, qkv, grad_attended), prob_space)
        self.send_attention(0)
        self.advance(GATE, (2,))
        self.advance(UP, (2,))
        self.advance(DOWN)
        self.attention_weights(0, planes, far)
        self.advance(GATE, (0, 1))
        self.advance(UP, (0, 1))
        pl.run_scoped(functools.partial(self.attend_back, half, 2 * half, qkv, grad_attended), prob_space)
        self.send_attention(1)
        self.advance(OUT)
        self.advance(GATE, (2,))
        self.advance(UP, (2,))
        self.advance(DOWN)
        self.attention_weights(1, planes, far)
        for weight in (QUERY, KEY, VALUE):
            self.advance(weight, (0,))
        groups = TILE // s.group
        pl.run_scoped(
            functools.partial(self.attention_input, back), pltpu.VMEM((2, 3, groups, s.group, s.width), BF16)
        )
        self.advance(OUT)
        for weight in (QUERY, KEY, VALUE):
            self.advance(weight, (1,))
        tokens.wait()
        self.norm_back(1, back, None)
        store = pltpu.make_async_copy(t.stream, o.input_grad, t.pre.at[0])
        store.start()
        for weight in (QUERY, KEY, VALUE):
            self.advance(weight, (0,))
        self.table_back()
        self.sums.start(t.totals[...])
        for weight in (QUERY, KEY, VALUE):
            self.advance(weight, (1,))
        turn, last = 0, len(plan.bits) + 1
        left = [(weight, part) for weight in (GATE, UP, DOWN, OUT) for part in range(len(self.reduces[weight]))]
        left += [(weight, part) for part in range(2) for weight in (QUERY, KEY, VALUE)]
        while left:
            for weight, part in list(left):
                if self.reduces[weight][part].done > last:
                    left.remove((weight, part))
                    continue
                self.advance(weight, (part,))
                if turn % 2 == 1 and turn // 2 < len(self.sums.rounds):
                    self.sums.step(turn // 2)
                turn += 1
        for k in range(turn // 2, len(self.sums.rounds)):
            self.sums.step(k)
        store.wait()
        for part in range(2):
            for copy in self.attention_copies(part):
                copy.wait_send()
        for pair in self.reduces:
            for item in pair:
                item.finish()
        self.sums.finish()

    def feed_input(self, loads, back, held):
        o, t, s = self.o, self.t, self.sizes
        groups = TILE // s.group
        last = s.ff - BLOCK * (s.blocks - 1)

        def weight_copies(slot, j):
            return [
                pltpu.make_async_copy(
                    o.full[weight].at[pl.ds(j * groups, groups)], held.at[slot, which], t.tile_sem.at[slot, which]
                )
                for which, weight in enumerate((GATE, UP))
            ]

        def body(j, slot):
            total = None
            for which in range(2):
                first = which * s.blocks
                near = [t.big[first + k] for k in range(s.blocks - 1)]
                near.append(t.big[first + s.blocks - 1, :, pl.ds(0, last)])
                found = times_trans(jnp.concatenate(near, axis=1), held[slot, which].reshape(TILE, s.ff))
                total = found if total is None else total + found
            back[:, at(j, TILE)] = total

        for copy in weight_copies(0, 0) + loads:
            copy.start()
        streamed(0, s.width // TILE, weight_copies, body, first=-1)

    def norm_back(self, which, back, grad_mid):
        i, t, s = self.i, self.t, self.sizes

        def body(j):
            block = at(j, 64)
            kept = t.keep[block, :] > 0.5
            grad = back[block, :]
            if which == 2:
                x = t.stream[block, :]
                before = i.cotangent[block, :].astype(F32)
            else:
                x = jnp.where(kept, t.normed[block, :].astype(F32), t.rows[0:1, :])
                before = t.stream[block, :]
            scale = lax.rsqrt(jnp.mean(x * x, axis=-1, keepdims=True) + EPSILON)
            scaled = x * scale
            u = grad * t.rows[which : which + 1, :]
            inner = jnp.mean(u * scaled, axis=-1, keepdims=True)
            total = before + scale * (u - scaled * inner)
            t.totals[which : which + 1, :] += jnp.sum(grad * scaled, axis=0, keepdims=True)
            if which == 2:
                t.stream[block, :] = total
                grad_mid[block, :] = total.astype(BF16)
            else:
                t.stream[block, :] = jnp.where(kept, total, 0.0)
                t.totals[0:1, :] += jnp.sum(jnp.where(kept, 0.0, total), axis=0, keepdims=True)

        loop(0, s.rows // 64, body)

    def out_back(self, out_copy, weight, planes, grad_mid, grad_attended, far):
        o, t, s = self.o, self.t, self.sizes
        groups = TILE // s.group

        def attended(j):
            block = weight[pl.ds(j * groups, groups)].reshape(TILE, s.width)
            grad_attended[:, at(j, TILE)] = times_trans(grad_mid[...], block).astype(BF16)

        loop(0, s.width // TILE, attended)
        out_copy.wait_recv()
        load = pltpu.make_async_copy(o.far_out, far, t.pre.at[6])
        load.start()
        load.wait()
        rows = self.plan.chunks * s.group
        for part, (start, size) in enumerate(s.half_windows):
            columns = pl.ds(start, size)
            left = jnp.concatenate([planes[0].reshape(rows, s.rows), planes[1].reshape(rows, s.rows)], axis=1)
            right = jnp.concatenate([grad_mid[:, columns], far[:, columns]], axis=0)
            acc = self.reduces[OUT][part].acc
            acc[...] = matmul(left, right).astype(BF16).reshape(acc.shape)
            self.advance(OUT, (part,))

    def attend_back(self, low, high, qkv, grad_attended, prob):
        o, t = self.o, self.t
        lane = lax.broadcasted_iota(I32, (1, LANES), 1)

        def prob_copies(slot, pair):
            return [pltpu.make_async_copy(o.prob.at[pl.ds(2 * pair, 2)], prob.at[slot], t.tile_sem.at[slot, 0])]

        def body(pair, slot):
            columns = at(pair, LANES)
            q, k, v = (ref[:, columns] for ref in qkv)
            grad = grad_attended[:, columns]
            found = [[], [], []]
            for e in range(2):
                own = jnp.where((lane < HEAD) == (e == 0), grad, jnp.zeros_like(grad))
                weights = prob[slot, e]
                wide = weights.astype(F32)
                grad_prob = times_trans(own, v)
                delta = jnp.sum(grad_prob * wide, axis=-1, keepdims=True)
                scores = (wide * (grad_prob - delta)).astype(BF16)
                t.big[2 * pair + e] = scores
                found[0].append(matmul(scores, k))
                found[1].append(trans_times(scores, q))
                found[2].append(trans_times(weights, grad))
            for ref, (first, second) in zip(self.grad_qkv, found):
                ref[:, columns] = jnp.where(lane < HEAD, first, second).astype(BF16)

        streamed(low, high, prob_copies, body)

    def attention_copies(self, part):
        window = pl.ds(*self.sizes.half_windows[part])
        return [
            to_sibling(
                self.place,
                self.grad_qkv[which].at[:, window],
                self.o.far_attn[which].at[:, window],
                self.t.attn_sem.at[part, which],
            )
            for which in range(3)
        ]

    def send_attention(self, part):
        for copy in self.attention_copies(part):
            copy.start()

    def attention_weights(self, part, planes, far):
        o, t, s = self.o, self.t, self.sizes
        columns = pl.ds(*s.half_windows[part])
        rows = self.plan.chunks * s.group
        loads = []
        for which, copy in enumerate(self.attention_copies(part)):
            copy.wait_recv()
            loads.append(pltpu.make_async_copy(o.far_attn[which].at[:, columns], far.at[which], t.pre.at[which]))
            loads[-1].start()
        for which in range(3):
            loads[which].wait()
            left = jnp.concatenate([planes[0].reshape(rows, s.rows), planes[1].reshape(rows, s.rows)], axis=1)
            right = jnp.concatenate([self.grad_qkv[which][:, columns], far[which]], axis=0)
            acc = self.reduces[which][part].acc
            acc[...] = matmul(left, right).astype(BF16).reshape(acc.shape)
            self.advance(which, (part,))

    def attention_input(self, back, held):
        o, t, s = self.o, self.t, self.sizes
        groups = TILE // s.group

        def weight_copies(slot, j):
            return [
                pltpu.make_async_copy(
                    o.full[which].at[pl.ds(j * groups, groups)], held.at[slot, which], t.tile_sem.at[slot, which]
                )
                for which in range(3)
            ]

        def body(j, slot):
            back[:, at(j, TILE)] = sum(
                times_trans(self.grad_qkv[which][...], held[slot, which].reshape(TILE, s.width)) for which in range(3)
            )

        streamed(0, s.width // TILE, weight_copies, body)

    def table_back(self):
        i, t, s = self.i, self.t, self.sizes
        width, step = BUCKETS * HEADS, 4

        def count(total, buckets):
            copy = pltpu.make_async_copy(i.buckets, buckets, t.pre.at[7])
            copy.start()
            total[...] = jnp.zeros_like(total)
            copy.wait()

            def body(j):
                left, right = [], []
                for k in range(step):
                    block = at(j * step + k, 16)
                    left.append(bucket_rows(buckets[block, :]))
                    right.append(t.big[:, block, :].reshape(HEADS * 16, s.rows))
                total[...] += times_trans(jnp.concatenate(left, axis=1), jnp.concatenate(right, axis=1))

            loop(0, s.rows // (16 * step), body)
            found = total[...].T
            row = lax.broadcasted_iota(I32, found.shape, 0)
            lane = lax.broadcasted_iota(I32, found.shape, 1)
            found = jnp.where(row % 16 == lane % 16, found, 0.0)
            by_head = jnp.sum(found.reshape(HEADS, 16, width), axis=1)
            summed = jnp.dot(
                by_head, same_bucket(width), precision=lax.Precision.HIGHEST, preferred_element_type=F32
            )
            head = lax.broadcasted_iota(I32, summed.shape, 0)
            lane = lax.broadcasted_iota(I32, summed.shape, 1)
            t.totals[3:4, :width] = jnp.sum(jnp.where(lane % HEADS == head, summed, 0.0), axis=0, keepdims=True)

        pl.run_scoped(count, pltpu.VMEM((width, HEADS * 16), F32), pltpu.VMEM((s.rows, s.rows), I32))


def hand_out(plan, large, sums, counts):
    def kernel(i, o, t):
        takes = [pltpu.make_async_copy(*pair, t.take.at[k]) for k, pair in enumerate(zip(i.large, t.held))]
        gives = [pltpu.make_async_copy(*pair, t.give.at[k]) for k, pair in enumerate(zip(t.held, o.large))]
        for copy in takes:
            copy.start()
        for take, give in zip(takes, gives):
            take.wait()
            give.start()
        device = lax.axis_index("wide") * plan.narrow + lax.axis_index("narrow")
        width = i.sums.shape[1]
        source = lax.broadcasted_iota(I32, (width, LANES), 0)
        lane = lax.broadcasted_iota(I32, (width, LANES), 1)
        found = {}
        for size in sorted(set(counts)):
            pick = (source == device * size + lane).astype(F32)
            found[size] = jnp.dot(
                i.sums[...], pick, precision=lax.Precision.HIGHEST, preferred_element_type=F32
            )
        for row, (size, target) in enumerate(zip(counts, o.owned)):
            target[...] = found[size][row : row + 1, :size]
        for copy in gives:
            copy.wait()

    done = run(
        kernel,
        dict(large=large, sums=sums),
        dict(large=[struct(x.shape, x.dtype) for x in large], owned=[struct((1, size), F32) for size in counts]),
        dict(take=sems(len(large)), give=sems(len(large)), held=[pltpu.VMEM(x.shape, x.dtype) for x in large]),
        {"sums", "owned"},
        set(),
        None,
        "hand_out",
    )
    return done.large, done.owned


def per_device(
    plan,
    tokens,
    patch_keep,
    text_len,
    buckets,
    mask_embed,
    norm_attn,
    w_query,
    w_key,
    w_value,
    w_out,
    bias_table,
    norm_ffn,
    w_gate,
    w_up,
    w_down,
    cotangent,
):
    rows, width = tokens.shape
    assert patch_keep.shape[0] == 1
    device = lax.axis_index("wide") * plan.narrow + lax.axis_index("narrow")
    small = (mask_embed, norm_attn, norm_ffn, bias_table)
    counts = [member.shape[0] for member in small]
    starts = [sum(counts[:k]) for k in range(len(counts))]
    vectors = sum(
        jnp.pad(member.reshape(1, -1), ((0, 0), (start, LANES - start - member.shape[0])))
        for start, member in zip(starts, small)
    )
    weights = (w_query, w_key, w_value, w_out, w_gate, w_up, w_down)
    shards = [jnp.pad(weight, ((0, -weight.shape[0] % 16), (0, 0))) for weight in weights[:DOWN]] + [w_down]
    sizes = Sizes(plan, rows, width, w_gate.shape[1], [weight.shape[0] for weight in weights])
    f = Layer(plan, sizes).call(vectors, counts, shards, tokens, patch_keep, text_len, buckets, cotangent)

    large = [f.result, f.input_grad] + f.grads
    (result, input_grad, query, key, value, out, gate, up, down), owned = hand_out(plan, large, f.sums, counts)
    embed, gain_one, gain_two, table = (part.reshape(-1) for part in owned)
    return (
        result,
        input_grad,
        embed,
        gain_one,
        query,
        key,
        value,
        out,
        table,
        gain_two,
        gate,
        up,
        down,
    )


def solution(mesh):
    rows, flat = P(("wide", "narrow"), None), P(("wide", "narrow"))
    plan = Plan(mesh.shape["wide"], mesh.shape["narrow"])
    return jax.shard_map(
        functools.partial(per_device, plan),
        mesh=mesh,
        in_specs=(rows, rows, flat, rows, flat, flat, rows, rows, rows, rows, flat, flat, rows, rows, rows, rows),
        out_specs=(rows, rows, flat, flat, rows, rows, rows, rows, flat, flat, rows, rows, rows),
        check_vma=False,
    )
```
